32 devices in a mesh: pair: 2 (over x), dp: 16 (over z, y, core).
Axes of the slice: x: 2, y: 2, z: 4, core: 2. Of those that a mesh axis runs over, the one named last changes fastest.
Arguments:
- token_shard: int32 [2, 16, 512, 1], P(None, 'dp'), may hold values from 0 to 15; in each aligned block of 512 rows (0 to 511, 512 to 1023, ..., all dimensions but the last counted through in order) at most 64 rows name the same one
- token_row: int32 [2, 16, 512], P(None, 'dp'), may hold values from 0 to 3143
- doc_ids: int32 [2, 16, 512], P(None, 'dp'), may hold values from 0 to 15, never falling along the last dimension, each value on 1 to 256 neighbouring positions
- loss_rows: int32 [2, 16, 16], P(None, 'dp'), may hold values from 0 to 510
- teacher_table: bfloat16 [50304, 768], P('dp'), may hold values from -0.41992188 to 0.41992188
- teacher_pos: bfloat16 [1024, 768], P('dp'), may hold values from -1.796875 to 1.796875
- teacher_attn_in: bfloat16 [768, 2304], P('dp'), may hold values from -0.21875 to 0.21875
- teacher_attn_out: bfloat16 [768, 768], P('dp'), may hold values from -0.875 to 0.875
- teacher_mlp_in: bfloat16 [768, 3072], P('dp'), may hold values from -0.21875 to 0.21875
- teacher_mlp_out: bfloat16 [3072, 768], P('dp'), may hold values from -0.21875 to 0.21875
- teacher_vecs: bfloat16 [14, 768], P(None, 'dp'), may hold values from -0.5 to 1.6, as said below
- table: float32 [50304, 768], P('dp'), may hold values from -0.42 to 0.42
- pos_table: float32 [1024, 768], P('dp'), may hold values from -1.8 to 1.8
- attn_in: float32 [768, 2304], P('dp'), may hold values from -0.21875 to 0.21875
- attn_out: float32 [768, 768], P('dp'), may hold values from -0.875 to 0.875
- mlp_in: float32 [768, 3072], P('dp'), may hold values from -0.21875 to 0.21875
- mlp_out: float32 [3072, 768], P('dp'), may hold values from -0.21875 to 0.21875
- vectors: float32 [14, 768], P(None, 'dp'), may hold values from -0.5 to 1.6, as said below
- table_m: float32 [50304, 768], P('dp'), may hold values from -1.8626451e-08 to 1.8626451e-08
- pos_m: float32 [1024, 768], P('dp'), may hold values from -1.9073486e-06 to 1.9073486e-06
- attn_in_m: float32 [768, 2304], P('dp'), may hold values from -1.9073486e-06 to 1.9073486e-06
- attn_out_m: float32 [768, 768], P('dp'), may hold values from -1.9073486e-06 to 1.9073486e-06
- mlp_in_m: float32 [768, 3072], P('dp'), may hold values from -1.9073486e-06 to 1.9073486e-06
- mlp_out_m: float32 [3072, 768], P('dp'), may hold values from -1.9073486e-06 to 1.9073486e-06
- vectors_m: float32 [14, 768], P(None, 'dp'), may hold values from -9.536743e-06 to 9.536743e-06
- table_v: float32 [50304, 768], P('dp'), may hold values from 8.60057e-15 to 3.440228e-14
- pos_v: float32 [1024, 768], P('dp'), may hold values from 8.60057e-15 to 3.440228e-14
- attn_in_v: float32 [768, 2304], P('dp'), may hold values from 8.60057e-15 to 3.440228e-14
- attn_out_v: float32 [768, 768], P('dp'), may hold values from 8.60057e-15 to 3.440228e-14
- mlp_in_v: float32 [768, 3072], P('dp'), may hold values from 8.60057e-15 to 3.440228e-14
- mlp_out_v: float32 [3072, 768], P('dp'), may hold values from 8.60057e-15 to 3.440228e-14
- vectors_v: float32 [14, 768], P(None, 'dp'), may hold values from 2.1501426e-13 to 8.6005703e-13
Outputs:
- table_new: float32 [50304, 768], P('dp')
- table_m_new: float32 [50304, 768], P('dp')
- table_v_new: float32 [50304, 768], P('dp')
- pos_new: float32 [1024, 768], P('dp')
- pos_m_new: float32 [1024, 768], P('dp')
- pos_v_new: float32 [1024, 768], P('dp')
- attn_in_new: float32 [768, 2304], P('dp')
- attn_in_m_new: float32 [768, 2304], P('dp')
- attn_in_v_new: float32 [768, 2304], P('dp')
- attn_out_new: float32 [768, 768], P('dp')
- attn_out_m_new: float32 [768, 768], P('dp')
- attn_out_v_new: float32 [768, 768], P('dp')
- mlp_in_new: float32 [768, 3072], P('dp')
- mlp_in_m_new: float32 [768, 3072], P('dp')
- mlp_in_v_new: float32 [768, 3072], P('dp')
- mlp_out_new: float32 [3072, 768], P('dp')
- mlp_out_m_new: float32 [3072, 768], P('dp')
- mlp_out_v_new: float32 [3072, 768], P('dp')
- vectors_new: float32 [14, 768], P(None, 'dp')
- vectors_m_new: float32 [14, 768], P(None, 'dp')
- vectors_v_new: float32 [14, 768], P(None, 'dp')
- grad_norm: float32 [], replicated
- kl_mean: float32 [], replicated
The draws below stay inside these ranges and needn't reach their ends.
Inputs may be any that keep to these rules, and one draw needn't show every extreme that they name: `token_shard`: in each micro-batch at most 64 tokens of one device's sequence fall into one vocabulary shard. `doc_ids`: document ids never fall along a sequence; a document has at most 256 tokens. `loss_rows`: positions may repeat; each repeat counts again. `teacher_vecs`: rows 0, 2 and 4 hold norms' gains, the others biases. `vectors`: rows 0, 2 and 4 hold norms' gains, the others biases.
All inputs are finite; a program needn't handle non-finite values.
Results may differ from the reference program's by a relative error of at most 0.015.
The reference program's roundings to bfloat16 on the way count: a program that leaves them out, or rounds other values in their place, can miss the bound.
Values may be sent and summed in bfloat16 or wider, within the bound.
No kernel may reach another device: no remote copies, remote signals or barrier semaphores. Data moves between devices by JAX's collectives and lax.ppermute only.
A program may use at most 256 MiB of HBM per device.

```python
import math
import jax
import jax.numpy as jnp
import numpy as np
from jax import lax

D = 768
H = 12
HD = 64
FF = 3072
POS = 1024
V = 50304
MB = 2
SEQ = 512
KSEL = 16
STEP = 10
NPARAM = 46508544
N_DP = 16


def vector_rows(base_key):
    gains = jnp.clip(1.0 + 0.15 * jax.random.normal(jax.random.fold_in(base_key, 11), (3, D), jnp.float32), 0.4, 1.6)
    shifts = jnp.clip(0.1 * jax.random.normal(jax.random.fold_in(base_key, 12), (11, D), jnp.float32), -0.5, 0.5)
    final_shift = jnp.clip(0.35 * jax.random.normal(jax.random.fold_in(base_key, 13), (1, D), jnp.float32), -0.5, 0.5)
    shifts = jnp.concatenate([shifts[:2], final_shift, shifts[3:]], axis=0)
    paired = jnp.stack([gains, shifts[:3]], axis=1).reshape(6, D)
    return jnp.concatenate([paired, shifts[3:]], axis=0)


def draw_teacher_vecs(key, part):
    return vector_rows(jax.random.fold_in(key, 1)).astype(jnp.bfloat16)


def draw_vectors(key, part):
    return vector_rows(jax.random.fold_in(key, 2))


def set_ends(array, rng, low, largest):
    longest = array.shape.index(max(array.shape))
    spots = []
    for shift in (0, 1):
        where = [jax.random.randint(jax.random.fold_in(rng, axis), (), 0, length) for axis, length in enumerate(array.shape)]
        where[longest] = (where[longest] + shift) % array.shape[longest]
        spots.append(tuple(where))
    return array.at[spots[0]].set(low).at[spots[1]].set(largest)


def block_levels(rng, dims, pieces, low, top_value):
    factor_of = 1.0
    for dim, shards_of in pieces:
        steps = jax.random.uniform(jax.random.fold_in(jax.random.fold_in(rng, 6), dim), (shards_of,), jnp.float32, low / len(pieces), top_value / len(pieces))
        factor_of = factor_of * jnp.repeat(jnp.exp(steps), dims[dim] // shards_of).reshape((-1,) + (1,) * (len(dims) - 1 - dim))
    return factor_of


def split_up(count, total, limit, slope):
    portions = [(1 << 20) // math.isqrt(rank ** slope) + 1 for rank in range(2, count + 1)]
    rest, holding = total - limit - (count - 1), [1] * (count - 1)
    while rest > 0:
        free = [i for i in range(count - 1) if holding[i] < limit]
        pool, remaining = sum([portions[i] for i in free]), rest
        for i in free:
            addition = min(limit - holding[i], max(1, remaining * portions[i] // pool), rest)
            holding[i] = holding[i] + addition
            rest = rest - addition
    return np.array([limit] + holding)


def uneven(key, count, total, bound, lean):
    if count == 2:
        one = jax.random.randint(key, (), max(1, total - bound), min(bound, total - 1) + 1)
        return jnp.stack([one, total - one])
    lengths = jnp.asarray(split_up(count, total, bound, lean), jnp.int32)
    twos = (count - 1) // 2
    giver, taker = lengths[1:1 + 2 * twos:2], lengths[2:2 + 2 * twos:2]
    slack = jnp.minimum(giver - 1, bound - taker)
    passed = jax.random.randint(jax.random.fold_in(key, 1), (twos,), 0, 1 << 20) % (slack + 1)
    lengths = lengths.at[1:1 + 2 * twos:2].set(giver - passed).at[2:2 + 2 * twos:2].set(taker + passed)
    return lengths[jax.random.permutation(jax.random.fold_in(key, 2), count)]


def assign_block(stream_key, own, number, rows, amount, top, bound, slope):
    order = jax.random.permutation(stream_key, amount)
    packed, usual = load_shares(amount, rows * top, bound, slope, True), load_shares(amount, rows * top, bound, slope, False)
    places = jnp.arange(amount)

    def named(lengths, rotation):
        used = int((lengths > 0).sum())
        fixed = max(1, used // 4)
        shifted = fixed + (places - fixed + rotation * (used - fixed)) % max(1, amount - fixed)
        return jnp.zeros((amount,), jnp.int32).at[order[jnp.where(places < fixed, places, shifted)]].set(jnp.asarray(lengths, jnp.int32))

    lengths = jnp.where(number % 4 == 0, named(packed, number // 4), named(usual, number - number // 4 - 1))
    mixed = jax.random.permutation(jax.random.fold_in(own, 3), amount)
    source_of, receiver = mixed[0:amount // 2 * 2:2], mixed[1:amount // 2 * 2:2]
    slack = jnp.minimum(lengths[source_of] - 1, bound - lengths[receiver]) // 2
    slack = jnp.where((source_of == order[0]) | (receiver == order[0]) | (lengths[receiver] == 0), 0, jnp.maximum(slack, 0))
    shifted = jax.random.randint(jax.random.fold_in(own, 4), (amount // 2,), 0, 1 << 20) % (slack + 1)
    lengths = lengths.at[source_of].add(-shifted).at[receiver].add(shifted)
    members = jnp.searchsorted(jnp.cumsum(lengths), jnp.arange(rows * top), side="right").astype(jnp.int32)
    table = members.reshape(top, rows).T
    table = table[jax.random.permutation(jax.random.fold_in(own, 1), rows)]
    rotation = jax.random.randint(jax.random.fold_in(own, 2), (rows, 1), 0, top)
    return jnp.take_along_axis(table, (jnp.arange(top)[None, :] + rotation) % top, axis=1)


def load_shares(count, total, bound, skew, full):
    loads = [(1 << 20) // math.isqrt(rank ** skew) + 1 for rank in range(1, count + 1)]
    largest = bound if full else min(bound, max(-(-total // count), total * loads[0] // sum(loads)))
    least = 1 if total - largest >= count - 1 else 0
    counts, surplus = [largest] + [least] * (count - 1), total - largest - least * (count - 1)
    while surplus > 0:
        movable = [i for i in range(1, count) if counts[i] < largest] or [i for i in range(1, count) if counts[i] < bound]
        whole, left = sum([loads[i] for i in movable]), surplus
        for i in movable:
            extra = min(bound - counts[i], max(1, left * loads[i] // whole), surplus)
            counts[i] = counts[i] + extra
            surplus = surplus - extra
    return np.array(counts)


def scatter_about(key, extent, scale, bound, split=(), kind=jnp.bfloat16):
    level = block_levels(key, extent, split, -0.22, 0.18) if split else 1.0
    values = jax.random.normal(key, extent, jnp.float32) * scale * level
    return jnp.minimum(jnp.maximum(values, -bound), bound).astype(kind)


def setup_inputs(seed: int = 0) -> dict:
    key_of = jax.random.split(jax.random.key(seed), 33)
    token_shard_keys = jax.random.split(jax.random.fold_in(key_of[0], 1), MB * N_DP * SEQ // SEQ)
    token_shard_turns = jax.random.permutation(jax.random.fold_in(key_of[0], 3), MB * N_DP * SEQ // SEQ)
    token_shard = jax.vmap(lambda own, number: assign_block(jax.random.fold_in(key_of[0], 2), own, number, SEQ, N_DP, 1, 2 * SEQ // N_DP, 1))(token_shard_keys, token_shard_turns).reshape((MB, N_DP, SEQ, 1))
    token_row = set_ends(jax.random.randint(key_of[1], (MB, N_DP, SEQ), 0, V // N_DP), jax.random.fold_in(key_of[1], 1), 0, (V // N_DP) - 1).astype(jnp.int32)
    doc_ids = jax.vmap(lambda own: jnp.searchsorted(jnp.cumsum(uneven(own, 16, SEQ, SEQ // 2, 2)), jnp.arange(SEQ), side="right"))(jax.random.split(key_of[2], MB * N_DP)).reshape((MB, N_DP, SEQ)).astype(jnp.int32)
    loss_rows = set_ends(jax.random.randint(key_of[3], (MB, N_DP, KSEL), 0, SEQ - 1), jax.random.fold_in(key_of[3], 1), 0, (SEQ - 1) - 1).astype(jnp.int32)
    teacher_table = scatter_about(key_of[4], (V, D), 0.07, 0.41992188, ((0, 16),))
    teacher_pos = scatter_about(key_of[5], (POS, D), 0.3, 1.796875, ((0, 16),))
    teacher_attn_in = scatter_about(key_of[6], (D, 3 * D), D ** -0.5, 0.21875, ((0, 16),))
    teacher_attn_out = scatter_about(key_of[7], (D, D), (D // 16) ** -0.5, 0.875, ((0, 16),))
    teacher_mlp_in = scatter_about(key_of[8], (D, FF), D ** -0.5, 0.21875, ((0, 16),))
    teacher_mlp_out = scatter_about(key_of[9], (FF, D), (FF // 4) ** -0.5, 0.21875, ((0, 16),))
    teacher_vecs = draw_teacher_vecs(jax.random.fold_in(key_of[32], 71), 0)
    table = scatter_about(key_of[11], (V, D), 0.07, 0.42, ((0, 16),), jnp.float32)
    pos_table = scatter_about(key_of[12], (POS, D), 0.3, 1.8, ((0, 16),), jnp.float32)
    attn_in = scatter_about(key_of[13], (D, 3 * D), D ** -0.5, 0.21875, ((0, 16),), jnp.float32)
    attn_out = scatter_about(key_of[14], (D, D), (D // 16) ** -0.5, 0.875, ((0, 16),), jnp.float32)
    mlp_in = scatter_about(key_of[15], (D, FF), D ** -0.5, 0.21875, ((0, 16),), jnp.float32)
    mlp_out = scatter_about(key_of[16], (FF, D), (FF // 4) ** -0.5, 0.21875, ((0, 16),), jnp.float32)
    vectors = draw_vectors(jax.random.fold_in(key_of[32], 71), 0)
    table_m = scatter_about(key_of[18], (V, D), (0.00111 * 0.02 / NPARAM ** 0.5), 1.862645149230957e-08, ((0, 16),), jnp.float32)
    pos_m = scatter_about(key_of[19], (POS, D), (0.111 * 0.02 / NPARAM ** 0.5), 1.9073486328125e-06, ((0, 16),), jnp.float32)
    attn_in_m = scatter_about(key_of[20], (D, 3 * D), (0.111 * 0.02 / NPARAM ** 0.5), 1.9073486328125e-06, ((0, 16),), jnp.float32)
    attn_out_m = scatter_about(key_of[21], (D, D), (0.111 * 0.02 / NPARAM ** 0.5), 1.9073486328125e-06, ((0, 16),), jnp.float32)
    mlp_in_m = scatter_about(key_of[22], (D, FF), (0.111 * 0.02 / NPARAM ** 0.5), 1.9073486328125e-06, ((0, 16),), jnp.float32)
    mlp_out_m = scatter_about(key_of[23], (FF, D), (0.111 * 0.02 / NPARAM ** 0.5), 1.9073486328125e-06, ((0, 16),), jnp.float32)
    vectors_m = scatter_about(key_of[24], (14, D), (0.555 * 0.02 / NPARAM ** 0.5), 9.5367431640625e-06, ((1, 16),), jnp.float32)
    table_v = jnp.clip(jnp.exp(math.log(3.440228042218309e-14) - 1.3862944 * jax.random.uniform(key_of[25], (V, D), jnp.float32) ** block_levels(key_of[25], (V, D), ((0, 16),), -0.2, 0.2)), 8.600570105545772e-15, 3.440228042218309e-14)
    pos_v = jnp.clip(jnp.exp(math.log(3.440228042218309e-14) - 1.3862944 * jax.random.uniform(key_of[26], (POS, D), jnp.float32) ** block_levels(key_of[26], (POS, D), ((0, 16),), -0.2, 0.2)), 8.600570105545772e-15, 3.440228042218309e-14)
    attn_in_v = jnp.clip(jnp.exp(math.log(3.440228042218309e-14) - 1.3862944 * jax.random.uniform(key_of[27], (D, 3 * D), jnp.float32) ** block_levels(key_of[27], (D, 3 * D), ((0, 16),), -0.2, 0.2)), 8.600570105545772e-15, 3.440228042218309e-14)
    attn_out_v = jnp.clip(jnp.exp(math.log(3.440228042218309e-14) - 1.3862944 * jax.random.uniform(key_of[28], (D, D), jnp.float32) ** block_levels(key_of[28], (D, D), ((0, 16),), -0.2, 0.2)), 8.600570105545772e-15, 3.440228042218309e-14)
    mlp_in_v = jnp.clip(jnp.exp(math.log(3.440228042218309e-14) - 1.3862944 * jax.random.uniform(key_of[29], (D, FF), jnp.float32) ** block_levels(key_of[29], (D, FF), ((0, 16),), -0.2, 0.2)), 8.600570105545772e-15, 3.440228042218309e-14)
    mlp_out_v = jnp.clip(jnp.exp(math.log(3.440228042218309e-14) - 1.3862944 * jax.random.uniform(key_of[30], (FF, D), jnp.float32) ** block_levels(key_of[30], (FF, D), ((0, 16),), -0.2, 0.2)), 8.600570105545772e-15, 3.440228042218309e-14)
    vectors_v = jnp.clip(jnp.exp(math.log(8.600570342714997e-13) - 1.3862944 * jax.random.uniform(key_of[31], (14, D), jnp.float32) ** block_levels(key_of[31], (14, D), ((1, 16),), -0.2, 0.2)), 2.1501425856787493e-13, 8.600570342714997e-13)
    return {"token_shard": token_shard, "token_row": token_row, "doc_ids": doc_ids, "loss_rows": loss_rows, "teacher_table": teacher_table, "teacher_pos": teacher_pos, "teacher_attn_in": teacher_attn_in, "teacher_attn_out": teacher_attn_out, "teacher_mlp_in": teacher_mlp_in, "teacher_mlp_out": teacher_mlp_out, "teacher_vecs": teacher_vecs, "table": table, "pos_table": pos_table, "attn_in": attn_in, "attn_out": attn_out, "mlp_in": mlp_in, "mlp_out": mlp_out, "vectors": vectors, "table_m": table_m, "pos_m": pos_m, "attn_in_m": attn_in_m, "attn_out_m": attn_out_m, "mlp_in_m": mlp_in_m, "mlp_out_m": mlp_out_m, "vectors_m": vectors_m, "table_v": table_v, "pos_v": pos_v, "attn_in_v": attn_in_v, "attn_out_v": attn_out_v, "mlp_in_v": mlp_in_v, "mlp_out_v": mlp_out_v, "vectors_v": vectors_v}


learn_rate = 0.25
beta_one = 0.9
beta_two = 0.999
adam_eps = 1e-08
decay_rate = 0.1
clip_limit = 0.02
norm_eps = 1e-05
neg_big = -1000000000.0

@jax.custom_vjp
def low(v):
    return lax.optimization_barrier(v.astype(jnp.bfloat16)).astype(jnp.float32)

@jax.custom_vjp
def low_back(v):
    return v

def low_keep(v):
    return (low(v), None)

def low_pass(kept, grad):
    return (grad,)

def back_keep(v):
    return (v, None)

def back_low(kept, grad):
    return (low(grad),)
low.defvjp(low_keep, low_pass)
low_back.defvjp(back_keep, back_low)

def high_dot(left_side, right_side):
    return jnp.dot(left_side, right_side, precision=lax.Precision.HIGHEST, preferred_element_type=jnp.float32)

def layer_norm(values, norm_gain, norm_shift):
    center = lax.optimization_barrier(jnp.mean(values, axis=-1, keepdims=True))
    offsets = values - center
    spread = lax.optimization_barrier(jnp.mean(offsets * offsets, axis=-1, keepdims=True))
    return offsets * lax.rsqrt(spread + norm_eps) * norm_gain + norm_shift

def gelu_tanh(values):
    return jax.nn.gelu(values, approximate=True)

def doc_positions(doc_row):
    indices = jnp.arange(doc_row.shape[0], dtype=jnp.int32)
    starts_here = jnp.concatenate([jnp.ones((1,), dtype=bool), doc_row[1:] != doc_row[:-1]])
    first_index = lax.cummax(jnp.where(starts_here, indices, 0), axis=0)
    return indices - first_index

def sequence_forward(weights, token_ids, doc_row, chosen):
    tab, pos_rows, w_attn_in, w_attn_out, w_mlp_in, w_mlp_out, vec_rows = weights
    length = token_ids.shape[0]
    positions = doc_positions(doc_row)
    x_embed = low_back(tab[token_ids]) + pos_rows[positions]
    normed_one = low(layer_norm(x_embed, vec_rows[0], vec_rows[1]))
    qkv_bias = jnp.concatenate([vec_rows[6], jnp.zeros_like(vec_rows[6]), vec_rows[7]])
    qkv_vals = low(low_back(high_dot(normed_one, w_attn_in) + qkv_bias))
    split_parts = qkv_vals.reshape(length, 3, H, HD)
    scaling = HD ** (-0.5)
    scores = jnp.einsum('qhd,khd->hqk', split_parts[:, 0], split_parts[:, 1], precision=lax.Precision.HIGHEST) * scaling
    scores = low_back(scores)
    indices = jnp.arange(length)
    allowed = (doc_row[:, None] == doc_row[None, :]) & (indices[None, :] <= indices[:, None])
    scores = jnp.where(allowed[None], scores, neg_big)
    row_max = lax.optimization_barrier(jnp.max(scores, axis=-1, keepdims=True))
    weights_exp = jnp.exp(scores - row_max)
    probs = weights_exp / lax.optimization_barrier(jnp.sum(weights_exp, axis=-1, keepdims=True))
    attended = jnp.einsum('hqk,khd->qhd', low(probs), split_parts[:, 2], precision=lax.Precision.HIGHEST).reshape(length, D)
    attended = low(low_back(attended))
    x_mid = x_embed + low_back(high_dot(attended, w_attn_out) + vec_rows[8])
    normed_two = low(layer_norm(x_mid, vec_rows[2], vec_rows[3]))
    pre_act = low_back(high_dot(normed_two, w_mlp_in) + vec_rows[10:].reshape(-1))
    x_top = x_mid + low_back(high_dot(low(gelu_tanh(pre_act)), w_mlp_out) + vec_rows[9])
    return low(layer_norm(x_top[chosen], vec_rows[4], vec_rows[5]))

def row_logsumexp(logits):
    row_max = lax.optimization_barrier(jnp.max(logits, axis=1, keepdims=True))
    return row_max + jnp.log(lax.optimization_barrier(jnp.sum(jnp.exp(logits - row_max), axis=1, keepdims=True)))

def head_sums(hidden, teacher_hidden, tab, teacher_tab, targets):
    logits = low_back(high_dot(hidden, tab.T))
    teacher_logits = high_dot(teacher_hidden, teacher_tab.T)
    own_total = row_logsumexp(logits)
    teacher_total = row_logsumexp(teacher_logits)
    picked = jnp.take_along_axis(logits, targets[:, None], axis=1)
    teacher_prob = jnp.exp(teacher_logits - teacher_total)
    kl_rows = lax.optimization_barrier(jnp.sum(teacher_prob * (teacher_logits - teacher_total - logits + own_total), axis=1))
    return (jnp.sum(own_total - picked), jnp.sum(kl_rows))

def adam_update(master, moment_one, moment_two, gradient, factor):
    clipped = gradient * factor
    new_one = beta_one * moment_one + (1.0 - beta_one) * clipped
    new_two = beta_two * moment_two + (1.0 - beta_two) * clipped * clipped
    fixed_one = new_one / (1.0 - beta_one ** STEP)
    fixed_two = new_two / (1.0 - beta_two ** STEP)
    updated = master - learn_rate * (fixed_one / (jnp.sqrt(fixed_two) + adam_eps) + decay_rate * master)
    return (updated, new_one, new_two)

def reference(token_shard, token_row, doc_ids, loss_rows, teacher_table, teacher_pos, teacher_attn_in, teacher_attn_out, teacher_mlp_in, teacher_mlp_out, teacher_vecs, table, pos_table, attn_in, attn_out, mlp_in, mlp_out, vectors, table_m, pos_m, attn_in_m, attn_out_m, mlp_in_m, mlp_out_m, vectors_m, table_v, pos_v, attn_in_v, attn_out_v, mlp_in_v, mlp_out_v, vectors_v):
    vocab_rows = V // N_DP
    token_ids = (token_shard[..., 0] * vocab_rows + token_row).reshape(MB * N_DP, SEQ).astype(jnp.int32)
    doc_rows = doc_ids.reshape(MB * N_DP, SEQ)
    chosen = loss_rows.reshape(MB * N_DP, KSEL).astype(jnp.int32)
    targets = jnp.take_along_axis(token_ids, chosen + 1, axis=1).reshape(MB, N_DP * KSEL)
    teacher_w = tuple((part.astype(jnp.float32) for part in (teacher_table, teacher_pos, teacher_attn_in, teacher_attn_out, teacher_mlp_in, teacher_mlp_out, teacher_vecs)))
    row_count = MB * N_DP * KSEL

    def run_all(weights):

        def one_sequence(one_item):
            return sequence_forward(weights, one_item[0], one_item[1], one_item[2])
        return lax.map(jax.checkpoint(one_sequence), (token_ids, doc_rows, chosen)).reshape(MB, N_DP * KSEL, D)
    teacher_hidden = run_all(teacher_w)
    masters = (table, pos_table, attn_in, attn_out, mlp_in, mlp_out, vectors)

    def loss_of(params):
        weights = tuple((low(part) for part in params))
        hidden = run_all(weights)

        def one_batch(one_item):
            return head_sums(one_item[0], one_item[1], weights[0], teacher_w[0], one_item[2])
        ce_sums, kl_sums = lax.map(jax.checkpoint(one_batch), (hidden, teacher_hidden, targets))
        return ((jnp.sum(ce_sums) + jnp.sum(kl_sums)) / row_count, jnp.sum(kl_sums) / row_count)
    loss_value, pullback, kl_value = jax.vjp(loss_of, masters, has_aux=True)
    grads = pullback(jnp.ones_like(loss_value))[0]
    squares = jnp.zeros((), jnp.float32)
    for gradient in grads:
        squares = squares + jnp.sum(gradient * gradient)
    grad_norm = jnp.sqrt(squares)
    factor = jnp.minimum(1.0, clip_limit / (grad_norm + 1e-06))
    firsts = (table_m, pos_m, attn_in_m, attn_out_m, mlp_in_m, mlp_out_m, vectors_m)
    seconds = (table_v, pos_v, attn_in_v, attn_out_v, mlp_in_v, mlp_out_v, vectors_v)
    results = []
    for master, moment_one, moment_two, gradient in zip(masters, firsts, seconds, grads):
        results.extend(adam_update(master, moment_one, moment_two, gradient, factor))
    return (results[0], results[1], results[2], results[3], results[4], results[5], results[6], results[7], results[8], results[9], results[10], results[11], results[12], results[13], results[14], results[15], results[16], results[17], results[18], results[19], results[20], grad_norm, kl_value)
```

```python
import jax
import jax.numpy as jnp
from jax import lax
from jax.sharding import PartitionSpec as P

H = 12
MB = 2
STEP = 10
LONGEST = 256
LANES = 128


learn_rate = 0.25
beta_one = 0.9
beta_two = 0.999
adam_eps = 1e-08
decay_rate = 0.1
clip_limit = 0.02
norm_eps = 1e-05
neg_big = -1000000000.0

low = jnp.bfloat16
wide = jnp.float32


def layer_norm(values, norm_gain, norm_shift):
    center = jnp.mean(values, axis=-1, keepdims=True)
    offsets = values - center
    spread = jnp.mean(offsets * offsets, axis=-1, keepdims=True)
    return offsets * lax.rsqrt(spread + norm_eps) * norm_gain + norm_shift


def gelu_tanh(values):
    return jax.nn.gelu(values, approximate=True)


def dot_plain(left_side, right_side):
    return jnp.dot(left_side, right_side, preferred_element_type=wide)


def dot_first(left_side, right_side):
    return lax.dot_general(
        left_side, right_side, (((0,), (0,)), ((), ())), preferred_element_type=wide
    )


def dot_last(left_side, right_side):
    return lax.dot_general(
        left_side, right_side, (((1,), (1,)), ((), ())), preferred_element_type=wide
    )


def exact_rows(one_hot, values):
    return lax.dot_general(
        one_hot.astype(wide),
        values,
        (((1,), (0,)), ((), ())),
        precision=lax.Precision.HIGHEST,
        preferred_element_type=wide,
    )


def chip_ring(chips):
    if chips % 8:
        return list(range(chips))
    if chips == 8:
        return [0, 2, 4, 6, 7, 5, 3, 1]
    lines = chips // 4
    order = list(range(lines))
    for k in range(0, lines - 3, 4):
        order[k + 2], order[k + 3] = order[k + 3], order[k + 2]
    ring = [order[0] * 4]
    for k, line in enumerate(order):
        columns = (1, 2, 3) if k % 2 == 0 else (3, 2, 1)
        ring = ring + [line * 4 + column for column in columns]
    return ring + [line * 4 for line in reversed(order[1:])]


def ring_gather(block):
    devices = lax.axis_size("dp")
    if devices % 4:
        return lax.all_gather(block, "dp", axis=0)
    chips = devices // 2
    ring = chip_ring(chips)
    place_of = [ring.index(chip) for chip in range(chips)]
    me = lax.axis_index("dp")
    core = me % 2
    place = jnp.asarray(place_of, jnp.int32)[me // 2]
    onward = [(2 * ring[k] + c, 2 * ring[(k + 1) % chips] + c) for k in range(chips) for c in (0, 1)]
    backward = [(there, here) for here, there in onward]
    across = [(d, d ^ 1) for d in range(devices)]
    half_rows = block.shape[0] // 2
    whole = jnp.zeros((devices,) + block.shape, block.dtype)

    def keep(whole, piece, distance):
        chip = jnp.asarray(ring, jnp.int32)[(place + distance) % chips]
        partner = lax.ppermute(piece, "dp", across)
        whole = lax.dynamic_update_slice(whole, piece[None], (2 * chip + core, 0, 0))
        return lax.dynamic_update_slice(whole, partner[None], (2 * chip + 1 - core, 0, 0))

    ahead, behind = block, block
    whole = keep(whole, block, 0)
    for distance in range(1, chips // 2):
        ahead = lax.ppermute(ahead, "dp", onward)
        behind = lax.ppermute(behind, "dp", backward)
        whole = keep(whole, ahead, -distance)
        whole = keep(whole, behind, distance)
    first = lax.ppermute(ahead[:half_rows], "dp", onward)
    second = lax.ppermute(behind[half_rows:], "dp", backward)
    return keep(whole, jnp.concatenate([first, second], axis=0), chips // 2)


def pack(attn_in, attn_out, mlp_in, mlp_out, pos, vecs):
    rows = attn_in.shape[0]
    width = attn_out.shape[1]
    folds = mlp_out.shape[0] // rows
    folded = mlp_out.reshape(folds, rows, width).transpose(1, 0, 2).reshape(rows, folds * width)
    turned = jnp.pad(vecs.T, ((0, 0), (0, LANES - vecs.shape[0])))
    return jnp.concatenate([attn_in, attn_out, mlp_in, folded, pos.reshape(rows, -1), turned], axis=1)


def unpack(whole, width, hidden, vec_count):
    devices, rows = whole.shape[:2]
    folds = hidden // width
    flat = whole.reshape(devices * rows, -1)
    cuts = [3 * width, width, hidden, hidden]
    starts = [0, 3 * width, 4 * width, 4 * width + hidden]
    attn_in, attn_out, mlp_in, folded = [
        flat[:, start : start + cut] for start, cut in zip(starts, cuts)
    ]
    mlp_out = folded.reshape(devices, rows, folds, width).transpose(0, 2, 1, 3).reshape(hidden, width)
    pos_start = 4 * width + 2 * hidden
    pos_width = flat.shape[1] - pos_start - LANES
    pos_rows = LONGEST * width // pos_width
    pos = flat[:pos_rows, pos_start : pos_start + pos_width].reshape(LONGEST, width)
    vecs = flat[:, flat.shape[1] - LANES :][:, :vec_count].T
    return attn_in, attn_out, mlp_in, mlp_out, pos, vecs


def head_marks(width):
    size = width // H
    columns = jnp.arange(width, dtype=jnp.int32) // size
    return columns[None, None, :] == jnp.arange(H, dtype=jnp.int32)[:, None, None]


def by_head(rows, marks):
    spread = jnp.where(marks, rows[None], jnp.zeros((), rows.dtype))
    return spread.reshape(-1, rows.shape[1])


def from_heads(spread, marks):
    parts = spread.reshape(H, -1, spread.shape[1])
    return jnp.sum(jnp.where(marks, parts, 0.0), axis=0)


def attend(queries, keys_all, values, allowed, marks):
    scaling = (queries.shape[1] // H) ** (-0.5)
    scores = dot_last(by_head(queries, marks), keys_all) * scaling
    scores = jnp.where(allowed, scores, neg_big)
    row_max = jnp.max(scores, axis=-1, keepdims=True)
    weights_exp = jnp.exp(scores - row_max)
    probs = weights_exp / jnp.sum(weights_exp, axis=-1, keepdims=True)
    attended = from_heads(dot_plain(probs.astype(low), values), marks).astype(low)
    return attended, probs


def attend_back(d_attended, queries, keys_all, values, probs, marks):
    scaling = (queries.shape[1] // H) ** (-0.5)
    d_spread = by_head(d_attended, marks)
    d_probs = dot_last(d_spread, values)
    row_inner = jnp.sum(probs * d_probs, axis=-1, keepdims=True)
    d_scores = (probs * (d_probs - row_inner)).astype(low)
    query_grads = from_heads(dot_plain(d_scores, keys_all), marks) * scaling
    key_grads = dot_first(d_scores, by_head(queries, marks)) * scaling
    value_grads = dot_first(probs.astype(low), d_spread)
    return query_grads.astype(low), key_grads.astype(low), value_grads.astype(low)


def adam_update(master, moment_one, moment_two, gradient, factor):
    clipped = gradient * factor
    new_one = beta_one * moment_one + (1.0 - beta_one) * clipped
    new_two = beta_two * moment_two + (1.0 - beta_two) * clipped * clipped
    fixed_one = new_one / (1.0 - beta_one**STEP)
    fixed_two = new_two / (1.0 - beta_two**STEP)
    updated = master - learn_rate * (
        fixed_one / (jnp.sqrt(fixed_two) + adam_eps) + decay_rate * master
    )
    return (updated, new_one, new_two)


def to_all(value, axis):
    copies = lax.axis_size(axis)
    spread = jnp.broadcast_to(value[None], (copies,) + value.shape)
    return lax.all_to_all(spread, axis, split_axis=0, concat_axis=0, tiled=True)


def shards(
    token_shard,
    token_row,
    doc_ids,
    loss_rows,
    teacher_table,
    teacher_pos,
    teacher_attn_in,
    teacher_attn_out,
    teacher_mlp_in,
    teacher_mlp_out,
    teacher_vecs,
    table,
    pos_table,
    attn_in,
    attn_out,
    mlp_in,
    mlp_out,
    vectors,
    table_m,
    pos_m,
    attn_in_m,
    attn_out_m,
    mlp_in_m,
    mlp_out_m,
    vectors_m,
    table_v,
    pos_v,
    attn_in_v,
    attn_out_v,
    mlp_in_v,
    mlp_out_v,
    vectors_v,
):
    part = lax.axis_index("pair")
    is_student = part == 1
    me = lax.axis_index("dp")
    devices = lax.axis_size("dp")
    vocab_rows, width = table.shape
    hidden = mlp_in.shape[1]
    rows = attn_in.shape[0]
    vec_count = vectors.shape[0]
    pos_count = pos_table.shape[0]
    swap = [(0, 1), (1, 0)]
    to_teacher = [(1, 0)]
    to_student = [(0, 1)]

    own_block = jnp.where(
        is_student,
        pack(*[w.astype(low) for w in (attn_in, attn_out, mlp_in, mlp_out, pos_table, vectors)]),
        pack(
            teacher_attn_in,
            teacher_attn_out,
            teacher_mlp_in,
            teacher_mlp_out,
            teacher_pos,
            teacher_vecs,
        ),
    )
    whole = ring_gather(own_block)
    w_attn_in, w_attn_out, w_mlp_in, w_mlp_out, w_pos, w_vecs = unpack(
        whole, width, hidden, vec_count
    )
    vec = w_vecs.astype(wide)

    owners = token_shard[:, 0, :, 0]
    shard_rows = token_row[:, 0]
    docs = doc_ids[:, 0]
    chosen = loss_rows[:, 0]
    length = owners.shape[1]
    picks = chosen.shape[1]
    capacity = 2 * length // devices
    total_rows = MB * devices * picks
    indices = jnp.arange(length, dtype=jnp.int32)
    before = indices[None, :] < indices[:, None]
    same_owner = owners[:, :, None] == owners[:, None, :]
    slot = owners * capacity + jnp.sum(same_owner & before, axis=-1, dtype=jnp.int32)
    positions = indices - jnp.sum(docs[:, None, :] < docs[:, :, None], axis=-1, dtype=jnp.int32)
    slots = jnp.arange(devices * capacity, dtype=jnp.int32)
    filled = slots[None, :, None] == slot[:, None, :]
    request = vocab_rows + jnp.sum(
        jnp.where(filled, shard_rows[:, None, :] - vocab_rows, 0), axis=-1
    )
    request = request.reshape(MB, devices, capacity).transpose(1, 0, 2).reshape(devices, -1)
    is_next = indices[None, None, :] == (chosen + 1)[:, :, None]
    next_ids = jnp.sum(
        jnp.where(is_next, (owners * vocab_rows + shard_rows)[:, None, :], 0), axis=-1
    )
    notes = jnp.broadcast_to(next_ids.reshape(1, -1), (devices, MB * picks))
    arrived_notes = lax.all_to_all(
        jnp.concatenate([request, notes], axis=1), "dp", split_axis=0, concat_axis=0, tiled=True
    )
    asked = arrived_notes[:, : MB * capacity].reshape(devices, MB, capacity).transpose(1, 0, 2)
    asked = asked.reshape(MB, devices * capacity)
    targets = arrived_notes[:, MB * capacity :].reshape(devices, MB, picks).transpose(1, 0, 2)
    targets = targets.reshape(MB, devices * picks)[part]

    safe = jnp.minimum(asked, vocab_rows - 1)
    found = lax.cond(
        is_student,
        lambda at: jnp.take(table, at, axis=0).astype(low),
        lambda at: jnp.take(teacher_table, at, axis=0),
        safe,
    )
    marks = head_marks(width)
    kept = []
    for m in range(MB):
        back = lax.all_to_all(
            found[m].reshape(devices, capacity, width),
            "dp",
            split_axis=0,
            concat_axis=0,
            tiled=True,
        ).reshape(devices * capacity, width)
        sources = jnp.concatenate([back, w_pos], axis=0)
        spots = jnp.arange(LONGEST, dtype=jnp.int32)
        pick_row = jnp.concatenate(
            [slot[m][:, None] == slots[None, :], positions[m][:, None] == spots[None, :]], axis=1
        ).astype(low)
        is_chosen = chosen[m][:, None] == indices[None, :]
        slot_c = jnp.sum(jnp.where(is_chosen, slot[m][None], 0), axis=1)
        position_c = jnp.sum(jnp.where(is_chosen, positions[m][None], 0), axis=1)
        doc_c = jnp.sum(jnp.where(is_chosen, docs[m][None], 0), axis=1)
        pick_c = jnp.concatenate(
            [slot_c[:, None] == slots[None, :], position_c[:, None] == spots[None, :]], axis=1
        ).astype(low)
        x_embed = dot_plain(pick_row, sources)
        x_embed_c = dot_plain(pick_c, sources)
        normed_one = layer_norm(x_embed, vec[0], vec[1]).astype(low)
        normed_one_c = layer_norm(x_embed_c, vec[0], vec[1]).astype(low)
        kv_bias = jnp.concatenate([jnp.zeros((width,), wide), vec[7]])
        kv_low = (dot_plain(normed_one, w_attn_in[:, width:]) + kv_bias).astype(low)
        queries = (dot_plain(normed_one_c, w_attn_in[:, :width]) + vec[6]).astype(low)
        allowed = (doc_c[:, None] == docs[m][None, :]) & (indices[None, :] <= chosen[m][:, None])
        allowed = jnp.broadcast_to(allowed[None], (H,) + allowed.shape).reshape(-1, length)
        attended, probs = attend(queries, kv_low[:, :width], kv_low[:, width:], allowed, marks)
        kept.append(
            (x_embed, x_embed_c, normed_one, kv_low, queries, attended, probs, pick_row, is_chosen)
        )

    x_embed_c = jnp.concatenate([k[1] for k in kept], axis=0)
    attended = jnp.concatenate([k[5] for k in kept], axis=0)
    x_mid = x_embed_c + dot_plain(attended, w_attn_out) + vec[8]
    normed_two = layer_norm(x_mid, vec[2], vec[3]).astype(low)
    pre_act = dot_plain(normed_two, w_mlp_in) + vec[10:].reshape(-1)
    activated = gelu_tanh(pre_act).astype(low)
    x_top = x_mid + dot_plain(activated, w_mlp_out) + vec[9]
    final = layer_norm(x_top, vec[4], vec[5]).astype(low).reshape(MB, picks, width)

    other_final = lax.ppermute(final[1 - part], "pair", swap)
    own_final = final[part]
    both = jnp.stack(
        [
            jnp.where(is_student, other_final, own_final),
            jnp.where(is_student, own_final, other_final),
        ]
    )
    every = lax.all_gather(both.reshape(2 * picks, width), "dp", axis=0)
    every = every.reshape(devices, 2, picks, width).transpose(1, 0, 2, 3)
    every = every.reshape(2, devices * picks, width)
    teacher_rows, student_rows = every[0], every[1]
    table_low = table.astype(low)
    teacher_logits = dot_last(teacher_rows, teacher_table)
    logits = dot_last(student_rows, table_low)
    teacher_max = jnp.max(teacher_logits, axis=1)
    teacher_sum = jnp.sum(jnp.exp(teacher_logits - teacher_max[:, None]), axis=1)
    own_max = jnp.max(logits, axis=1)
    own_sum = jnp.sum(jnp.exp(logits - own_max[:, None]), axis=1)
    stats = to_all(jnp.stack([teacher_max, teacher_sum, own_max, own_sum]), "dp")

    def log_total(maxima, sums):
        big = jnp.max(maxima, axis=0)
        return big + jnp.log(jnp.sum(sums * jnp.exp(maxima - big[None]), axis=0))

    teacher_total = log_total(stats[:, 0], stats[:, 1])[:, None]
    own_total = log_total(stats[:, 2], stats[:, 3])[:, None]
    teacher_log = teacher_logits - teacher_total
    teacher_prob = jnp.exp(teacher_log)
    own_log = logits - own_total
    own_prob = jnp.exp(own_log)
    kl_local = jnp.sum(teacher_prob * (teacher_log - own_log))
    vocab_iota = jnp.arange(vocab_rows, dtype=jnp.int32)
    target_hit = (targets - me * vocab_rows)[:, None] == vocab_iota[None, :]
    d_logits = (2.0 * own_prob - target_hit.astype(wide) - teacher_prob) * (1.0 / total_rows)
    d_low = d_logits.astype(low)
    d_final_parts = dot_plain(d_low, table_low).astype(low).reshape(devices, picks, width)
    d_final_parts = lax.all_to_all(d_final_parts, "dp", split_axis=0, concat_axis=0, tiled=True)
    d_final = jnp.sum(d_final_parts.astype(wide), axis=0)
    d_final_first = lax.ppermute(d_final, "pair", to_student)
    d_final = jnp.concatenate([d_final_first, d_final], axis=0)
    d_low_other = lax.ppermute(d_low, "pair", swap)
    student_rows_other = lax.ppermute(student_rows, "pair", swap)

    final_back = jax.vjp(layer_norm, x_top, vec[4], vec[5])[1]
    d_top, d_gain_final, d_shift_final = final_back(d_final)
    d_branch = d_top.astype(low)
    d_act = dot_last(d_branch, w_mlp_out)
    d_pre = jax.vjp(gelu_tanh, pre_act)[1](d_act)[0].astype(low)
    d_normed_two = dot_last(d_pre, w_mlp_in)
    d_mid, d_gain_two, d_shift_two = jax.vjp(layer_norm, x_mid, vec[2], vec[3])[1](d_normed_two)
    d_mid = d_top + d_mid
    d_attn_branch = d_mid.astype(low)
    d_attended = dot_last(d_attn_branch, w_attn_out).astype(low)

    def column_blocks(values):
        return values.reshape(values.shape[0], devices, -1).transpose(1, 0, 2)

    lefts = jnp.concatenate(
        [column_blocks(activated), column_blocks(normed_two), column_blocks(attended)], axis=2
    )
    rights = jnp.concatenate([d_branch, d_pre, d_attn_branch], axis=1)
    lefts = lax.ppermute(lefts, "pair", to_teacher) + jnp.where(is_student, lefts, 0)
    rights = lax.ppermute(rights, "pair", to_teacher) + jnp.where(is_student, rights, 0)
    lefts = lax.all_to_all(lefts, "dp", split_axis=0, concat_axis=0, tiled=True)
    lefts = lefts.reshape(-1, lefts.shape[2])
    rights = lax.all_gather(rights, "dp", axis=0, tiled=True)
    fold_rows = mlp_out.shape[0]
    g_mlp_out = dot_first(lefts[:, :fold_rows], rights[:, :width])
    g_mlp_in = dot_first(lefts[:, fold_rows : fold_rows + rows], rights[:, width : width + hidden])
    g_attn_out = dot_first(lefts[:, fold_rows + rows :], rights[:, width + hidden :])

    g_attn_in = jnp.zeros((width, 3 * width), wide)
    g_pos = jnp.zeros((LONGEST, width), wide)
    d_gain_one = jnp.zeros((width,), wide)
    d_shift_one = jnp.zeros((width,), wide)
    qkv_sums = jnp.zeros((3 * width,), wide)
    sent = []
    for m in range(MB):
        x_embed, _, normed_one, kv_low, queries, _, probs, pick_row, is_chosen = kept[m]
        d_query_c, d_keys, d_values = attend_back(
            d_attended[m * picks : (m + 1) * picks],
            queries,
            kv_low[:, :width],
            kv_low[:, width:],
            probs,
            marks,
        )
        to_chosen = is_chosen.T
        d_queries = dot_plain(to_chosen.astype(low), d_query_c).astype(low)
        d_qkv = jnp.concatenate([d_queries, d_keys, d_values], axis=1)
        g_attn_in = g_attn_in + dot_first(normed_one, d_qkv)
        qkv_sums = qkv_sums + jnp.sum(d_qkv, axis=0, dtype=wide)
        d_normed_one = dot_last(d_qkv, w_attn_in)
        norm_one_back = jax.vjp(layer_norm, x_embed, vec[0], vec[1])[1]
        d_embed, d_gain, d_shift = norm_one_back(d_normed_one)
        d_gain_one = d_gain_one + d_gain
        d_shift_one = d_shift_one + d_shift
        d_embed = d_embed + exact_rows(to_chosen, d_mid[m * picks : (m + 1) * picks])
        d_embed = d_embed.astype(low)
        slot_count = devices * capacity
        g_pos = g_pos + dot_first(pick_row[:, slot_count:], d_embed)
        here = lax.ppermute(d_embed, "pair", to_teacher) + jnp.where(is_student, d_embed, 0)
        out_rows = dot_first(pick_row[:, :slot_count], here).astype(low)
        sent.append(
            lax.all_to_all(
                out_rows.reshape(devices, capacity, width),
                "dp",
                split_axis=0,
                concat_axis=0,
                tiled=True,
            ).reshape(slot_count, width)
        )

    vector_part = jnp.stack(
        [
            d_gain_one,
            d_shift_one,
            d_gain_two,
            d_shift_two,
            d_gain_final,
            d_shift_final,
            qkv_sums[:width],
            qkv_sums[2 * width :],
            jnp.sum(d_attn_branch, axis=0, dtype=wide),
            jnp.sum(d_branch, axis=0, dtype=wide),
        ]
    )
    bias_part = jnp.sum(d_pre, axis=0, dtype=wide).reshape(-1, width)
    g_vecs = jnp.concatenate([vector_part, bias_part], axis=0)
    g_vecs = jnp.pad(g_vecs.T, ((0, 0), (0, LANES - vec_count)))
    pos_share = LONGEST // devices
    shared = jnp.concatenate([g_attn_in, g_vecs, g_pos.reshape(width, -1)], axis=1).astype(low)
    shared = lax.psum_scatter(shared, "dp", scatter_dimension=0, tiled=True)
    shared = lax.ppermute(shared, "pair", to_teacher) + jnp.where(is_student, shared, 0)
    shared = shared.astype(wide)
    g_attn_in = shared[:, : 3 * width]
    g_vecs = shared[:, 3 * width : 3 * width + vec_count].T
    pos_near = shared[:, 3 * width + LANES :].reshape(pos_share, width).astype(low)
    pos_near = lax.all_gather(pos_near, "dp", axis=0, tiled=True).astype(wide)
    pos_all = jnp.concatenate([pos_near, jnp.zeros((pos_count, width), wide)], axis=0)
    g_pos = lax.dynamic_slice(
        pos_all, (jnp.minimum(me * pos_count, LONGEST), 0), (pos_count, width)
    )

    d_low_all = jnp.concatenate(
        [jnp.where(is_student, d_low_other, d_low), jnp.where(is_student, d_low, d_low_other)],
        axis=0,
    )
    rows_all = jnp.concatenate(
        [
            jnp.where(is_student, student_rows_other, student_rows),
            jnp.where(is_student, student_rows, student_rows_other),
        ],
        axis=0,
    )
    arrived = jnp.concatenate(sent, axis=0)
    wanted = (asked.reshape(-1)[:, None] == vocab_iota[None, :]).astype(low)
    g_table = dot_first(d_low_all, rows_all) + dot_first(wanted, arrived)

    summed = (g_attn_in, g_attn_out, g_mlp_in, g_mlp_out, g_pos, g_vecs, g_table)
    squares = jnp.zeros((), wide)
    for gradient in summed:
        squares = squares + jnp.sum(gradient * gradient)
    lane = jnp.arange(LANES, dtype=jnp.int32)[None, :]
    totals = to_all(
        jnp.where(lane == 0, squares, jnp.where(lane == 1, kl_local, 0.0)), ("pair", "dp")
    )
    grad_norm = jnp.sqrt(jnp.sum(totals[devices:, 0, 0]))
    kl_mean = jnp.sum(totals[:, 0, 1]) / total_rows
    factor = jnp.minimum(1.0, clip_limit / (grad_norm + 1e-06))
    table_out = adam_update(table, table_m, table_v, summed[6], factor)
    pos_out = adam_update(pos_table, pos_m, pos_v, summed[4], factor)
    attn_in_out = adam_update(attn_in, attn_in_m, attn_in_v, summed[0], factor)
    attn_out_out = adam_update(attn_out, attn_out_m, attn_out_v, summed[1], factor)
    mlp_in_out = adam_update(mlp_in, mlp_in_m, mlp_in_v, summed[2], factor)
    mlp_out_out = adam_update(mlp_out, mlp_out_m, mlp_out_v, summed[3], factor)
    vectors_out = adam_update(vectors, vectors_m, vectors_v, summed[5], factor)
    return (
        *table_out,
        *pos_out,
        *attn_in_out,
        *attn_out_out,
        *mlp_in_out,
        *mlp_out_out,
        *vectors_out,
        grad_norm,
        kl_mean,
    )


def solution(mesh):
    return jax.shard_map(
        shards,
        mesh=mesh,
        in_specs=(
            P(None, "dp", None, None),
            P(None, "dp", None),
            P(None, "dp", None),
            P(None, "dp", None),
            P("dp", None),
            P("dp", None),
            P("dp", None),
            P("dp", None),
            P("dp", None),
            P("dp", None),
            P(None, "dp"),
            P("dp", None),
            P("dp", None),
            P("dp", None),
            P("dp", None),
            P("dp", None),
            P("dp", None),
            P(None, "dp"),
            P("dp", None),
            P("dp", None),
            P("dp", None),
            P("dp", None),
            P("dp", None),
            P("dp", None),
            P(None, "dp"),
            P("dp", None),
            P("dp", None),
            P("dp", None),
            P("dp", None),
            P("dp", None),
            P("dp", None),
            P(None, "dp"),
        ),
        out_specs=(
            P("dp", None),
            P("dp", None),
            P("dp", None),
            P("dp", None),
            P("dp", None),
            P("dp", None),
            P("dp", None),
            P("dp", None),
            P("dp", None),
            P("dp", None),
            P("dp", None),
            P("dp", None),
            P("dp", None),
            P("dp", None),
            P("dp", None),
            P("dp", None),
            P("dp", None),
            P("dp", None),
            P(None, "dp"),
            P(None, "dp"),
            P(None, "dp"),
            P(),
            P(),
        ),
        check_vma=False,
    )
```

```python
import functools

import jax
import jax.numpy as jnp
from jax import lax
from jax.experimental import pallas as pl
from jax.experimental.pallas import tpu as pltpu
from jax.sharding import PartitionSpec as P

H = 12
MB = 2
STEP = 10
LONGEST = 256
LANES = 128
VMEM_BYTES = 56 * 1024 * 1024


learn_rate = 0.25
beta_one = 0.9
beta_two = 0.999
adam_eps = 1e-08
decay_rate = 0.1
clip_limit = 0.02
norm_eps = 1e-05
neg_big = -1000000000.0
gelu_scale = 0.7978845608028654
gelu_cube = 0.044715

low = jnp.bfloat16
wide = jnp.float32


def layer_norm(values, norm_gain, norm_shift):
    center = jnp.mean(values, axis=-1, keepdims=True)
    offsets = values - center
    spread = jnp.mean(offsets * offsets, axis=-1, keepdims=True)
    return offsets * lax.rsqrt(spread + norm_eps) * norm_gain + norm_shift


def gelu_tanh(values):
    return jax.nn.gelu(values, approximate=True)


def dot_plain(left_side, right_side):
    return jnp.dot(left_side, right_side, preferred_element_type=wide)


def dot_first(left_side, right_side):
    return lax.dot_general(
        left_side, right_side, (((0,), (0,)), ((), ())), preferred_element_type=wide
    )


def dot_last(left_side, right_side):
    return lax.dot_general(
        left_side, right_side, (((1,), (1,)), ((), ())), preferred_element_type=wide
    )


def chip_ring(chips):
    if chips % 8:
        return list(range(chips))
    if chips == 8:
        return [0, 2, 4, 6, 7, 5, 3, 1]
    lines = chips // 4
    order = list(range(lines))
    for k in range(0, lines - 3, 4):
        order[k + 2], order[k + 3] = order[k + 3], order[k + 2]
    ring = [order[0] * 4]
    for k, line in enumerate(order):
        columns = (1, 2, 3) if k % 2 == 0 else (3, 2, 1)
        ring = ring + [line * 4 + column for column in columns]
    return ring + [line * 4 for line in reversed(order[1:])]


def ring_gather(block, hold):
    devices = lax.axis_size("dp")
    if devices % 4:
        return lax.all_gather(block, "dp", axis=0), hold
    chips = devices // 2
    ring = chip_ring(chips)
    place_of = [ring.index(chip) for chip in range(chips)]
    me = lax.axis_index("dp")
    core = me % 2
    place = jnp.asarray(place_of, jnp.int32)[me // 2]
    onward = [(2 * ring[k] + c, 2 * ring[(k + 1) % chips] + c) for k in range(chips) for c in (0, 1)]
    backward = [(there, here) for here, there in onward]
    across = [(d, d ^ 1) for d in range(devices)]
    half_rows = block.shape[0] // 32 * 16
    whole = jnp.zeros((devices,) + block.shape, block.dtype)

    def keep(whole, piece, distance):
        chip = jnp.asarray(ring, jnp.int32)[(place + distance) % chips]
        partner = lax.ppermute(piece, "dp", across)
        whole = lax.dynamic_update_slice(whole, piece[None], (2 * chip + core, 0, 0))
        return lax.dynamic_update_slice(whole, partner[None], (2 * chip + 1 - core, 0, 0))

    ahead, behind = block, block
    for distance in range(1, chips // 2):
        ahead = lax.ppermute(ahead, "dp", onward)
        behind = lax.ppermute(behind, "dp", backward)
        if distance == 1:
            whole = keep(whole, block, 0)
            ahead, behind, hold = lax.optimization_barrier((ahead, behind, hold))
        whole = keep(whole, ahead, -distance)
        whole = keep(whole, behind, distance)
    first = lax.ppermute(ahead[:half_rows], "dp", onward)
    second = lax.ppermute(behind[half_rows:], "dp", backward)
    whole = keep(whole, jnp.concatenate([first, second], axis=0), chips // 2)
    return whole, hold


def adam_update(master, moment_one, moment_two, gradient, factor):
    clipped = gradient * factor
    new_one = beta_one * moment_one + (1.0 - beta_one) * clipped
    new_two = beta_two * moment_two + (1.0 - beta_two) * clipped * clipped
    fixed_one = new_one / (1.0 - beta_one**STEP)
    fixed_two = new_two / (1.0 - beta_two**STEP)
    updated = master - learn_rate * (
        fixed_one / (jnp.sqrt(fixed_two) + adam_eps) + decay_rate * master
    )
    return (updated, new_one, new_two)


def to_all(value, axis):
    copies = lax.axis_size(axis)
    spread = jnp.broadcast_to(value[None], (copies,) + value.shape)
    return lax.all_to_all(spread, axis, split_axis=0, concat_axis=0, tiled=True)


def norm_parts(values):
    center = jnp.mean(values, axis=-1, keepdims=True)
    offsets = values - center
    spread = jnp.mean(offsets * offsets, axis=-1, keepdims=True)
    scale = lax.rsqrt(spread + norm_eps)
    return offsets * scale, scale


def norm_back(grad, centered, scale, gain):
    inner = grad * gain
    mean_one = jnp.mean(inner, axis=-1, keepdims=True)
    mean_two = jnp.mean(inner * centered, axis=-1, keepdims=True)
    d_values = scale * (inner - mean_one - centered * mean_two)
    d_gain = jnp.sum(grad * centered, axis=0, keepdims=True)
    return d_values, d_gain, jnp.sum(grad, axis=0, keepdims=True)


def gelu_back(values):
    inner = gelu_scale * (values + gelu_cube * values * values * values)
    bend = jnp.tanh(inner)
    slope = gelu_scale * (1.0 + 3.0 * gelu_cube * values * values)
    return 0.5 * (1.0 + bend) + 0.5 * values * (1.0 - bend * bend) * slope


def spread_heads(rows, width):
    size = width // H
    head_of = lax.broadcasted_iota(jnp.int32, rows.shape, 1) // size
    nothing = jnp.zeros_like(rows)
    return jnp.concatenate([jnp.where(head_of == h, rows, nothing) for h in range(H)], axis=0)


def join_heads(spread, count, width):
    size = width // H
    head_of = lax.broadcasted_iota(jnp.int32, (count, width), 1) // size
    total = jnp.zeros((count, width), wide)
    for h in range(H):
        total = total + jnp.where(head_of == h, spread[h * count : (h + 1) * count], 0.0)
    return total


def one_hot(column, count):
    spots = lax.broadcasted_iota(jnp.int32, (column.shape[0], count), 1)
    return jnp.where(column == spots, 1.0, 0.0).astype(low)


def weight(w_ref, j):
    devices, _, width = w_ref.shape
    rows = width // devices
    return w_ref[:, j * rows : (j + 1) * rows, :].reshape(width, width)


def weight_copies(w_hbm, w_ref, sems):
    rows = w_ref.shape[2] // w_ref.shape[0]
    cuts = (0, 3, 4, 8, 12)
    copies = []
    for k in range(4):
        span = pl.ds(cuts[k] * rows, (cuts[k + 1] - cuts[k]) * rows)
        copies.append(
            pltpu.make_async_copy(w_hbm.at[:, span, :], w_ref.at[:, span, :], sems.at[k])
        )
    for copy in copies:
        copy.start()
    return copies


def weight_tail(w_ref):
    devices, _, width = w_ref.shape
    rows = width // devices
    folds = w_ref.shape[1] // rows - 8
    return w_ref[:, 8 * rows : (8 + folds) * rows, :].reshape(folds * width, width)


def forward_kernel(
    cols_ref,
    docs_ref,
    picks_ref,
    back_ref,
    pos_ref,
    vec_ref,
    w_hbm,
    final_ref,
    x_ref,
    kv_ref,
    q_ref,
    probs_ref,
    attn_ref,
    mid_ref,
    pre_ref,
    top_ref,
    w_ref,
    sems,
):
    copies = weight_copies(w_hbm, w_ref, sems)
    batches, length, width = x_ref.shape
    picks = picks_ref.shape[1]
    devices, held, _ = back_ref.shape
    capacity = held // batches
    slot_count = devices * capacity
    scaling = (width // H) ** (-0.5)
    vec = vec_ref[...]

    def row(k):
        return vec[k : k + 1]

    for m in range(batches):
        sources = back_ref[:, m * capacity : (m + 1) * capacity, :].reshape(slot_count, width)
        pos = pos_ref[...]
        pick = one_hot(cols_ref[m, :, 0:1], slot_count)
        pick_pos = one_hot(cols_ref[m, :, 1:2], LONGEST)
        chosen = picks_ref[m, :, 0:1]
        select = one_hot(chosen, length)
        x_embed = dot_plain(pick, sources) + dot_plain(pick_pos, pos)
        x_ref[m] = x_embed
        pick_c = dot_plain(select, pick).astype(low)
        pick_pos_c = dot_plain(select, pick_pos).astype(low)
        x_chosen = dot_plain(pick_c, sources) + dot_plain(pick_pos_c, pos)
        normed = (norm_parts(x_embed)[0] * row(0) + row(1)).astype(low)
        normed_c = dot_plain(select, normed).astype(low)
        if m == 0:
            copies[0].wait()
        kv_ref[m, :, :width] = dot_plain(normed, weight(w_ref, 1)).astype(low)
        kv_ref[m, :, width:] = (dot_plain(normed, weight(w_ref, 2)) + row(7)).astype(low)
        queries = (dot_plain(normed_c, weight(w_ref, 0)) + row(6)).astype(low)
        q_ref[m * picks : (m + 1) * picks] = queries
        scores = dot_last(spread_heads(queries, width), kv_ref[m, :, :width]) * scaling
        spots = lax.broadcasted_iota(jnp.int32, (picks, length), 1)
        allowed = (picks_ref[m, :, 1:2] == docs_ref[m]) & (spots <= chosen)
        penalty = jnp.where(allowed, 0.0, 1.0)
        blocked = jnp.concatenate([penalty] * H, axis=0) > 0.5
        scores = jnp.where(blocked, neg_big, scores)
        row_max = jnp.max(scores, axis=-1, keepdims=True)
        weights_exp = jnp.exp(scores - row_max)
        probs = weights_exp / jnp.sum(weights_exp, axis=-1, keepdims=True)
        probs_ref[m] = probs
        spread = dot_plain(probs.astype(low), kv_ref[m, :, width:])
        attn_ref[m * picks : (m + 1) * picks] = join_heads(spread, picks, width).astype(low)
        mid_ref[m * picks : (m + 1) * picks] = x_chosen
    copies[1].wait()
    x_mid = mid_ref[...] + dot_plain(attn_ref[...], weight(w_ref, 3)) + row(8)
    mid_ref[...] = x_mid
    normed_two = (norm_parts(x_mid)[0] * row(2) + row(3)).astype(low)
    copies[2].wait()
    for j in range(4):
        span = slice(j * width, (j + 1) * width)
        pre_ref[:, span] = dot_plain(normed_two, weight(w_ref, 4 + j)) + row(10 + j)
    activated = gelu_tanh(pre_ref[...]).astype(low)
    copies[3].wait()
    x_top = x_mid + dot_plain(activated, weight_tail(w_ref)) + row(9)
    top_ref[...] = x_top
    final_ref[...] = (norm_parts(x_top)[0] * row(4) + row(5)).astype(low)


def run_forward(cols, docs, picked, back, pos, vec, whole):
    batches, length = cols.shape[:2]
    picks = picked.shape[1]
    width = vec.shape[1]
    devices = whole.shape[0]
    weight_rows = 12 * (width // devices)
    vmem = pl.BlockSpec(memory_space=pltpu.VMEM)
    count = batches * picks

    def shape(dims, kind):
        return jax.ShapeDtypeStruct(dims, kind)

    return pl.pallas_call(
        forward_kernel,
        out_shape=(
            shape((count, width), low),
            shape((batches, length, width), wide),
            shape((batches, length, 2 * width), low),
            shape((count, width), low),
            shape((batches, H * picks, length), wide),
            shape((count, width), low),
            shape((count, width), wide),
            shape((count, 4 * width), wide),
            shape((count, width), wide),
        ),
        in_specs=[vmem] * 6 + [pl.BlockSpec(memory_space=pl.ANY)],
        out_specs=(vmem,) * 9,
        scratch_shapes=[
            pltpu.VMEM((devices, weight_rows, width), low),
            pltpu.SemaphoreType.DMA((4,)),
        ],
        compiler_params=pltpu.CompilerParams(vmem_limit_bytes=VMEM_BYTES),
        name="layer_forward",
    )(cols, docs, picked, back, pos, vec, whole)


def backward_kernel(
    d_final_ref,
    cols_ref,
    picks_ref,
    vec_ref,
    x_ref,
    kv_ref,
    q_ref,
    probs_ref,
    attn_ref,
    mid_ref,
    pre_ref,
    top_ref,
    w_hbm,
    d_embed_ref,
    g_attn_ref,
    g_vec_ref,
    g_pos_ref,
    lefts_ref,
    rights_ref,
    w_ref,
    sems,
):
    copies = weight_copies(w_hbm, w_ref, sems)
    batches, length, width = x_ref.shape
    picks = picks_ref.shape[1]
    hidden = 4 * width
    scaling = (width // H) ** (-0.5)
    vec = vec_ref[...]

    def row(k):
        return vec[k : k + 1]

    def column_sum(values):
        return jnp.sum(values.astype(wide), axis=0, keepdims=True)

    centered, scale = norm_parts(top_ref[...])
    d_top, d_gain, d_shift = norm_back(d_final_ref[...], centered, scale, row(4))
    g_vec_ref[4:5] = d_gain
    g_vec_ref[5:6] = d_shift
    d_branch = d_top.astype(low)
    rights_ref[:, :width] = d_branch
    g_vec_ref[9:10] = column_sum(d_branch)
    pre = pre_ref[...]
    lefts_ref[:, :hidden] = gelu_tanh(pre).astype(low)
    copies[3].wait()
    d_pre = (dot_last(d_branch, weight_tail(w_ref)) * gelu_back(pre)).astype(low)
    rights_ref[:, width : width + hidden] = d_pre
    copies[2].wait()
    d_normed = jnp.zeros(d_top.shape, wide)
    for j in range(4):
        piece = d_pre[:, j * width : (j + 1) * width]
        g_vec_ref[10 + j : 11 + j] = column_sum(piece)
        d_normed = d_normed + dot_last(piece, weight(w_ref, 4 + j))
    centered, scale = norm_parts(mid_ref[...])
    lefts_ref[:, hidden : hidden + width] = (centered * row(2) + row(3)).astype(low)
    d_mid, d_gain, d_shift = norm_back(d_normed, centered, scale, row(2))
    g_vec_ref[2:3] = d_gain
    g_vec_ref[3:4] = d_shift
    d_mid = d_top + d_mid
    d_attn_branch = d_mid.astype(low)
    rights_ref[:, width + hidden :] = d_attn_branch
    lefts_ref[:, hidden + width :] = attn_ref[...]
    g_vec_ref[8:9] = column_sum(d_attn_branch)
    copies[1].wait()
    d_attended = dot_last(d_attn_branch, weight(w_ref, 3)).astype(low)
    copies[0].wait()
    for m in range(batches):
        mine = slice(m * picks, (m + 1) * picks)
        keys_all = kv_ref[m, :, :width]
        values = kv_ref[m, :, width:]
        probs = probs_ref[m]
        d_spread = spread_heads(d_attended[mine], width)
        d_probs = dot_last(d_spread, values)
        row_inner = jnp.sum(probs * d_probs, axis=-1, keepdims=True)
        d_scores = (probs * (d_probs - row_inner)).astype(low)
        q_spread = spread_heads(q_ref[mine], width)
        d_query = (join_heads(dot_plain(d_scores, keys_all), picks, width) * scaling).astype(low)
        select = one_hot(picks_ref[m, :, 0:1], length)
        d_query = dot_first(select, d_query).astype(low)
        d_key = (dot_first(d_scores, q_spread) * scaling).astype(low)
        d_value = dot_first(probs.astype(low), d_spread).astype(low)
        centered, scale = norm_parts(x_ref[m])
        normed = (centered * row(0) + row(1)).astype(low)
        d_normed = jnp.zeros((length, width), wide)
        for j, piece in enumerate((d_query, d_key, d_value)):
            span = slice(j * width, (j + 1) * width)
            product = dot_first(normed, piece)
            if m == 0:
                g_attn_ref[:, span] = product
            else:
                g_attn_ref[:, span] += product
            d_normed = d_normed + dot_last(piece, weight(w_ref, j))
        d_embed, d_gain, d_shift = norm_back(d_normed, centered, scale, row(0))
        d_embed = d_embed + lax.dot_general(
            jnp.where(
                picks_ref[m, :, 0:1]
                == lax.broadcasted_iota(jnp.int32, (picks, length), 1),
                1.0,
                0.0,
            ),
            d_mid[mine],
            (((0,), (0,)), ((), ())),
            precision=lax.Precision.HIGHEST,
            preferred_element_type=wide,
        )
        d_embed = d_embed.astype(low)
        d_embed_ref[m] = d_embed
        sums = (d_gain, d_shift, column_sum(d_query), column_sum(d_value))
        g_pos = dot_first(one_hot(cols_ref[m, :, 1:2], LONGEST), d_embed)
        for k, value in zip((0, 1, 6, 7), sums):
            if m == 0:
                g_vec_ref[k : k + 1] = value
            else:
                g_vec_ref[k : k + 1] += value
        if m == 0:
            g_pos_ref[...] = g_pos
        else:
            g_pos_ref[...] += g_pos
    g_vec_ref[14:16] = jnp.zeros((2, width), wide)


def run_backward(d_final, cols, picked, vec, kept, whole):
    batches, length = cols.shape[:2]
    picks = picked.shape[1]
    width = vec.shape[1]
    devices = whole.shape[0]
    weight_rows = 12 * (width // devices)
    vmem = pl.BlockSpec(memory_space=pltpu.VMEM)
    count = batches * picks

    def shape(dims, kind):
        return jax.ShapeDtypeStruct(dims, kind)

    return pl.pallas_call(
        backward_kernel,
        out_shape=(
            shape((batches, length, width), low),
            shape((width, 3 * width), wide),
            shape((16, width), wide),
            shape((LONGEST, width), wide),
            shape((count, 6 * width), low),
            shape((count, 6 * width), low),
        ),
        in_specs=[vmem] * 12 + [pl.BlockSpec(memory_space=pl.ANY)],
        out_specs=(vmem,) * 6,
        scratch_shapes=[
            pltpu.VMEM((devices, weight_rows, width), low),
            pltpu.SemaphoreType.DMA((4,)),
        ],
        compiler_params=pltpu.CompilerParams(vmem_limit_bytes=VMEM_BYTES),
        name="layer_backward",
    )(d_final, cols, picked, vec, *kept, whole)


def pack_kernel(
    student_ref, attn_in, attn_out, mlp_in, mlp_out, pos, vecs, t_attn_in, t_attn_out, t_mlp_in, t_mlp_out, t_pos, t_vecs, out_ref
):
    is_student = student_ref[0] == 1
    rows, width = attn_out.shape

    def write(refs):
        ins, out, up, down, spots, small = refs
        for j in range(3):
            out_ref[j * rows : (j + 1) * rows] = ins[:, j * width : (j + 1) * width].astype(low)
        out_ref[3 * rows : 4 * rows] = out[...].astype(low)
        for j in range(4):
            out_ref[(4 + j) * rows : (5 + j) * rows] = up[
                :, j * width : (j + 1) * width
            ].astype(low)
        out_ref[8 * rows : 12 * rows] = down[...].astype(low)
        end = 12 * rows + spots.shape[0]
        out_ref[12 * rows : end] = spots[...].astype(low)
        out_ref[end : end + 16] = small[...].astype(low)

    @pl.when(is_student)
    def _():
        write((attn_in, attn_out, mlp_in, mlp_out, pos, vecs))

    @pl.when(jnp.logical_not(is_student))
    def _():
        write((t_attn_in, t_attn_out, t_mlp_in, t_mlp_out, t_pos, t_vecs))


def pack_plain(attn_in, attn_out, mlp_in, mlp_out, pos, vecs):
    width = attn_out.shape[1]
    ins = [attn_in[:, j * width : (j + 1) * width] for j in range(3)]
    up = [mlp_in[:, j * width : (j + 1) * width] for j in range(4)]
    parts = [*ins, attn_out, *up, mlp_out, pos, vecs]
    return jnp.concatenate([p.astype(low) for p in parts], axis=0)


def pack(is_student, student, teacher):
    rows, width = student[1].shape

    def padded(parts):
        vecs = parts[5]
        fill = ((0, 16 - vecs.shape[0]), (0, width - vecs.shape[1]))
        return [*parts[:5], jnp.pad(vecs, fill)]

    student, teacher = padded(student), padded(teacher)
    if rows % 16 or student[4].shape[0] % 16:
        return jnp.where(is_student, pack_plain(*student), pack_plain(*teacher))
    total = 12 * rows + student[4].shape[0] + 16
    vmem = pl.BlockSpec(memory_space=pltpu.VMEM)
    return pl.pallas_call(
        pack_kernel,
        out_shape=jax.ShapeDtypeStruct((total, width), low),
        in_specs=[pl.BlockSpec(memory_space=pltpu.SMEM)] + [vmem] * 12,
        out_specs=vmem,
        compiler_params=pltpu.CompilerParams(vmem_limit_bytes=VMEM_BYTES),
        name="pack_weights",
    )(is_student.astype(jnp.int32).reshape(1), *student, *teacher)


def unpack(whole, pos_rows, vec_width):
    devices, _, width = whole.shape
    rows = width // devices
    base = 12 * rows
    owners = LONGEST // pos_rows
    pos = whole[:owners, base : base + pos_rows].reshape(LONGEST, width)
    small = whole[:, base + pos_rows : base + pos_rows + 16, :vec_width]
    vec = small.transpose(1, 0, 2).reshape(16, width).astype(wide)
    if rows % 16:
        blocks = whole[:, : 8 * rows].reshape(devices, 8, rows, width).transpose(1, 0, 2, 3)
        tail = whole[:, 8 * rows : base].reshape(1, 4 * width, width)
        whole = jnp.concatenate([blocks.reshape(1, 8 * width, width), tail], axis=1)
    return whole, pos, vec


def place_kernel(student_ref, slots_ref, mine_ref, theirs_ref, out_ref):
    batches, _, length = slots_ref.shape
    devices, held, width = out_ref.shape
    capacity = held // batches
    for m in range(batches):
        spots = lax.broadcasted_iota(jnp.int32, (devices * capacity, length), 0)
        pick = jnp.where(spots == slots_ref[m], 1.0, 0.0).astype(low)
        rows = jnp.where(student_ref[0] == 1, mine_ref[m], theirs_ref[m])
        placed = dot_plain(pick, rows).astype(low)
        out_ref[:, m * capacity : (m + 1) * capacity, :] = placed.reshape(devices, capacity, width)


def run_place(is_student, slots, mine, theirs, devices, capacity):
    batches, _, width = mine.shape
    vmem = pl.BlockSpec(memory_space=pltpu.VMEM)
    return pl.pallas_call(
        place_kernel,
        out_shape=jax.ShapeDtypeStruct((devices, batches * capacity, width), low),
        in_specs=[pl.BlockSpec(memory_space=pltpu.SMEM)] + [vmem] * 3,
        out_specs=vmem,
        compiler_params=pltpu.CompilerParams(vmem_limit_bytes=VMEM_BYTES),
        name="place_rows",
    )(is_student.astype(jnp.int32).reshape(1), slots, mine, theirs)


def table_kernel(limit, d_low_ref, rows_ref, asked_ref, arrived_ref, out_ref, square_ref):
    step = pl.program_id(0)
    block, width = out_ref.shape
    ids = step * block + lax.broadcasted_iota(jnp.int32, (block, 1), 0)
    wanted = jnp.where(ids == asked_ref[...], 1.0, 0.0).astype(low)
    gradient = dot_plain(wanted, arrived_ref[...]) + dot_plain(d_low_ref[...], rows_ref[...])
    out_ref[...] = gradient
    inside = jnp.where(ids < limit, gradient, 0.0)
    squares = jnp.sum((inside * inside).reshape(block // 8, 8, width), axis=0)

    @pl.when(step == 0)
    def _():
        square_ref[...] = squares

    @pl.when(step > 0)
    def _():
        square_ref[...] += squares


def run_table(d_low, rows, asked, arrived, vocab_rows):
    width = rows.shape[1]
    block = -(-vocab_rows // 96) * 16
    steps = -(-vocab_rows // block)
    count = asked.shape[1]

    def fixed(dims):
        return pl.BlockSpec(dims, lambda k: (0, 0))

    return pl.pallas_call(
        functools.partial(table_kernel, vocab_rows),
        grid=(steps,),
        out_shape=(
            jax.ShapeDtypeStruct((vocab_rows, width), wide),
            jax.ShapeDtypeStruct((8, width), wide),
        ),
        in_specs=[
            pl.BlockSpec((block, rows.shape[0]), lambda k: (k, 0)),
            fixed(rows.shape),
            fixed((1, count)),
            fixed((count, width)),
        ],
        out_specs=(pl.BlockSpec((block, width), lambda k: (k, 0)), fixed((8, width))),
        compiler_params=pltpu.CompilerParams(vmem_limit_bytes=VMEM_BYTES),
        name="table_gradient",
    )(d_low, rows, asked, arrived)


def adam_kernel(count, factor_ref, *refs):
    ins, outs = refs[: 4 * count], refs[4 * count :]
    for k in range(count):
        master, one, two, gradient = [ref[...] for ref in ins[4 * k : 4 * k + 4]]
        results = adam_update(master, one, two, gradient, factor_ref[0])
        for ref, value in zip(outs[3 * k : 3 * k + 3], results):
            ref[...] = value


def run_adam(factor, groups):
    flat = [value for group in groups for value in group]
    vmem = pl.BlockSpec(memory_space=pltpu.VMEM)
    outs = [jax.ShapeDtypeStruct(g[0].shape, wide) for g in groups for _ in range(3)]
    return pl.pallas_call(
        functools.partial(adam_kernel, len(groups)),
        out_shape=tuple(outs),
        in_specs=[pl.BlockSpec(memory_space=pltpu.SMEM)] + [vmem] * len(flat),
        out_specs=(vmem,) * len(outs),
        compiler_params=pltpu.CompilerParams(vmem_limit_bytes=VMEM_BYTES),
        name="small_updates",
    )(factor.reshape(1), *flat)


def shards(
    token_shard,
    token_row,
    doc_ids,
    loss_rows,
    teacher_table,
    teacher_pos,
    teacher_attn_in,
    teacher_attn_out,
    teacher_mlp_in,
    teacher_mlp_out,
    teacher_vecs,
    table,
    pos_table,
    attn_in,
    attn_out,
    mlp_in,
    mlp_out,
    vectors,
    table_m,
    pos_m,
    attn_in_m,
    attn_out_m,
    mlp_in_m,
    mlp_out_m,
    vectors_m,
    table_v,
    pos_v,
    attn_in_v,
    attn_out_v,
    mlp_in_v,
    mlp_out_v,
    vectors_v,
):
    part = lax.axis_index("pair")
    is_student = part == 1
    me = lax.axis_index("dp")
    devices = lax.axis_size("dp")
    vocab_rows, width = table.shape
    hidden = mlp_in.shape[1]
    rows = attn_in.shape[0]
    fold_rows = mlp_out.shape[0]
    vec_count, vec_width = vectors.shape
    pos_count = pos_table.shape[0]
    swap = [(0, 1), (1, 0)]
    to_teacher = [(1, 0)]
    to_student = [(0, 1)]

    owners = token_shard[:, 0, :, 0]
    shard_rows = token_row[:, 0]
    docs = doc_ids[:, 0]
    chosen = loss_rows[:, 0]
    length = owners.shape[1]
    picks = chosen.shape[1]
    capacity = 2 * length // devices
    slot_count = devices * capacity
    total_rows = MB * devices * picks
    indices = jnp.arange(length, dtype=jnp.int32)
    before = indices[None, :] < indices[:, None]
    same_owner = owners[:, :, None] == owners[:, None, :]
    slot = owners * capacity + jnp.sum(same_owner & before, axis=-1, dtype=jnp.int32)
    slots = jnp.arange(slot_count, dtype=jnp.int32)
    filled = slots[None, :, None] == slot[:, None, :]
    request = vocab_rows + jnp.sum(
        jnp.where(filled, shard_rows[:, None, :] - vocab_rows, 0), axis=-1
    )
    request = request.reshape(MB, devices, capacity).transpose(1, 0, 2).reshape(devices, -1)
    is_next = indices[None, None, :] == (chosen + 1)[:, :, None]
    next_ids = jnp.sum(
        jnp.where(is_next, (owners * vocab_rows + shard_rows)[:, None, :], 0), axis=-1
    )
    notes = jnp.broadcast_to(next_ids.reshape(1, -1), (devices, MB * picks))
    notes = jnp.concatenate([request, notes], axis=1)
    arrived_notes = lax.all_to_all(notes, "dp", split_axis=0, concat_axis=0, tiled=True)
    asked = arrived_notes[:, : MB * capacity]
    targets = arrived_notes[:, MB * capacity :].reshape(devices, MB, picks).transpose(1, 0, 2)
    targets = targets.reshape(MB, devices * picks)[part]

    _, flag = lax.optimization_barrier((notes, is_student))
    own_block = pack(
        flag,
        (attn_in, attn_out, mlp_in, mlp_out, pos_table, vectors),
        (
            teacher_attn_in,
            teacher_attn_out,
            teacher_mlp_in,
            teacher_mlp_out,
            teacher_pos,
            teacher_vecs,
        ),
    )
    safe = jnp.minimum(asked, vocab_rows - 1)
    found = lax.cond(
        is_student,
        lambda at: jnp.take(table, at, axis=0).astype(low),
        lambda at: jnp.take(teacher_table, at, axis=0),
        safe,
    )
    whole, found = ring_gather(own_block, found)
    back = lax.all_to_all(found, "dp", split_axis=0, concat_axis=0, tiled=True)
    whole, w_pos, vec = unpack(whole, pos_count, vec_width)

    positions = indices - jnp.sum(docs[:, None, :] < docs[:, :, None], axis=-1, dtype=jnp.int32)
    is_chosen = chosen[:, :, None] == indices[None, None, :]
    doc_c = jnp.sum(jnp.where(is_chosen, docs[:, None, :], 0), axis=-1)
    cols = jnp.stack([slot, positions], axis=-1)
    picked = jnp.stack([chosen, doc_c], axis=-1)
    final, *kept = run_forward(cols, docs[:, None, :], picked, back, w_pos, vec, whole)
    final = final.reshape(MB, picks, width)

    other_final = lax.ppermute(final[1 - part], "pair", swap)
    own_final = final[part]
    both = jnp.stack(
        [
            jnp.where(is_student, other_final, own_final),
            jnp.where(is_student, own_final, other_final),
        ]
    )
    every = lax.all_gather(both.reshape(2 * picks, width), "dp", axis=0)
    every = every.reshape(devices, 2, picks, width).transpose(1, 0, 2, 3)
    every = every.reshape(2, devices * picks, width)
    teacher_rows, student_rows = every[0], every[1]
    table_low = table.astype(low)
    teacher_logits = dot_last(teacher_rows, teacher_table)
    logits = dot_last(student_rows, table_low)
    teacher_max = jnp.max(teacher_logits, axis=1)
    teacher_sum = jnp.sum(jnp.exp(teacher_logits - teacher_max[:, None]), axis=1)
    own_max = jnp.max(logits, axis=1)
    own_sum = jnp.sum(jnp.exp(logits - own_max[:, None]), axis=1)
    stats = to_all(jnp.stack([teacher_max, teacher_sum, own_max, own_sum]), "dp")

    def log_total(maxima, sums):
        big = jnp.max(maxima, axis=0)
        return big + jnp.log(jnp.sum(sums * jnp.exp(maxima - big[None]), axis=0))

    teacher_total = log_total(stats[:, 0], stats[:, 1])[:, None]
    own_total = log_total(stats[:, 2], stats[:, 3])[:, None]
    teacher_log = teacher_logits - teacher_total
    teacher_prob = jnp.exp(teacher_log)
    own_log = logits - own_total
    own_prob = jnp.exp(own_log)
    kl_local = jnp.sum(teacher_prob * (teacher_log - own_log))
    vocab_iota = jnp.arange(vocab_rows, dtype=jnp.int32)
    target_hit = (targets - me * vocab_rows)[:, None] == vocab_iota[None, :]
    d_logits = (2.0 * own_prob - target_hit.astype(wide) - teacher_prob) * (1.0 / total_rows)
    d_low = d_logits.astype(low)
    d_final_parts = dot_plain(d_low, table_low).astype(low).reshape(devices, picks, width)
    d_final_parts = lax.all_to_all(d_final_parts, "dp", split_axis=0, concat_axis=0, tiled=True)
    d_final = jnp.sum(d_final_parts.astype(wide), axis=0)
    d_final_first = lax.ppermute(d_final, "pair", to_student)
    d_final = jnp.concatenate([d_final_first, d_final], axis=0)

    d_embed, g_attn_in, g_vecs, g_pos, lefts, rights = run_backward(
        d_final, cols, picked, vec, kept, whole
    )
    d_embed_there = lax.ppermute(d_embed, "pair", to_teacher)
    out_rows = run_place(is_student, slot[:, None, :], d_embed, d_embed_there, devices, capacity)
    arrived = lax.all_to_all(out_rows, "dp", split_axis=0, concat_axis=0, tiled=True)
    arrived = arrived.reshape(devices * MB * capacity, width)

    g_vecs = jnp.pad(g_vecs.T, ((0, 0), (0, LANES - g_vecs.shape[0])))
    pos_share = LONGEST // devices
    shared = jnp.concatenate([g_attn_in, g_vecs, g_pos.reshape(width, -1)], axis=1).astype(low)
    shared = lax.psum_scatter(shared, "dp", scatter_dimension=0, tiled=True)
    _, d_low_sent, rows_sent, lefts, rights = lax.optimization_barrier(
        (d_embed_there, d_low, student_rows, lefts, rights)
    )
    d_low_other = lax.ppermute(d_low_sent, "pair", swap)
    student_rows_other = lax.ppermute(rows_sent, "pair", swap)

    def column_blocks(values):
        return values.reshape(values.shape[0], devices, -1).transpose(1, 0, 2)

    cuts = (0, hidden, hidden + width, hidden + 2 * width)
    lefts = jnp.concatenate(
        [column_blocks(lefts[:, a:b]) for a, b in zip(cuts, cuts[1:])], axis=2
    )
    lefts = lax.ppermute(lefts, "pair", to_teacher) + jnp.where(is_student, lefts, 0)
    rights = lax.ppermute(rights, "pair", to_teacher) + jnp.where(is_student, rights, 0)
    lefts = lax.all_to_all(lefts, "dp", split_axis=0, concat_axis=0, tiled=True)
    lefts = lefts.reshape(-1, lefts.shape[2])
    rights = lax.all_gather(rights, "dp", axis=0, tiled=True)
    g_mlp_out = dot_first(lefts[:, :fold_rows], rights[:, :width])
    g_mlp_in = dot_first(lefts[:, fold_rows : fold_rows + rows], rights[:, width : width + hidden])
    g_attn_out = dot_first(lefts[:, fold_rows + rows :], rights[:, width + hidden :])

    shared = lax.ppermute(shared, "pair", to_teacher) + jnp.where(is_student, shared, 0)
    shared = shared.astype(wide)
    g_attn_in = shared[:, : 3 * width]
    g_vecs = shared[:, 3 * width : 3 * width + vec_count].T
    pos_near = shared[:, 3 * width + LANES :].reshape(pos_share, width).astype(low)
    pos_near = lax.all_gather(pos_near, "dp", axis=0, tiled=True).astype(wide)
    pos_all = jnp.concatenate([pos_near, jnp.zeros((pos_count, width), wide)], axis=0)
    g_pos = lax.dynamic_slice(
        pos_all, (jnp.minimum(me * pos_count, LONGEST), 0), (pos_count, width)
    )
    smalls = (g_pos, g_attn_in, g_attn_out, g_mlp_in, g_mlp_out, g_vecs)
    squares = jnp.zeros((), wide)
    for gradient in smalls:
        squares = squares + jnp.sum(gradient * gradient)

    d_low_all = jnp.concatenate(
        [jnp.where(is_student, d_low_other, d_low), jnp.where(is_student, d_low, d_low_other)],
        axis=0,
    )
    rows_all = jnp.concatenate(
        [
            jnp.where(is_student, student_rows_other, student_rows),
            jnp.where(is_student, student_rows, student_rows_other),
        ],
        axis=0,
    )
    g_table, table_squares = run_table(
        d_low_all.T, rows_all, asked.reshape(1, -1), arrived, vocab_rows
    )
    squares = squares + jnp.sum(table_squares)
    lane = jnp.arange(LANES, dtype=jnp.int32)[None, :]
    totals = to_all(
        jnp.where(lane == 0, squares, jnp.where(lane == 1, kl_local, 0.0)), ("pair", "dp")
    )
    grad_norm = jnp.sqrt(jnp.sum(totals[devices:, 0, 0]))
    kl_mean = jnp.sum(totals[:, 0, 1]) / total_rows
    factor = jnp.minimum(1.0, clip_limit / (grad_norm + 1e-06))
    masters = (pos_table, attn_in, attn_out, mlp_in, mlp_out, vectors)
    firsts = (pos_m, attn_in_m, attn_out_m, mlp_in_m, mlp_out_m, vectors_m)
    seconds = (pos_v, attn_in_v, attn_out_v, mlp_in_v, mlp_out_v, vectors_v)
    small_out = run_adam(factor, list(zip(masters, firsts, seconds, smalls)))
    table_out = adam_update(table, table_m, table_v, g_table, factor)
    return (*table_out, *small_out, grad_norm, kl_mean)


def solution(mesh):
    return jax.shard_map(
        shards,
        mesh=mesh,
        in_specs=(
            P(None, "dp", None, None),
            P(None, "dp", None),
            P(None, "dp", None),
            P(None, "dp", None),
            P("dp", None),
            P("dp", None),
            P("dp", None),
            P("dp", None),
            P("dp", None),
            P("dp", None),
            P(None, "dp"),
            P("dp", None),
            P("dp", None),
            P("dp", None),
            P("dp", None),
            P("dp", None),
            P("dp", None),
            P(None, "dp"),
            P("dp", None),
            P("dp", None),
            P("dp", None),
            P("dp", None),
            P("dp", None),
            P("dp", None),
            P(None, "dp"),
            P("dp", None),
            P("dp", None),
            P("dp", None),
            P("dp", None),
            P("dp", None),
            P("dp", None),
            P(None, "dp"),
        ),
        out_specs=(
            P("dp", None),
            P("dp", None),
            P("dp", None),
            P("dp", None),
            P("dp", None),
            P("dp", None),
            P("dp", None),
            P("dp", None),
            P("dp", None),
            P("dp", None),
            P("dp", None),
            P("dp", None),
            P("dp", None),
            P("dp", None),
            P("dp", None),
            P("dp", None),
            P("dp", None),
            P("dp", None),
            P(None, "dp"),
            P(None, "dp"),
            P(None, "dp"),
            P(),
            P(),
        ),
        check_vma=False,
    )
```

```python
import functools

import jax
import jax.numpy as jnp
from jax import lax
from jax.experimental import pallas as pl
from jax.experimental.pallas import tpu as pltpu
from jax.sharding import PartitionSpec as P

H = 12
MB = 2
STEP = 10
LONGEST = 256
LANES = 128
MEBI = 1024 * 1024


learn_rate = 0.25
beta_one = 0.9
beta_two = 0.999
adam_eps = 1e-08
decay_rate = 0.1
clip_limit = 0.02
norm_eps = 1e-05
neg_big = -1000000000.0
gelu_scale = 0.7978845608028654
gelu_cube = 0.044715

low = jnp.bfloat16
wide = jnp.float32


def layer_norm(values, norm_gain, norm_shift):
    center = jnp.mean(values, axis=-1, keepdims=True)
    offsets = values - center
    spread = jnp.mean(offsets * offsets, axis=-1, keepdims=True)
    return offsets * lax.rsqrt(spread + norm_eps) * norm_gain + norm_shift


def gelu_tanh(values):
    return jax.nn.gelu(values, approximate=True)


def dot_plain(left_side, right_side):
    return jnp.dot(left_side, right_side, preferred_element_type=wide)


def dot_first(left_side, right_side):
    return lax.dot_general(
        left_side, right_side, (((0,), (0,)), ((), ())), preferred_element_type=wide
    )


def dot_last(left_side, right_side):
    return lax.dot_general(
        left_side, right_side, (((1,), (1,)), ((), ())), preferred_element_type=wide
    )


def tied(*values):
    return lax.optimization_barrier(values)


def kernel_cost(micros):
    return pl.CostEstimate(
        flops=int(micros * 1e8), transcendentals=0, bytes_accessed=int(micros * 3.4e6)
    )


def kernel_limit(mebi):
    return pltpu.CompilerParams(vmem_limit_bytes=mebi * MEBI)


distances = (0, -1, 1, -2, 2, -3, 3, 4)


def ring_gather(block, after, over, share):
    devices = lax.axis_size("dp")
    chips = devices // 2
    ring = [*range(0, chips, 2), *range(chips - 1, 0, -2)]
    onward = [(2 * ring[k] + c, 2 * ring[(k + 1) % chips] + c) for k in range(chips) for c in (0, 1)]
    backward = [(there, here) for here, there in onward]
    across = [(d, d ^ 1) for d in range(devices)]
    half_rows = block.shape[0] // 32 * 16
    whole = jnp.zeros((devices,) + block.shape, block.dtype)

    def keep(whole, piece, distance):
        k = 2 * distances.index(distance)
        partner = lax.ppermute(piece, "dp", across)
        whole = lax.dynamic_update_slice(whole, piece[None], (piece_slot(k, devices), 0, 0))
        return lax.dynamic_update_slice(whole, partner[None], (piece_slot(k + 1, devices), 0, 0))

    ahead, behind = block, block
    sent = [over(block[:share])]
    for distance in range(1, chips // 2):
        ahead = lax.ppermute(ahead, "dp", onward)
        behind = lax.ppermute(behind, "dp", backward)
        if distance == 1:
            ahead, behind = after(ahead, behind)
            whole = keep(whole, block, 0)
        else:
            ahead, behind, *sent = tied(ahead, behind, *sent)
        if distance < 3:
            sent += [over(ahead[:share]), over(behind[:share])]
        whole = keep(whole, ahead, -distance)
        whole = keep(whole, behind, distance)
    first = lax.ppermute(ahead[:half_rows], "dp", onward)
    second = lax.ppermute(behind[half_rows:], "dp", backward)
    last = jnp.concatenate([first, second], axis=0)
    late = jnp.stack([ahead[:share], behind[:share], last[:share]])
    return keep(whole, last, chips // 2), jnp.stack(sent), late


def piece_slot(k, count):
    if count == 1:
        return 0
    me = lax.axis_index("dp")
    chip, core = me // 2, me % 2
    chips = count // 2
    line, side = chip // 2, chip % 2
    place = jnp.where(side == 0, line, chips - 1 - line)
    spot = lax.rem(place + distances[k // 2] + chips, chips)
    there = jnp.where(spot < chips // 2, 2 * spot, 2 * (chips - 1 - spot) + 1)
    return 2 * there + (core if k % 2 == 0 else 1 - core)


def adam_update(master, moment_one, moment_two, gradient, factor):
    clipped = gradient * factor
    new_one = beta_one * moment_one + (1.0 - beta_one) * clipped
    new_two = beta_two * moment_two + (1.0 - beta_two) * clipped * clipped
    fixed_one = new_one / (1.0 - beta_one**STEP)
    fixed_two = new_two / (1.0 - beta_two**STEP)
    updated = master - learn_rate * (
        fixed_one / (jnp.sqrt(fixed_two) + adam_eps) + decay_rate * master
    )
    return (updated, new_one, new_two)


def to_all(value, axis):
    copies = lax.axis_size(axis)
    spread = jnp.broadcast_to(value[None], (copies,) + value.shape)
    return lax.all_to_all(spread, axis, split_axis=0, concat_axis=0, tiled=True)


def norm_parts(values):
    center = jnp.mean(values, axis=-1, keepdims=True)
    offsets = values - center
    spread = jnp.mean(offsets * offsets, axis=-1, keepdims=True)
    scale = lax.rsqrt(spread + norm_eps)
    return offsets * scale, scale


def norm_back(grad, centered, scale, gain):
    inner = grad * gain
    mean_one = jnp.mean(inner, axis=-1, keepdims=True)
    mean_two = jnp.mean(inner * centered, axis=-1, keepdims=True)
    d_values = scale * (inner - mean_one - centered * mean_two)
    d_gain = jnp.sum(grad * centered, axis=0, keepdims=True)
    return d_values, d_gain, jnp.sum(grad, axis=0, keepdims=True)


def gelu_back(values):
    inner = gelu_scale * (values + gelu_cube * values * values * values)
    bend = jnp.tanh(inner)
    slope = gelu_scale * (1.0 + 3.0 * gelu_cube * values * values)
    return 0.5 * (1.0 + bend) + 0.5 * values * (1.0 - bend * bend) * slope


def spread_heads(rows, width):
    size = width // H
    head_of = lax.broadcasted_iota(jnp.int32, rows.shape, 1) // size
    nothing = jnp.zeros_like(rows)
    return jnp.concatenate([jnp.where(head_of == h, rows, nothing) for h in range(H)], axis=0)


def join_heads(spread, count, width):
    size = width // H
    head_of = lax.broadcasted_iota(jnp.int32, (count, width), 1) // size
    total = jnp.zeros((count, width), wide)
    for h in range(H):
        total = total + jnp.where(head_of == h, spread[h * count : (h + 1) * count], 0.0)
    return total


def one_hot(column, count):
    spots = lax.broadcasted_iota(jnp.int32, (column.shape[0], count), 1)
    return jnp.where(column == spots, 1.0, 0.0).astype(low)


def weight(w_ref, j):
    devices, _, width = w_ref.shape
    rows = width // devices
    return w_ref[:, j * rows : (j + 1) * rows, :].reshape(width, width)


def weight_tail(w_ref, first):
    devices, _, width = w_ref.shape
    rows = width // devices
    return w_ref[:, first * rows : (first + 4) * rows, :].reshape(4 * width, width)


def position_rows(w_ref, first, owners):
    devices, _, width = w_ref.shape
    base = first * (width // devices)
    return w_ref[:owners, base : base + LONGEST // owners, :].reshape(LONGEST, width)


def weight_copies(w_hbm, w_ref, sems):
    rows = w_ref.shape[2] // w_ref.shape[0]
    cuts = (0, 3 * rows, 4 * rows, 8 * rows, w_ref.shape[1])
    copies = []
    for k in range(4):
        span = pl.ds(cuts[k], cuts[k + 1] - cuts[k])
        copies.append(
            pltpu.make_async_copy(w_hbm.at[:, span, :], w_ref.at[:, span, :], sems.at[k])
        )
    return copies


def attention_weights(queries, keys_all, picked, docs):
    width = queries.shape[1]
    picks, length = queries.shape[0], keys_all.shape[0]
    scaling = (width // H) ** (-0.5)
    scores = dot_last(spread_heads(queries, width), keys_all) * scaling
    spots = lax.broadcasted_iota(jnp.int32, (picks, length), 1)
    allowed = (picked[:, 1:2] == docs) & (spots <= picked[:, 0:1])
    penalty = jnp.where(allowed, 0.0, 1.0)
    blocked = jnp.concatenate([penalty] * H, axis=0) > 0.5
    scores = jnp.where(blocked, neg_big, scores)
    row_max = jnp.max(scores, axis=-1, keepdims=True)
    weights_exp = jnp.exp(scores - row_max)
    return weights_exp / jnp.sum(weights_exp, axis=-1, keepdims=True)


def forward_kernel(
    owners,
    cols_ref,
    docs_ref,
    picks_ref,
    back_ref,
    vec_ref,
    w_hbm,
    final_ref,
    x_ref,
    q_ref,
    mid_ref,
    pre_ref,
    top_ref,
    lefts_ref,
    w_ref,
    sems,
):
    copies = weight_copies(w_hbm, w_ref, sems)
    for k in (3, 0, 1, 2):
        copies[k].start()
    devices, held, width = back_ref.shape
    batches, length = cols_ref.shape[:2]
    picks = picks_ref.shape[1]
    capacity = held // batches
    slot_count = devices * capacity
    vec = vec_ref[...]

    def row(k):
        return vec[k : k + 1]

    mixed = []
    for m in range(batches):
        sources = back_ref[:, m * capacity : (m + 1) * capacity, :].reshape(slot_count, width)
        pick = one_hot(cols_ref[m, :, 0:1], slot_count)
        pick_pos = one_hot(cols_ref[m, :, 1:2], LONGEST)
        picked = picks_ref[m]
        select = one_hot(picked[:, 0:1], length)
        embedded = dot_plain(pick, sources)
        if m == 0:
            copies[3].wait()
        pos = position_rows(w_ref, 12, owners)
        x_embed = embedded + dot_plain(pick_pos, pos)
        x_ref[m] = x_embed
        pick_c = dot_plain(select, pick).astype(low)
        pick_pos_c = dot_plain(select, pick_pos).astype(low)
        x_chosen = dot_plain(pick_c, sources) + dot_plain(pick_pos_c, pos)
        normed = (norm_parts(x_embed)[0] * row(0) + row(1)).astype(low)
        normed_c = dot_plain(select, normed).astype(low)
        if m == 0:
            copies[0].wait()
        keys_all = dot_plain(normed, weight(w_ref, 1)).astype(low)
        values = (dot_plain(normed, weight(w_ref, 2)) + row(7)).astype(low)
        queries = (dot_plain(normed_c, weight(w_ref, 0)) + row(6)).astype(low)
        q_ref[m * picks : (m + 1) * picks] = queries
        probs = attention_weights(queries, keys_all, picked, docs_ref[m])
        spread = dot_plain(probs.astype(low), values)
        mixed.append(join_heads(spread, picks, width).astype(low))
        mid_ref[m * picks : (m + 1) * picks] = x_chosen
    mixed = jnp.concatenate(mixed, axis=0)
    copies[1].wait()
    x_mid = mid_ref[...] + dot_plain(mixed, weight(w_ref, 3)) + row(8)
    mid_ref[...] = x_mid
    normed_two = (norm_parts(x_mid)[0] * row(2) + row(3)).astype(low)
    copies[2].wait()
    for j in range(4):
        span = slice(j * width, (j + 1) * width)
        pre_ref[:, span] = dot_plain(normed_two, weight(w_ref, 4 + j)) + row(10 + j)
    activated = gelu_tanh(pre_ref[...]).astype(low)
    x_top = x_mid + dot_plain(activated, weight_tail(w_ref, 8)) + row(9)
    top_ref[...] = x_top
    final_ref[...] = (norm_parts(x_top)[0] * row(4) + row(5)).astype(low)
    share = width // devices
    for d in range(devices):
        lefts_ref[d, :, : 4 * share] = activated[:, 4 * share * d : 4 * share * (d + 1)]
        lefts_ref[d, :, 4 * share : 5 * share] = normed_two[:, share * d : share * (d + 1)]
        lefts_ref[d, :, 5 * share :] = mixed[:, share * d : share * (d + 1)]


def run_forward(cols, docs, picked, back, vec, whole, owners):
    batches, length = cols.shape[:2]
    picks = picked.shape[1]
    devices = back.shape[0]
    width = vec.shape[1]
    vmem = pl.BlockSpec(memory_space=pltpu.VMEM)
    count = batches * picks

    def shape(dims, kind):
        return jax.ShapeDtypeStruct(dims, kind)

    return pl.pallas_call(
        functools.partial(forward_kernel, owners),
        out_shape=(
            shape((count, width), low),
            shape((batches, length, width), wide),
            shape((count, width), low),
            shape((count, width), wide),
            shape((count, 4 * width), wide),
            shape((count, width), wide),
            shape((devices, count, 6 * width // devices), low),
        ),
        in_specs=[vmem] * 5 + [pl.BlockSpec(memory_space=pl.ANY)],
        out_specs=(vmem,) * 7,
        scratch_shapes=[
            pltpu.VMEM(whole.shape, low),
            pltpu.SemaphoreType.DMA((4,)),
        ],
        compiler_params=kernel_limit(44),
        cost_estimate=kernel_cost(15),
        name="layer_forward",
    )(cols, docs, picked, back, vec, whole)


def column_sum(values):
    return jnp.sum(values.astype(wide), axis=0, keepdims=True)


def upper_kernel(
    d_final_ref,
    vec_ref,
    mid_ref,
    pre_ref,
    top_ref,
    w_hbm,
    d_mid_ref,
    d_attended_ref,
    g_vec_ref,
    rights_ref,
    w_ref,
    sems,
):
    rows = w_ref.shape[2] // w_ref.shape[0]
    copies = []
    for k, (first, last) in enumerate(((8, 12), (4, 8), (3, 4))):
        count = (last - first) * rows
        copies.append(
            pltpu.make_async_copy(
                w_hbm.at[:, pl.ds(first * rows, count), :],
                w_ref.at[:, pl.ds((first - 3) * rows, count), :],
                sems.at[k],
            )
        )
        copies[k].start()
    width = mid_ref.shape[1]
    hidden = 4 * width
    vec = vec_ref[...]

    def row(k):
        return vec[k : k + 1]

    centered, scale = norm_parts(top_ref[...])
    d_top, d_gain, d_shift = norm_back(d_final_ref[...], centered, scale, row(4))
    g_vec_ref[0:4] = jnp.zeros((4, width), wide)
    g_vec_ref[4:5] = d_gain
    g_vec_ref[5:6] = d_shift
    g_vec_ref[6:8] = jnp.zeros((2, width), wide)
    g_vec_ref[14:16] = jnp.zeros((2, width), wide)
    d_branch = d_top.astype(low)
    rights_ref[:, :width] = d_branch
    g_vec_ref[9:10] = column_sum(d_branch)
    pre = pre_ref[...]
    bend = gelu_back(pre)
    centered, scale = norm_parts(mid_ref[...])
    copies[0].wait()
    d_pre = (dot_last(d_branch, weight_tail(w_ref, 5)) * bend).astype(low)
    rights_ref[:, width : width + hidden] = d_pre
    copies[1].wait()
    d_normed = jnp.zeros(d_top.shape, wide)
    for j in range(4):
        piece = d_pre[:, j * width : (j + 1) * width]
        g_vec_ref[10 + j : 11 + j] = column_sum(piece)
        d_normed = d_normed + dot_last(piece, weight(w_ref, 1 + j))
    d_mid, d_gain, d_shift = norm_back(d_normed, centered, scale, row(2))
    g_vec_ref[2:3] = d_gain
    g_vec_ref[3:4] = d_shift
    d_mid = d_top + d_mid
    d_mid_ref[...] = d_mid
    d_attn_branch = d_mid.astype(low)
    rights_ref[:, width + hidden :] = d_attn_branch
    g_vec_ref[8:9] = column_sum(d_attn_branch)
    copies[2].wait()
    d_attended_ref[...] = dot_last(d_attn_branch, weight(w_ref, 0)).astype(low)


def lower_kernel(
    count,
    flag_ref,
    d_mid_ref,
    d_attended_ref,
    g_vec_in_ref,
    cols_ref,
    docs_ref,
    picks_ref,
    vec_ref,
    x_ref,
    q_ref,
    w_hbm,
    *refs,
):
    there, near, rest = refs[:count], refs[count : 2 * count], refs[2 * count :]
    sent_ref, g_attn_ref, g_vec_ref, g_pos_ref, w_ref, sems = rest
    length, width = x_ref.shape
    devices, capacity, _ = sent_ref.shape
    slabs, share, _ = w_ref.shape

    def slab_copy(source, slab, sem):
        return pltpu.make_async_copy(source, w_ref.at[slab], sems.at[sem])

    @pl.when(flag_ref[0] == 1)
    def _():
        for k in range(slabs):
            slab_copy(w_hbm.at[k, pl.ds(0, share)], k, k).start()

    @pl.when(flag_ref[0] == 0)
    def _():
        at = 0
        for own, other in zip(there, near):
            for k in range(own.shape[0]):
                slab_copy(own.at[k], piece_slot(at, slabs), at).start()
                if slabs > 1:
                    slab_copy(other.at[k], piece_slot(at + 1, slabs), at + 1).start()
                at = at + 2

    picks = picks_ref.shape[0]
    scaling = (width // H) ** (-0.5)
    vec = vec_ref[...]

    def row(k):
        return vec[k : k + 1]

    pick_pos = one_hot(cols_ref[:, 1:2], LONGEST)
    picked = picks_ref[...]
    select = one_hot(picked[:, 0:1], length)
    queries = q_ref[...]
    d_spread = spread_heads(d_attended_ref[...], width)
    q_spread = spread_heads(queries, width)
    g_vec_ref[...] = g_vec_in_ref[...]
    centered, scale = norm_parts(x_ref[...])
    normed = (centered * row(0) + row(1)).astype(low)
    normed_c = dot_plain(select, normed).astype(low)
    for k in range(slabs):
        slab_copy(w_hbm.at[k, pl.ds(0, share)], k, k).wait()
    keys_all = dot_plain(normed, weight(w_ref, 1)).astype(low)
    values = (dot_plain(normed, weight(w_ref, 2)) + row(7)).astype(low)
    probs = attention_weights(queries, keys_all, picked, docs_ref[...])
    d_probs = dot_last(d_spread, values)
    row_inner = jnp.sum(probs * d_probs, axis=-1, keepdims=True)
    d_scores = (probs * (d_probs - row_inner)).astype(low)
    d_query = (join_heads(dot_plain(d_scores, keys_all), picks, width) * scaling).astype(low)
    g_attn_ref[:, :width] = dot_first(normed_c, d_query).astype(low)
    g_vec_ref[6:7] += column_sum(d_query)
    d_key = (dot_first(d_scores, q_spread) * scaling).astype(low)
    d_value = dot_first(probs.astype(low), d_spread).astype(low)
    g_vec_ref[7:8] += column_sum(d_value)
    d_chosen = dot_first(select, dot_last(d_query, weight(w_ref, 0)).astype(low))
    d_normed = dot_last(d_key, weight(w_ref, 1)) + dot_last(d_value, weight(w_ref, 2))
    d_normed = d_normed + d_chosen
    d_embed, d_gain, d_shift = norm_back(d_normed, centered, scale, row(0))
    g_vec_ref[0:1] += d_gain
    g_vec_ref[1:2] += d_shift
    d_embed = d_embed + lax.dot_general(
        select.astype(wide),
        d_mid_ref[...],
        (((0,), (0,)), ((), ())),
        precision=lax.Precision.HIGHEST,
        preferred_element_type=wide,
    )
    d_embed = d_embed.astype(low)
    pick = one_hot(cols_ref[:, 0:1], devices * capacity)
    sent_ref[...] = dot_first(pick, d_embed).astype(low).reshape(devices, capacity, width)
    g_attn_ref[:, width : 2 * width] = dot_first(normed, d_key).astype(low)
    g_attn_ref[:, 2 * width : 3 * width] = dot_first(normed, d_value).astype(low)
    g_pos = dot_first(pick_pos, d_embed)
    pos_share = LONGEST // devices
    if pos_share % 16:
        g_pos_ref[...] = g_pos
        return
    lane = lax.broadcasted_iota(jnp.int32, (16, LANES), 1)
    unit = jnp.where(lane == lax.broadcasted_iota(jnp.int32, (16, LANES), 0), 1.0, 0.0)
    turned_vec = lax.dot_general(
        g_vec_ref[...],
        unit,
        (((0,), (0,)), ((), ())),
        precision=lax.Precision.HIGHEST,
        preferred_element_type=wide,
    )
    g_attn_ref[:, 3 * width : 3 * width + LANES] = turned_vec.astype(low)
    g_pos = g_pos.astype(low)
    folds = width // devices // pos_share
    part = width // folds
    for d in range(devices):
        for k in range(folds):
            first = (d * folds + k) * pos_share
            g_attn_ref[first : first + pos_share, 3 * width + LANES :] = g_pos[
                d * pos_share : (d + 1) * pos_share, k * part : (k + 1) * part
            ]
    g_pos_ref[...] = jnp.zeros(g_pos_ref.shape, wide)


def run_upper(d_final, vec, kept, whole):
    count, width = d_final.shape
    slabs = whole.shape[0]
    vmem = pl.BlockSpec(memory_space=pltpu.VMEM)
    hbm = pl.BlockSpec(memory_space=pl.ANY)
    return pl.pallas_call(
        upper_kernel,
        out_shape=(
            jax.ShapeDtypeStruct((count, width), wide),
            jax.ShapeDtypeStruct((count, width), low),
            jax.ShapeDtypeStruct((16, width), wide),
            jax.ShapeDtypeStruct((count, 6 * width), low),
        ),
        in_specs=[vmem] * 5 + [hbm],
        out_specs=(vmem,) * 4,
        scratch_shapes=[
            pltpu.VMEM((slabs, 9 * width // slabs, width), low),
            pltpu.SemaphoreType.DMA((3,)),
        ],
        compiler_params=kernel_limit(44),
        cost_estimate=kernel_cost(9),
        name="upper_backward",
    )(d_final, vec, *kept, whole)


def run_lower(flag, upper, cols, docs, picked, vec, x_embed, queries, whole, there, near, devices):
    length = cols.shape[0]
    width = vec.shape[1]
    capacity = 2 * length // devices
    loose = LONGEST // devices % 16
    vmem = pl.BlockSpec(memory_space=pltpu.VMEM)
    hbm = pl.BlockSpec(memory_space=pl.ANY)

    def shape(dims, kind):
        return jax.ShapeDtypeStruct(dims, kind)

    return pl.pallas_call(
        functools.partial(lower_kernel, len(there)),
        out_shape=(
            shape((devices, capacity, width), low),
            shape((width, 3 * width + (0 if loose else LANES + LONGEST)), low),
            shape((16, width), wide),
            shape((LONGEST if loose else 8, width), wide),
        ),
        in_specs=[pl.BlockSpec(memory_space=pltpu.SMEM)] + [vmem] * 9 + [hbm] * (1 + 2 * len(there)),
        out_specs=(vmem,) * 4,
        scratch_shapes=[
            pltpu.VMEM((whole.shape[0], 3 * width // whole.shape[0], width), low),
            pltpu.SemaphoreType.DMA((whole.shape[0],)),
        ],
        compiler_params=kernel_limit(44),
        cost_estimate=kernel_cost(15),
        name="lower_backward",
    )(flag, *upper, cols, docs, picked, vec, x_embed, queries, whole, *there, *near)


def turned(column):
    count = column.shape[0]
    here = lax.broadcasted_iota(jnp.int32, (count, count), 0)
    there = lax.broadcasted_iota(jnp.int32, (count, count), 1)
    return jnp.sum(jnp.where(here == there, column, 0), axis=0, keepdims=True)


def stood(row):
    count = row.shape[1]
    here = lax.broadcasted_iota(jnp.int32, (count, count), 0)
    there = lax.broadcasted_iota(jnp.int32, (count, count), 1)
    return jnp.sum(jnp.where(here == there, row, 0), axis=1, keepdims=True)


def route_kernel(vocab_rows, shard_ref, row_ref, docs_ref, chosen_ref, notes_ref, cols_ref, picks_ref):
    batches, length, _ = cols_ref.shape
    picks = picks_ref.shape[1]
    devices = notes_ref.shape[0]
    capacity = 2 * length // devices
    slot_count = devices * capacity
    here = lax.broadcasted_iota(jnp.int32, (length, length), 0)
    there = lax.broadcasted_iota(jnp.int32, (length, length), 1)
    for m in range(batches):
        owner = shard_ref[m]
        row = stood(row_ref[m])
        docs = docs_ref[m]
        chosen = chosen_ref[m]
        earlier = jnp.where((owner == turned(owner)) & (there < here), 1, 0)
        slot = owner * capacity + jnp.sum(earlier, axis=1, keepdims=True)
        smaller = jnp.where(docs < stood(docs), 1, 0)
        spot = lax.broadcasted_iota(jnp.int32, (length, 1), 0)
        position = spot - jnp.sum(smaller, axis=1, keepdims=True)
        cols_ref[m, :, 0:1] = slot
        cols_ref[m, :, 1:2] = position
        slots = lax.broadcasted_iota(jnp.int32, (length, slot_count), 1)
        request = vocab_rows + jnp.sum(
            jnp.where(slots == slot, row - vocab_rows, 0), axis=0, keepdims=True
        )
        for d in range(devices):
            notes_ref[d : d + 1, m * capacity : (m + 1) * capacity] = request[
                :, d * capacity : (d + 1) * capacity
            ]
        is_next = lax.broadcasted_iota(jnp.int32, (length, picks), 0) == chosen + 1
        ids = jnp.sum(
            jnp.where(is_next, owner * vocab_rows + row, 0), axis=0, keepdims=True
        )
        base = batches * capacity + m * picks
        notes_ref[:, base : base + picks] = jnp.broadcast_to(ids, (devices, picks))
        chosen = stood(chosen)
        among = lax.broadcasted_iota(jnp.int32, (picks, length), 1) == chosen
        picks_ref[m, :, 0:1] = chosen
        picks_ref[m, :, 1:2] = jnp.sum(jnp.where(among, docs, 0), axis=1, keepdims=True)


def run_route(shard, row, docs, chosen, devices, vocab_rows):
    batches, length, _ = shard.shape
    picks = chosen.shape[2]
    vmem = pl.BlockSpec(memory_space=pltpu.VMEM)
    held = batches * (2 * length // devices + picks)
    return pl.pallas_call(
        functools.partial(route_kernel, vocab_rows),
        out_shape=(
            jax.ShapeDtypeStruct((devices, held), jnp.int32),
            jax.ShapeDtypeStruct((batches, length, 2), jnp.int32),
            jax.ShapeDtypeStruct((batches, picks, 2), jnp.int32),
        ),
        in_specs=[vmem] * 4,
        out_specs=(vmem,) * 3,
        compiler_params=kernel_limit(56),
        cost_estimate=kernel_cost(3),
        name="route_tokens",
    )(shard, row, docs, chosen)


def pack_kernel(
    student_ref, attn_in, attn_out, mlp_in, mlp_out, pos, vecs, t_attn_in, t_attn_out, t_mlp_in, t_mlp_out, t_pos, t_vecs, out_ref
):
    is_student = student_ref[0] == 1
    rows, width = attn_out.shape

    def write(refs):
        ins, out, up, down, spots, small = refs
        for j in range(3):
            out_ref[j * rows : (j + 1) * rows] = ins[:, j * width : (j + 1) * width].astype(low)
        out_ref[3 * rows : 4 * rows] = out[...].astype(low)
        for j in range(4):
            out_ref[(4 + j) * rows : (5 + j) * rows] = up[
                :, j * width : (j + 1) * width
            ].astype(low)
        out_ref[8 * rows : 12 * rows] = down[...].astype(low)
        end = 12 * rows + spots.shape[0]
        out_ref[12 * rows : end] = spots[...].astype(low)
        out_ref[end : end + 16] = small[...].astype(low)

    @pl.when(is_student)
    def _():
        write((attn_in, attn_out, mlp_in, mlp_out, pos, vecs))

    @pl.when(jnp.logical_not(is_student))
    def _():
        write((t_attn_in, t_attn_out, t_mlp_in, t_mlp_out, t_pos, t_vecs))


def pack_plain(attn_in, attn_out, mlp_in, mlp_out, pos, vecs):
    width = attn_out.shape[1]
    ins = [attn_in[:, j * width : (j + 1) * width] for j in range(3)]
    up = [mlp_in[:, j * width : (j + 1) * width] for j in range(4)]
    parts = [*ins, attn_out, *up, mlp_out, pos, vecs]
    return jnp.concatenate([p.astype(low) for p in parts], axis=0)


def pack(is_student, student, teacher):
    rows, width = student[1].shape

    def padded(parts):
        vecs = parts[5]
        fill = ((0, 16 - vecs.shape[0]), (0, width - vecs.shape[1]))
        return [*parts[:5], jnp.pad(vecs, fill)]

    student, teacher = padded(student), padded(teacher)
    if rows % 16 or student[4].shape[0] % 16:
        return jnp.where(is_student, pack_plain(*student), pack_plain(*teacher))
    total = 12 * rows + student[4].shape[0] + 16
    vmem = pl.BlockSpec(memory_space=pltpu.VMEM)
    return pl.pallas_call(
        pack_kernel,
        out_shape=jax.ShapeDtypeStruct((total, width), low),
        in_specs=[pl.BlockSpec(memory_space=pltpu.SMEM)] + [vmem] * 12,
        out_specs=vmem,
        compiler_params=kernel_limit(56),
        cost_estimate=kernel_cost(3),
        name="pack_weights",
    )(is_student.astype(jnp.int32).reshape(1), *student, *teacher)


def unpack(whole, pos_rows, vec_width):
    devices, _, width = whole.shape
    rows = width // devices
    base = 12 * rows
    owners = LONGEST // pos_rows
    small = whole[:, base + pos_rows : base + pos_rows + 16, :vec_width]
    vec = small.transpose(1, 0, 2).reshape(16, width).astype(wide)
    if devices != 16 or rows % 16 or pos_rows % 16:
        pos = whole[:owners, base : base + pos_rows].reshape(1, LONGEST, width)
        blocks = whole[:, : 8 * rows].reshape(devices, 8, rows, width).transpose(1, 0, 2, 3)
        tail = whole[:, 8 * rows : base].reshape(1, 4 * width, width)
        whole = jnp.concatenate([blocks.reshape(1, 8 * width, width), tail, pos], axis=1)
        owners = 1
    return whole, vec, owners


def table_part(limit, step, block, refs):
    flag_ref, own_ref, rows_ref, other_ref, rows_other_ref, asked_ref, asked_last_ref = refs[:7]
    arrived_ref, arrived_other_ref, both_ref = refs[7:]
    count = arrived_ref.shape[0]

    @pl.when((step == 0) & (flag_ref[0] == 1))
    def _():
        both_ref[:count] = arrived_other_ref[...]
        both_ref[count:] = arrived_ref[...]

    @pl.when((step == 0) & (flag_ref[0] == 0))
    def _():
        both_ref[:count] = arrived_ref[...]
        both_ref[count:] = arrived_other_ref[...]

    ids = step * block + lax.broadcasted_iota(jnp.int32, (block, 1), 0)
    wanted = jnp.where(ids == asked_ref[...], 1.0, 0.0).astype(low)
    wanted_last = jnp.where(ids == asked_last_ref[...], 1.0, 0.0).astype(low)
    is_last = flag_ref[0] == 1

    def ordered(own_ref, other_ref):
        own, other = own_ref[...], other_ref[...]
        return jnp.where(is_last, other, own), jnp.where(is_last, own, other)

    d_low_first, d_low_last = ordered(own_ref, other_ref)
    rows_first, rows_last = ordered(rows_ref, rows_other_ref)
    return ids, (
        dot_plain(d_low_first, rows_first)
        + dot_plain(d_low_last, rows_last)
        + dot_plain(wanted, both_ref[:count])
        + dot_plain(wanted_last, both_ref[count:])
    )


def table_kernel(limit, *refs):
    out_ref, square_ref, both_ref = refs[9:]
    step = pl.program_id(0)
    block = refs[1].shape[0]
    ids, gradient = table_part(limit, step, block, (*refs[:9], both_ref))
    out_ref[...] = gradient
    inside = jnp.where(ids < limit, gradient, 0.0)
    squares = jnp.sum((inside * inside).reshape(block // 8, 8, -1), axis=0)

    @pl.when(step == 0)
    def _():
        square_ref[...] = squares

    @pl.when(step > 0)
    def _():
        square_ref[...] += squares


def table_specs(parts, vocab_rows, cuts):
    block = -(-vocab_rows // (16 * cuts)) * 16
    steps = -(-vocab_rows // block)

    def fixed(dims):
        return pl.BlockSpec(dims, lambda k: (0, 0))

    tall = pl.BlockSpec((block, parts[1].shape[1]), lambda k: (k, 0))
    specs = [pl.BlockSpec(memory_space=pltpu.SMEM), tall, fixed(parts[2].shape), tall]
    specs += [fixed(part.shape) for part in parts[4:]]
    both = pltpu.VMEM((2 * parts[7].shape[0], parts[7].shape[1]), low)
    return block, steps, specs, fixed, both


def run_table(parts, vocab_rows):
    width = parts[2].shape[1]
    block, steps, specs, fixed, both = table_specs(parts, vocab_rows, 6)
    return pl.pallas_call(
        functools.partial(table_kernel, vocab_rows),
        grid=(steps,),
        out_shape=(
            jax.ShapeDtypeStruct((vocab_rows, width), wide),
            jax.ShapeDtypeStruct((8, width), wide),
        ),
        in_specs=specs,
        out_specs=(pl.BlockSpec((block, width), lambda k: (k, 0)), fixed((8, width))),
        scratch_shapes=[both],
        compiler_params=kernel_limit(58),
        cost_estimate=kernel_cost(17),
        name="table_gradient",
    )(*parts)


def adam_kernel(count, factor_ref, *refs):
    ins, outs = refs[: 4 * count], refs[4 * count :]
    for k in range(count):
        master, one, two, gradient = [ref[...] for ref in ins[4 * k : 4 * k + 4]]
        results = adam_update(master, one, two, gradient, factor_ref[0])
        for ref, value in zip(outs[3 * k : 3 * k + 3], results):
            ref[...] = value


def run_adam(factor, groups):
    flat = [value for group in groups for value in group]
    vmem = pl.BlockSpec(memory_space=pltpu.VMEM)
    outs = [jax.ShapeDtypeStruct(g[0].shape, wide) for g in groups for _ in range(3)]
    return pl.pallas_call(
        functools.partial(adam_kernel, len(groups)),
        out_shape=tuple(outs),
        in_specs=[pl.BlockSpec(memory_space=pltpu.SMEM)] + [vmem] * len(flat),
        out_specs=(vmem,) * len(outs),
        compiler_params=kernel_limit(58),
        cost_estimate=kernel_cost(6),
        name="small_updates",
    )(factor.reshape(1), *flat)


def shards(
    token_shard,
    token_row,
    doc_ids,
    loss_rows,
    teacher_table,
    teacher_pos,
    teacher_attn_in,
    teacher_attn_out,
    teacher_mlp_in,
    teacher_mlp_out,
    teacher_vecs,
    table,
    pos_table,
    attn_in,
    attn_out,
    mlp_in,
    mlp_out,
    vectors,
    table_m,
    pos_m,
    attn_in_m,
    attn_out_m,
    mlp_in_m,
    mlp_out_m,
    vectors_m,
    table_v,
    pos_v,
    attn_in_v,
    attn_out_v,
    mlp_in_v,
    mlp_out_v,
    vectors_v,
):
    part = lax.axis_index("pair")
    is_student = part == 1
    me = lax.axis_index("dp")
    devices = lax.axis_size("dp")
    vocab_rows, width = table.shape
    hidden = mlp_in.shape[1]
    rows = attn_in.shape[0]
    fold_rows = mlp_out.shape[0]
    vec_count, vec_width = vectors.shape
    pos_count = pos_table.shape[0]
    swap = [(0, 1), (1, 0)]
    to_teacher = [(1, 0)]
    to_student = [(0, 1)]

    length = token_row.shape[2]
    picks = loss_rows.shape[2]
    capacity = 2 * length // devices
    slot_count = devices * capacity
    total_rows = MB * devices * picks
    student_flag = is_student.astype(jnp.int32).reshape(1)
    docs = doc_ids
    notes, cols, picked = run_route(
        token_shard[:, 0], token_row, docs, loss_rows, devices, vocab_rows
    )
    arrived_notes = lax.all_to_all(notes, "dp", split_axis=0, concat_axis=0, tiled=True)
    arrived_notes, flag = tied(arrived_notes, is_student)
    asked = arrived_notes[:, : MB * capacity]
    targets = arrived_notes[:, MB * capacity :].reshape(devices, MB, picks).transpose(1, 0, 2)
    targets = targets.reshape(MB, devices * picks)[part]

    own_block = pack(
        flag,
        (attn_in, attn_out, mlp_in, mlp_out, pos_table, vectors),
        (
            teacher_attn_in,
            teacher_attn_out,
            teacher_mlp_in,
            teacher_mlp_out,
            teacher_pos,
            teacher_vecs,
        ),
    )
    safe = jnp.minimum(asked, vocab_rows - 1)
    found = lax.cond(
        is_student,
        lambda at: jnp.take(table, at, axis=0).astype(low),
        lambda at: jnp.take(teacher_table, at, axis=0),
        safe,
    )
    def over(value):
        return lax.ppermute(value, "pair", to_teacher)

    def after(ahead, behind):
        nonlocal found
        ahead, behind, found = tied(ahead, behind, found)
        return ahead, behind

    if devices == 16 and rows % 16 == 0 and pos_count % 16 == 0:
        whole, early, late = ring_gather(own_block, after, over, 3 * rows)
    else:
        whole, early, late = lax.all_gather(own_block, "dp", axis=0), None, None
    back = lax.all_to_all(found, "dp", split_axis=0, concat_axis=0, tiled=True)
    whole, vec, owners_pos = unpack(whole, pos_count, vec_width)
    final, x_embed, queries, mid, pre, top, lefts = run_forward(
        cols, docs, picked, back, vec, whole, owners_pos
    )
    final = final.reshape(MB, picks, width)

    def on_both(value):
        return jnp.where(is_student, value, over(value))

    def across(value):
        return lax.ppermute(value, "dp", [(d, d ^ 1) for d in range(devices)])

    core = me % 2
    other_final = lax.ppermute(final[1 - part], "pair", swap)
    own_final = final[part]
    if late is None:
        there = [over(whole[:, : 3 * width])]
    else:
        other_final, late = tied(other_final, late)
        there = [early, over(late)]
    x_over = jnp.concatenate([x_embed[0], queries[:picks].astype(wide), vec], axis=0)
    both = jnp.stack(
        [
            jnp.where(is_student, other_final, own_final),
            jnp.where(is_student, own_final, other_final),
        ]
    )
    every = lax.all_gather(both.reshape(2 * picks, width), "dp", axis=0)
    cuts = (0, 5 * length // 16, 11 * length // 16, x_over.shape[0])
    x_over = [x_over[a:b] for a, b in zip(cuts, cuts[1:])]
    other_final, x_over[0] = tied(other_final, x_over[0])
    x_over[0] = over(x_over[0])
    lefts = lax.all_to_all(lefts, "dp", split_axis=0, concat_axis=0, tiled=True)
    every, lefts, x_over[0], x_over[1] = tied(every, lefts, x_over[0], x_over[1])
    lefts = lefts.reshape(-1, lefts.shape[2])
    x_over[1] = over(x_over[1])
    every = every.reshape(devices, 2, picks, width).transpose(1, 0, 2, 3)
    every = every.reshape(2, devices * picks, width)
    teacher_rows, student_rows = every[0], every[1]
    table_low = table.astype(low)
    teacher_logits = dot_last(teacher_rows, teacher_table)
    logits = dot_last(student_rows, table_low)
    teacher_max = jnp.max(teacher_logits, axis=1)
    teacher_sum = jnp.sum(jnp.exp(teacher_logits - teacher_max[:, None]), axis=1)
    own_max = jnp.max(logits, axis=1)
    own_sum = jnp.sum(jnp.exp(logits - own_max[:, None]), axis=1)
    stats = to_all(jnp.stack([teacher_max, teacher_sum, own_max, own_sum]), "dp")

    stats, x_over[1], x_over[2], *there = tied(stats, x_over[1], x_over[2], *there)
    x_over[2] = over(x_over[2])
    near = [across(value) for value in there]

    def log_total(maxima, sums):
        big = jnp.max(maxima, axis=0)
        return big + jnp.log(jnp.sum(sums * jnp.exp(maxima - big[None]), axis=0))

    teacher_total = log_total(stats[:, 0], stats[:, 1])[:, None]
    own_total = log_total(stats[:, 2], stats[:, 3])[:, None]
    teacher_log = teacher_logits - teacher_total
    teacher_prob = jnp.exp(teacher_log)
    own_log = logits - own_total
    own_prob = jnp.exp(own_log)
    kl_local = jnp.sum(teacher_prob * (teacher_log - own_log))
    vocab_iota = jnp.arange(vocab_rows, dtype=jnp.int32)
    target_hit = (targets - me * vocab_rows)[:, None] == vocab_iota[None, :]
    d_logits = (2.0 * own_prob - target_hit.astype(wide) - teacher_prob) * (1.0 / total_rows)
    d_low = d_logits.astype(low)
    d_final_parts = dot_plain(d_low, table_low).astype(low).reshape(devices, picks, width)
    d_final_parts, x_over[2] = tied(d_final_parts, x_over[2])
    d_final_parts = lax.all_to_all(d_final_parts, "dp", split_axis=0, concat_axis=0, tiled=True)
    d_final = jnp.sum(d_final_parts.astype(wide), axis=0)
    d_final_first = lax.ppermute(d_final, "pair", to_student)
    d_final = jnp.concatenate([d_final_first, d_final], axis=0)

    d_final, rows_sent = tied(d_final, student_rows)
    rows_other = lax.ppermute(rows_sent, "pair", swap)
    d_mid, d_attended, g_vecs, rights = run_upper(d_final, vec, (mid, pre, top), whole)
    d_mid, rows_other = tied(d_mid, rows_other)
    passed = jnp.concatenate([d_mid, d_attended.astype(wide)], axis=1)
    passed = jnp.where(is_student, passed[picks:], over(passed[:picks]))
    x_last = jnp.concatenate([x_embed[1], queries[picks:].astype(wide), vec], axis=0)
    x_last = jnp.where(is_student, x_last, jnp.concatenate(x_over, axis=0))
    sent, g_attn, g_vecs, g_pos = run_lower(
        student_flag,
        (passed[:, :width], passed[:, width:].astype(low), jnp.where(is_student, g_vecs, 0.0)),
        cols[part],
        docs[part],
        picked[part],
        x_last[length + picks :],
        x_last[:length],
        x_last[length : length + picks].astype(low),
        whole,
        there,
        near,
        devices,
    )
    arrived = lax.all_to_all(sent, "dp", split_axis=0, concat_axis=0, tiled=True)
    arrived = arrived.reshape(slot_count, width)

    pos_share = LONGEST // devices
    if pos_share % 16:
        g_vecs = jnp.pad(g_vecs.T, ((0, 0), (0, LANES - g_vecs.shape[0]))).astype(low)
        parts = g_pos.reshape(devices, pos_share, -1, LONGEST).transpose(0, 2, 1, 3)
        parts = parts.reshape(width, LONGEST).astype(low)
        shared = jnp.concatenate([g_attn, g_vecs, parts], axis=1)
    else:
        shared = g_attn
    d_low_sent = d_low
    if devices % 2:
        shared = lax.psum_scatter(shared, "dp", scatter_dimension=0, tiled=True)
    else:
        chips = shared.reshape(devices // 2, 2, rows, -1)
        near_sum = across(lax.dynamic_index_in_dim(chips, 1 - core, 1, keepdims=False))
        near_sum, d_low_sent = tied(near_sum, d_low)
        mine = lax.dynamic_index_in_dim(chips, core, 1, keepdims=False)
        chips = (mine.astype(wide) + near_sum.astype(wide)).astype(low)
    d_low_other = lax.ppermute(d_low_sent, "pair", swap)

    rights = lax.all_gather(rights, "dp", axis=0, tiled=True)
    at = (0, fold_rows, fold_rows + rows, fold_rows + 2 * rows)
    ends = (0, width, width + hidden, 2 * width + hidden)
    products = [
        dot_first(lefts[:, at[k] : at[k + 1]], rights[:, ends[k] : ends[k + 1]]).astype(low)
        for k in range(3)
    ]
    squares = jnp.zeros((), wide)
    for product in products:
        squares = squares + jnp.sum(jnp.square(product.astype(wide)))
    products[1] = products[1].reshape(rows, 4, width).transpose(1, 0, 2).reshape(4 * rows, width)
    products = jnp.concatenate(products, axis=0)
    d_low_turned, d_low_other = d_low.T, d_low_other.T
    arrived, products, squares, d_low_turned, d_low_other = tied(
        arrived, products, squares, d_low_turned, d_low_other
    )
    arrived_other = lax.ppermute(arrived, "pair", swap)
    if devices % 2 == 0:
        chips, arrived = tied(chips, arrived)
        columns = [[2 * k + c for k in range(devices // 2)] for c in (0, 1)]
        chips = lax.all_to_all(
            chips, "dp", split_axis=0, concat_axis=0, axis_index_groups=columns, tiled=True
        )
    asked = asked.reshape(devices, MB, capacity).transpose(1, 0, 2).reshape(MB, 1, slot_count)
    asked_first, asked_last = asked[0], asked[1]
    own_last = is_student.astype(jnp.int32).reshape(1)
    parts = (
        own_last,
        d_low_turned,
        student_rows,
        d_low_other,
        rows_other,
        asked_first,
        asked_last,
        arrived,
        arrived_other,
    )
    if devices % 2 == 0:
        shared = jnp.sum(chips.astype(wide), axis=0).astype(low)
    pos_near = shared[:, 3 * width + LANES :]
    pos_near = pos_near.reshape(-1, pos_share, LONGEST).transpose(1, 0, 2).reshape(pos_share, width)
    pos_near = jnp.pad(pos_near, ((0, max(0, LANES // 2 - pos_share)), (0, 0)))
    pos_near = lax.all_gather(pos_near, "dp", axis=0)[:, :pos_share].reshape(LONGEST, width)
    pos_near = jnp.concatenate([pos_near, jnp.zeros((pos_count, width), low)], axis=0)
    pos_near = lax.dynamic_slice(
        pos_near, (jnp.minimum(me * pos_count, LONGEST), 0), (pos_count, width)
    )
    arrived_other, shared = tied(arrived_other, shared)
    shared_other = lax.ppermute(shared, "pair", swap)
    arrived_other, products = tied(arrived_other, products)
    products_there = over(products)
    parts = (*parts[:-1], arrived_other)
    g_table, table_squares = run_table(parts, vocab_rows)
    table_squares, products_there, shared_other = tied(
        table_squares, products_there, shared_other
    )
    shared = shared.astype(wide) + shared_other.astype(wide)
    squares = squares + jnp.sum(shared * shared) + jnp.sum(table_squares)
    lane = jnp.arange(LANES, dtype=jnp.int32)[None, :]
    totals = to_all(
        jnp.where(lane == 0, squares, jnp.where(lane == 1, kl_local, 0.0)), ("pair", "dp")
    )
    grad_norm = jnp.sqrt(jnp.sum(totals[devices:, 0, 0]))
    kl_mean = jnp.sum(totals[:, 0, 1]) / total_rows
    factor = jnp.minimum(1.0, clip_limit / (grad_norm + 1e-06))
    table_out = adam_update(table, table_m, table_v, g_table, factor)
    products = jnp.where(is_student, products, products_there).astype(wide)
    g_mlp_out, g_attn_out = products[:fold_rows], products[fold_rows + 4 * rows :]
    g_mlp_in = products[fold_rows : fold_rows + 4 * rows].reshape(4, rows, width)
    g_mlp_in = g_mlp_in.transpose(1, 0, 2).reshape(rows, hidden)
    g_pos = pos_near.astype(wide) + lax.ppermute(pos_near, "pair", swap).astype(wide)
    g_attn_in = shared[:, : 3 * width]
    g_vecs = shared[:, 3 * width : 3 * width + vec_count].T
    smalls = (g_pos, g_attn_in, g_attn_out, g_mlp_in, g_mlp_out, g_vecs)
    masters = (pos_table, attn_in, attn_out, mlp_in, mlp_out, vectors)
    firsts = (pos_m, attn_in_m, attn_out_m, mlp_in_m, mlp_out_m, vectors_m)
    seconds = (pos_v, attn_in_v, attn_out_v, mlp_in_v, mlp_out_v, vectors_v)
    small_out = run_adam(factor, list(zip(masters, firsts, seconds, smalls)))
    return (*table_out, *small_out, grad_norm, kl_mean)


def solution(mesh):
    return jax.shard_map(
        shards,
        mesh=mesh,
        in_specs=(
            P(None, "dp", None, None),
            P(None, "dp", None),
            P(None, "dp", None),
            P(None, "dp", None),
            P("dp", None),
            P("dp", None),
            P("dp", None),
            P("dp", None),
            P("dp", None),
            P("dp", None),
            P(None, "dp"),
            P("dp", None),
            P("dp", None),
            P("dp", None),
            P("dp", None),
            P("dp", None),
            P("dp", None),
            P(None, "dp"),
            P("dp", None),
            P("dp", None),
            P("dp", None),
            P("dp", None),
            P("dp", None),
            P("dp", None),
            P(None, "dp"),
            P("dp", None),
            P("dp", None),
            P("dp", None),
            P("dp", None),
            P("dp", None),
            P("dp", None),
            P(None, "dp"),
        ),
        out_specs=(
            P("dp", None),
            P("dp", None),
            P("dp", None),
            P("dp", None),
            P("dp", None),
            P("dp", None),
            P("dp", None),
            P("dp", None),
            P("dp", None),
            P("dp", None),
            P("dp", None),
            P("dp", None),
            P("dp", None),
            P("dp", None),
            P("dp", None),
            P("dp", None),
            P("dp", None),
            P("dp", None),
            P(None, "dp"),
            P(None, "dp"),
            P(None, "dp"),
            P(),
            P(),
        ),
        check_vma=False,
    )
```

```python
import functools

import jax
import jax.numpy as jnp
from jax import lax
from jax.experimental import pallas as pl
from jax.experimental.pallas import tpu as pltpu
from jax.sharding import PartitionSpec as P

H = 12
MB = 2
STEP = 10
LONGEST = 256
LANES = 128
MEBI = 1024 * 1024


learn_rate = 0.25
beta_one = 0.9
beta_two = 0.999
adam_eps = 1e-08
decay_rate = 0.1
clip_limit = 0.02
norm_eps = 1e-05
neg_big = -1000000000.0
gelu_scale = 0.7978845608028654
gelu_cube = 0.044715

low = jnp.bfloat16
wide = jnp.float32


def layer_norm(values, norm_gain, norm_shift):
    center = jnp.mean(values, axis=-1, keepdims=True)
    offsets = values - center
    spread = jnp.mean(offsets * offsets, axis=-1, keepdims=True)
    return offsets * lax.rsqrt(spread + norm_eps) * norm_gain + norm_shift


def gelu_tanh(values):
    return jax.nn.gelu(values, approximate=True)


def dot_plain(left_side, right_side):
    return jnp.dot(left_side, right_side, preferred_element_type=wide)


def dot_first(left_side, right_side):
    return lax.dot_general(
        left_side, right_side, (((0,), (0,)), ((), ())), preferred_element_type=wide
    )


def dot_last(left_side, right_side):
    return lax.dot_general(
        left_side, right_side, (((1,), (1,)), ((), ())), preferred_element_type=wide
    )


def tied(*values):
    return lax.optimization_barrier(values)


def kernel_cost(micros):
    return pl.CostEstimate(
        flops=int(micros * 1e8), transcendentals=0, bytes_accessed=int(micros * 3.4e6)
    )


def kernel_limit(mebi):
    return pltpu.CompilerParams(vmem_limit_bytes=mebi * MEBI)


distances = (0, -1, 1, -2, 2, -3, 3, 4)


def ring_gather(block, after, over, share):
    devices = lax.axis_size("dp")
    chips = devices // 2
    ring = [*range(0, chips, 2), *range(chips - 1, 0, -2)]
    onward = [(2 * ring[k] + c, 2 * ring[(k + 1) % chips] + c) for k in range(chips) for c in (0, 1)]
    backward = [(there, here) for here, there in onward]
    across = [(d, d ^ 1) for d in range(devices)]
    half_rows = block.shape[0] // 32 * 16

    def keep(whole, piece, distance):
        k = 2 * distances.index(distance)
        partner = lax.ppermute(piece, "dp", across)
        whole = lax.dynamic_update_slice(whole, piece[None], (piece_slot(k, devices), 0, 0))
        return lax.dynamic_update_slice(whole, partner[None], (piece_slot(k + 1, devices), 0, 0))

    def step(ahead, behind):
        return lax.ppermute(ahead, "dp", onward), lax.ppermute(behind, "dp", backward)

    near = after(1, *step(block, block))
    far = after(2, *step(*near))
    *far, block, near_ahead, near_behind, blank = tied(
        *far, block, *near, jnp.zeros((), block.dtype)
    )
    whole = jnp.broadcast_to(blank, (devices,) + block.shape)
    sent = [over(piece[:share]) for piece in (block, near_ahead, near_behind)]
    whole = keep(whole, block, 0)
    whole = keep(whole, near_ahead, -1)
    whole = keep(whole, near_behind, 1)
    ahead, behind = after(3, *step(*far))
    ahead, behind, *sent = tied(ahead, behind, *sent)
    sent += [over(piece[:share]) for piece in far]
    whole = keep(whole, far[0], -2)
    whole = keep(whole, far[1], 2)
    first = lax.ppermute(ahead[:half_rows], "dp", onward)
    second = lax.ppermute(behind[half_rows:], "dp", backward)
    whole = keep(whole, ahead, -3)
    whole = keep(whole, behind, 3)
    last = jnp.concatenate([first, second], axis=0)
    late = jnp.stack([ahead[:share], behind[:share], last[:share]])
    return keep(whole, last, 4), jnp.stack(sent), late


def piece_slot(k, count):
    if count == 1:
        return 0
    me = lax.axis_index("dp")
    chip, core = me // 2, me % 2
    chips = count // 2
    line, side = chip // 2, chip % 2
    place = jnp.where(side == 0, line, chips - 1 - line)
    spot = lax.rem(place + distances[k // 2] + chips, chips)
    there = jnp.where(spot < chips // 2, 2 * spot, 2 * (chips - 1 - spot) + 1)
    return 2 * there + (core if k % 2 == 0 else 1 - core)


def adam_update(master, moment_one, moment_two, gradient, factor):
    clipped = gradient * factor
    new_one = beta_one * moment_one + (1.0 - beta_one) * clipped
    new_two = beta_two * moment_two + (1.0 - beta_two) * clipped * clipped
    fixed_one = new_one / (1.0 - beta_one**STEP)
    fixed_two = new_two / (1.0 - beta_two**STEP)
    updated = master - learn_rate * (
        fixed_one / (jnp.sqrt(fixed_two) + adam_eps) + decay_rate * master
    )
    return (updated, new_one, new_two)


def to_all(value, axis):
    copies = lax.axis_size(axis)
    spread = jnp.broadcast_to(value[None], (copies,) + value.shape)
    return lax.all_to_all(spread, axis, split_axis=0, concat_axis=0, tiled=True)


def norm_parts(values):
    center = jnp.mean(values, axis=-1, keepdims=True)
    offsets = values - center
    spread = jnp.mean(offsets * offsets, axis=-1, keepdims=True)
    scale = lax.rsqrt(spread + norm_eps)
    return offsets * scale, scale


def norm_back(grad, centered, scale, gain):
    inner = grad * gain
    mean_one = jnp.mean(inner, axis=-1, keepdims=True)
    mean_two = jnp.mean(inner * centered, axis=-1, keepdims=True)
    d_values = scale * (inner - mean_one - centered * mean_two)
    d_gain = jnp.sum(grad * centered, axis=0, keepdims=True)
    return d_values, d_gain, jnp.sum(grad, axis=0, keepdims=True)


def gelu_back(values):
    inner = gelu_scale * (values + gelu_cube * values * values * values)
    bend = jnp.tanh(inner)
    slope = gelu_scale * (1.0 + 3.0 * gelu_cube * values * values)
    return 0.5 * (1.0 + bend) + 0.5 * values * (1.0 - bend * bend) * slope


def spread_heads(rows, width):
    size = width // H
    head_of = lax.broadcasted_iota(jnp.int32, rows.shape, 1) // size
    nothing = jnp.zeros_like(rows)
    return jnp.concatenate([jnp.where(head_of == h, rows, nothing) for h in range(H)], axis=0)


def join_heads(spread, count, width):
    size = width // H
    head_of = lax.broadcasted_iota(jnp.int32, (count, width), 1) // size
    total = jnp.zeros((count, width), wide)
    for h in range(H):
        total = total + jnp.where(head_of == h, spread[h * count : (h + 1) * count], 0.0)
    return total


def one_hot(column, count):
    spots = lax.broadcasted_iota(jnp.int32, (column.shape[0], count), 1)
    return jnp.where(column == spots, 1.0, 0.0).astype(low)


def weight(w_ref, j):
    devices, _, width = w_ref.shape
    rows = width // devices
    return w_ref[:, j * rows : (j + 1) * rows, :].reshape(width, width)


def weight_tail(w_ref, first):
    devices, _, width = w_ref.shape
    rows = width // devices
    return w_ref[:, first * rows : (first + 4) * rows, :].reshape(4 * width, width)


def position_rows(w_ref, first, owners):
    devices, _, width = w_ref.shape
    base = first * (width // devices)
    return w_ref[:owners, base : base + LONGEST // owners, :].reshape(LONGEST, width)


def weight_copies(w_hbm, w_ref, sems):
    rows = w_ref.shape[2] // w_ref.shape[0]
    cuts = (0, 3 * rows, 4 * rows, 8 * rows, w_ref.shape[1])
    copies = []
    for k in range(4):
        span = pl.ds(cuts[k], cuts[k + 1] - cuts[k])
        copies.append(
            pltpu.make_async_copy(w_hbm.at[:, span, :], w_ref.at[:, span, :], sems.at[k])
        )
    return copies


def attention_weights(queries, keys_all, picked, docs):
    width = queries.shape[1]
    picks, length = queries.shape[0], keys_all.shape[0]
    scaling = (width // H) ** (-0.5)
    scores = dot_last(spread_heads(queries, width), keys_all) * scaling
    spots = lax.broadcasted_iota(jnp.int32, (picks, length), 1)
    allowed = (picked[:, 1:2] == docs) & (spots <= picked[:, 0:1])
    penalty = jnp.where(allowed, 0.0, 1.0)
    blocked = jnp.concatenate([penalty] * H, axis=0) > 0.5
    scores = jnp.where(blocked, neg_big, scores)
    row_max = jnp.max(scores, axis=-1, keepdims=True)
    weights_exp = jnp.exp(scores - row_max)
    return weights_exp / jnp.sum(weights_exp, axis=-1, keepdims=True)


def forward_kernel(
    owners,
    flag_ref,
    cols_ref,
    docs_ref,
    picks_ref,
    back_ref,
    vec_ref,
    w_hbm,
    send_ref,
    own_ref,
    aims_ref,
    x_ref,
    q_ref,
    mid_ref,
    pre_ref,
    top_ref,
    lefts_ref,
    w_ref,
    sems,
):
    copies = weight_copies(w_hbm, w_ref, sems)
    for k in (3, 0, 1, 2):
        copies[k].start()
    devices, held, width = back_ref.shape
    batches, length = cols_ref.shape[:2]
    picks = picks_ref.shape[1]
    capacity = held // batches
    slot_count = devices * capacity
    vec = vec_ref[...]

    def row(k):
        return vec[k : k + 1]

    mixed = []
    for m in range(batches):
        sources = back_ref[:, m * capacity : (m + 1) * capacity, :].reshape(slot_count, width)
        pick = one_hot(cols_ref[m, :, 0:1], slot_count)
        pick_pos = one_hot(cols_ref[m, :, 1:2], LONGEST)
        picked = picks_ref[m]
        select = one_hot(picked[:, 0:1], length)
        embedded = dot_plain(pick, sources)
        if m == 0:
            copies[3].wait()
        pos = position_rows(w_ref, 12, owners)
        x_embed = embedded + dot_plain(pick_pos, pos)
        x_ref[m] = x_embed
        pick_c = dot_plain(select, pick).astype(low)
        pick_pos_c = dot_plain(select, pick_pos).astype(low)
        following = one_hot(picked[:, 0:1] + 1, length)
        aims_ref[m * picks : (m + 1) * picks] = dot_plain(
            dot_plain(following, pick).astype(low), sources
        )
        x_chosen = dot_plain(pick_c, sources) + dot_plain(pick_pos_c, pos)
        normed = (norm_parts(x_embed)[0] * row(0) + row(1)).astype(low)
        normed_c = dot_plain(select, normed).astype(low)
        if m == 0:
            copies[0].wait()
        keys_all = dot_plain(normed, weight(w_ref, 1)).astype(low)
        values = (dot_plain(normed, weight(w_ref, 2)) + row(7)).astype(low)
        queries = (dot_plain(normed_c, weight(w_ref, 0)) + row(6)).astype(low)
        q_ref[m * picks : (m + 1) * picks] = queries
        probs = attention_weights(queries, keys_all, picked, docs_ref[m])
        spread = dot_plain(probs.astype(low), values)
        mixed.append(join_heads(spread, picks, width).astype(low))
        mid_ref[m * picks : (m + 1) * picks] = x_chosen
    mixed = jnp.concatenate(mixed, axis=0)
    copies[1].wait()
    x_mid = mid_ref[...] + dot_plain(mixed, weight(w_ref, 3)) + row(8)
    mid_ref[...] = x_mid
    normed_two = (norm_parts(x_mid)[0] * row(2) + row(3)).astype(low)
    copies[2].wait()
    for j in range(4):
        span = slice(j * width, (j + 1) * width)
        pre_ref[:, span] = dot_plain(normed_two, weight(w_ref, 4 + j)) + row(10 + j)
    activated = gelu_tanh(pre_ref[...]).astype(low)
    x_top = x_mid + dot_plain(activated, weight_tail(w_ref, 8)) + row(9)
    top_ref[...] = x_top
    final = (norm_parts(x_top)[0] * row(4) + row(5)).astype(low)
    is_last = flag_ref[0] == 1
    send_ref[...] = jnp.where(is_last, final[:picks], final[picks:])
    own_ref[...] = jnp.where(is_last, final[picks:], final[:picks])
    share = width // devices
    for d in range(devices):
        lefts_ref[d, :, : 4 * share] = activated[:, 4 * share * d : 4 * share * (d + 1)]
        lefts_ref[d, :, 4 * share : 5 * share] = normed_two[:, share * d : share * (d + 1)]
        lefts_ref[d, :, 5 * share :] = mixed[:, share * d : share * (d + 1)]


def run_forward(flag, cols, docs, picked, back, vec, whole, owners):
    batches, length = cols.shape[:2]
    picks = picked.shape[1]
    devices = back.shape[0]
    width = vec.shape[1]
    vmem = pl.BlockSpec(memory_space=pltpu.VMEM)
    count = batches * picks

    def shape(dims, kind):
        return jax.ShapeDtypeStruct(dims, kind)

    return pl.pallas_call(
        functools.partial(forward_kernel, owners),
        out_shape=(
            shape((picks, width), low),
            shape((picks, width), low),
            shape((count, width), wide),
            shape((batches, length, width), wide),
            shape((count, width), low),
            shape((count, width), wide),
            shape((count, 4 * width), wide),
            shape((count, width), wide),
            shape((devices, count, 6 * width // devices), low),
        ),
        in_specs=[pl.BlockSpec(memory_space=pltpu.SMEM)] + [vmem] * 5 + [pl.BlockSpec(memory_space=pl.ANY)],
        out_specs=(vmem,) * 9,
        scratch_shapes=[
            pltpu.VMEM(whole.shape, low),
            pltpu.SemaphoreType.DMA((4,)),
        ],
        compiler_params=kernel_limit(36),
        cost_estimate=kernel_cost(15),
        name="layer_forward",
    )(flag, cols, docs, picked, back, vec, whole)


def column_sum(values):
    return jnp.sum(values.astype(wide), axis=0, keepdims=True)


def upper_kernel(
    d_final_ref,
    vec_ref,
    mid_ref,
    pre_ref,
    top_ref,
    w_hbm,
    first_ref,
    last_ref,
    g_vec_ref,
    rights_ref,
    w_ref,
    sems,
):
    rows = w_ref.shape[2] // w_ref.shape[0]
    copies = []
    for k, (first, last) in enumerate(((8, 12), (4, 8), (3, 4))):
        count = (last - first) * rows
        copies.append(
            pltpu.make_async_copy(
                w_hbm.at[:, pl.ds(first * rows, count), :],
                w_ref.at[:, pl.ds((first - 3) * rows, count), :],
                sems.at[k],
            )
        )
        copies[k].start()
    width = mid_ref.shape[1]
    hidden = 4 * width
    vec = vec_ref[...]

    def row(k):
        return vec[k : k + 1]

    centered, scale = norm_parts(top_ref[...])
    d_top, d_gain, d_shift = norm_back(d_final_ref[...], centered, scale, row(4))
    g_vec_ref[0:4] = jnp.zeros((4, width), wide)
    g_vec_ref[4:5] = d_gain
    g_vec_ref[5:6] = d_shift
    g_vec_ref[6:8] = jnp.zeros((2, width), wide)
    g_vec_ref[14:16] = jnp.zeros((2, width), wide)
    d_branch = d_top.astype(low)
    rights_ref[:, :width] = d_branch
    g_vec_ref[9:10] = column_sum(d_branch)
    pre = pre_ref[...]
    bend = gelu_back(pre)
    centered, scale = norm_parts(mid_ref[...])
    copies[0].wait()
    d_pre = (dot_last(d_branch, weight_tail(w_ref, 5)) * bend).astype(low)
    rights_ref[:, width : width + hidden] = d_pre
    copies[1].wait()
    d_normed = jnp.zeros(d_top.shape, wide)
    for j in range(4):
        piece = d_pre[:, j * width : (j + 1) * width]
        g_vec_ref[10 + j : 11 + j] = column_sum(piece)
        d_normed = d_normed + dot_last(piece, weight(w_ref, 1 + j))
    d_mid, d_gain, d_shift = norm_back(d_normed, centered, scale, row(2))
    g_vec_ref[2:3] = d_gain
    g_vec_ref[3:4] = d_shift
    d_mid = d_top + d_mid
    picks = first_ref.shape[0]
    first_ref[:, :width] = d_mid[:picks]
    last_ref[:, :width] = d_mid[picks:]
    d_attn_branch = d_mid.astype(low)
    rights_ref[:, width + hidden :] = d_attn_branch
    g_vec_ref[8:9] = column_sum(d_attn_branch)
    copies[2].wait()
    d_attended = dot_last(d_attn_branch, weight(w_ref, 0)).astype(low).astype(wide)
    first_ref[:, width:] = d_attended[:picks]
    last_ref[:, width:] = d_attended[picks:]


def lower_kernel(
    count,
    flag_ref,
    d_mid_ref,
    d_attended_ref,
    g_vec_in_ref,
    cols_ref,
    docs_ref,
    picks_ref,
    vec_ref,
    x_ref,
    q_ref,
    w_hbm,
    *refs,
):
    there, near, rest = refs[:count], refs[count : 2 * count], refs[2 * count :]
    sent_ref, g_attn_ref, g_vec_ref, g_pos_ref, w_ref, sems = rest
    length, width = x_ref.shape
    devices, capacity, _ = sent_ref.shape
    slabs, share, _ = w_ref.shape

    def slab_copy(source, slab, sem):
        return pltpu.make_async_copy(source, w_ref.at[slab], sems.at[sem])

    @pl.when(flag_ref[0] == 1)
    def _():
        for k in range(slabs):
            slab_copy(w_hbm.at[k, pl.ds(0, share)], k, k).start()

    @pl.when(flag_ref[0] == 0)
    def _():
        at = 0
        for own, other in zip(there, near):
            for k in range(own.shape[0]):
                slab_copy(own.at[k], piece_slot(at, slabs), at).start()
                if slabs > 1:
                    slab_copy(other.at[k], piece_slot(at + 1, slabs), at + 1).start()
                at = at + 2

    picks = picks_ref.shape[0]
    scaling = (width // H) ** (-0.5)
    vec = vec_ref[...]

    def row(k):
        return vec[k : k + 1]

    pick_pos = one_hot(cols_ref[:, 1:2], LONGEST)
    picked = picks_ref[...]
    select = one_hot(picked[:, 0:1], length)
    queries = q_ref[...]
    d_spread = spread_heads(d_attended_ref[...], width)
    q_spread = spread_heads(queries, width)
    g_vec_ref[...] = g_vec_in_ref[...]
    centered, scale = norm_parts(x_ref[...])
    normed = (centered * row(0) + row(1)).astype(low)
    normed_c = dot_plain(select, normed).astype(low)
    for k in range(slabs):
        slab_copy(w_hbm.at[k, pl.ds(0, share)], k, k).wait()
    keys_all = dot_plain(normed, weight(w_ref, 1)).astype(low)
    values = (dot_plain(normed, weight(w_ref, 2)) + row(7)).astype(low)
    probs = attention_weights(queries, keys_all, picked, docs_ref[...])
    d_probs = dot_last(d_spread, values)
    row_inner = jnp.sum(probs * d_probs, axis=-1, keepdims=True)
    d_scores = (probs * (d_probs - row_inner)).astype(low)
    d_query = (join_heads(dot_plain(d_scores, keys_all), picks, width) * scaling).astype(low)
    g_attn_ref[:, :width] = dot_first(normed_c, d_query).astype(low)
    g_vec_ref[6:7] += column_sum(d_query)
    d_key = (dot_first(d_scores, q_spread) * scaling).astype(low)
    d_value = dot_first(probs.astype(low), d_spread).astype(low)
    g_vec_ref[7:8] += column_sum(d_value)
    d_chosen = dot_first(select, dot_last(d_query, weight(w_ref, 0)).astype(low))
    d_normed = dot_last(d_key, weight(w_ref, 1)) + dot_last(d_value, weight(w_ref, 2))
    d_normed = d_normed + d_chosen
    d_embed, d_gain, d_shift = norm_back(d_normed, centered, scale, row(0))
    g_vec_ref[0:1] += d_gain
    g_vec_ref[1:2] += d_shift
    d_embed = d_embed + lax.dot_general(
        select.astype(wide),
        d_mid_ref[...],
        (((0,), (0,)), ((), ())),
        precision=lax.Precision.HIGHEST,
        preferred_element_type=wide,
    )
    d_embed = d_embed.astype(low)
    pick = one_hot(cols_ref[:, 0:1], devices * capacity)
    sent_ref[...] = dot_first(pick, d_embed).astype(low).reshape(devices, capacity, width)
    d_both = jnp.concatenate([d_key, d_value], axis=1)
    g_attn_ref[:, width : 3 * width] = dot_first(normed, d_both).astype(low)
    g_pos = dot_first(pick_pos, d_embed)
    pos_share = LONGEST // devices
    if pos_share % 16:
        g_pos_ref[...] = g_pos
        return
    lane = lax.broadcasted_iota(jnp.int32, (16, LANES), 1)
    unit = jnp.where(lane == lax.broadcasted_iota(jnp.int32, (16, LANES), 0), 1.0, 0.0)
    turned_vec = lax.dot_general(
        g_vec_ref[...],
        unit,
        (((0,), (0,)), ((), ())),
        precision=lax.Precision.HIGHEST,
        preferred_element_type=wide,
    )
    g_attn_ref[:, 3 * width : 3 * width + LANES] = turned_vec.astype(low)
    g_pos = g_pos.astype(low)
    folds = width // devices // pos_share
    part = width // folds
    for d in range(devices):
        for k in range(folds):
            first = (d * folds + k) * pos_share
            g_attn_ref[first : first + pos_share, 3 * width + LANES :] = g_pos[
                d * pos_share : (d + 1) * pos_share, k * part : (k + 1) * part
            ]
    g_pos_ref[...] = jnp.zeros(g_pos_ref.shape, wide)


def run_upper(d_final, vec, kept, whole):
    count, width = d_final.shape
    slabs = whole.shape[0]
    vmem = pl.BlockSpec(memory_space=pltpu.VMEM)
    hbm = pl.BlockSpec(memory_space=pl.ANY)
    return pl.pallas_call(
        upper_kernel,
        out_shape=(
            jax.ShapeDtypeStruct((count // MB, 2 * width), wide),
            jax.ShapeDtypeStruct((count // MB, 2 * width), wide),
            jax.ShapeDtypeStruct((16, width), wide),
            jax.ShapeDtypeStruct((count, 6 * width), low),
        ),
        in_specs=[vmem] * 5 + [hbm],
        out_specs=(vmem,) * 4,
        scratch_shapes=[
            pltpu.VMEM((slabs, 9 * width // slabs, width), low),
            pltpu.SemaphoreType.DMA((3,)),
        ],
        compiler_params=kernel_limit(44),
        cost_estimate=kernel_cost(9),
        name="upper_backward",
    )(d_final, vec, *kept, whole)


def run_lower(flag, upper, cols, docs, picked, vec, x_embed, queries, whole, there, near, devices):
    length = cols.shape[0]
    width = vec.shape[1]
    capacity = 2 * length // devices
    loose = LONGEST // devices % 16
    vmem = pl.BlockSpec(memory_space=pltpu.VMEM)
    hbm = pl.BlockSpec(memory_space=pl.ANY)

    def shape(dims, kind):
        return jax.ShapeDtypeStruct(dims, kind)

    return pl.pallas_call(
        functools.partial(lower_kernel, len(there)),
        out_shape=(
            shape((devices, capacity, width), low),
            shape((width, 3 * width + (0 if loose else LANES + LONGEST)), low),
            shape((16, width), wide),
            shape((LONGEST if loose else 8, width), wide),
        ),
        in_specs=[pl.BlockSpec(memory_space=pltpu.SMEM)] + [vmem] * 9 + [hbm] * (1 + 2 * len(there)),
        out_specs=(vmem,) * 4,
        scratch_shapes=[
            pltpu.VMEM((whole.shape[0], 3 * width // whole.shape[0], width), low),
            pltpu.SemaphoreType.DMA((whole.shape[0],)),
        ],
        compiler_params=kernel_limit(44),
        cost_estimate=kernel_cost(15),
        name="lower_backward",
    )(flag, *upper, cols, docs, picked, vec, x_embed, queries, whole, *there, *near)


def combine_kernel(parts_ref, d_final_ref, totals_ref):
    devices, held, width = parts_ref.shape
    picks = d_final_ref.shape[0]
    count = width // 3
    stats = parts_ref[:, 2 * picks :, :].astype(wide)
    stats = (
        stats[:, :, :count] + stats[:, :, count : 2 * count] + stats[:, :, 2 * count :]
    )
    here = lax.axis_index("dp") * picks + lax.broadcasted_iota(jnp.int32, (picks, count), 0)
    mine = jnp.where(here == lax.broadcasted_iota(jnp.int32, (picks, count), 1), 1.0, 0.0)
    shares = []
    for k in range(2):
        maxima, sums = stats[:, 2 * k], stats[:, 2 * k + 1]
        big = jnp.max(maxima, axis=0, keepdims=True)
        total = big + jnp.log(jnp.sum(sums * jnp.exp(maxima - big), axis=0, keepdims=True))
        totals_ref[k : k + 1] = total
        shares.append(
            lax.dot_general(
                mine,
                jnp.exp(maxima - total),
                (((1,), (1,)), ((), ())),
                precision=lax.Precision.HIGHEST,
                preferred_element_type=wide,
            )
        )
    total = jnp.zeros((picks, width), wide)
    for d in range(devices):
        total = total + 2.0 * shares[1][:, d : d + 1] * parts_ref[d, picks : 2 * picks].astype(wide)
        total = total - shares[0][:, d : d + 1] * parts_ref[d, :picks].astype(wide)
    d_final_ref[...] = total


def run_combine(parts, picks):
    width = parts.shape[2]
    vmem = pl.BlockSpec(memory_space=pltpu.VMEM)
    return pl.pallas_call(
        combine_kernel,
        out_shape=(
            jax.ShapeDtypeStruct((picks, width), wide),
            jax.ShapeDtypeStruct((2, width // 3), wide),
        ),
        in_specs=[vmem],
        out_specs=(vmem, vmem),
        compiler_params=kernel_limit(16),
        cost_estimate=kernel_cost(3),
        name="combine_parts",
    )(parts)


def turned(column):
    count = column.shape[0]
    here = lax.broadcasted_iota(jnp.int32, (count, count), 0)
    there = lax.broadcasted_iota(jnp.int32, (count, count), 1)
    return jnp.sum(jnp.where(here == there, column, 0), axis=0, keepdims=True)


def stood(row):
    count = row.shape[1]
    here = lax.broadcasted_iota(jnp.int32, (count, count), 0)
    there = lax.broadcasted_iota(jnp.int32, (count, count), 1)
    return jnp.sum(jnp.where(here == there, row, 0), axis=1, keepdims=True)


def route_kernel(vocab_rows, shard_ref, row_ref, docs_ref, chosen_ref, notes_ref, cols_ref, picks_ref):
    batches, length, _ = cols_ref.shape
    picks = picks_ref.shape[1]
    devices = notes_ref.shape[0]
    capacity = 2 * length // devices
    slot_count = devices * capacity
    here = lax.broadcasted_iota(jnp.int32, (length, length), 0)
    there = lax.broadcasted_iota(jnp.int32, (length, length), 1)
    for m in range(batches):
        owner = shard_ref[m]
        row = stood(row_ref[m])
        docs = docs_ref[m]
        chosen = chosen_ref[m]
        earlier = jnp.where((owner == turned(owner)) & (there < here), 1, 0)
        slot = owner * capacity + jnp.sum(earlier, axis=1, keepdims=True)
        smaller = jnp.where(docs < stood(docs), 1, 0)
        spot = lax.broadcasted_iota(jnp.int32, (length, 1), 0)
        position = spot - jnp.sum(smaller, axis=1, keepdims=True)
        cols_ref[m, :, 0:1] = slot
        cols_ref[m, :, 1:2] = position
        slots = lax.broadcasted_iota(jnp.int32, (length, slot_count), 1)
        request = vocab_rows + jnp.sum(
            jnp.where(slots == slot, row - vocab_rows, 0), axis=0, keepdims=True
        )
        for d in range(devices):
            notes_ref[d : d + 1, m * capacity : (m + 1) * capacity] = request[
                :, d * capacity : (d + 1) * capacity
            ]
        is_next = lax.broadcasted_iota(jnp.int32, (length, picks), 0) == chosen + 1
        ids = jnp.sum(
            jnp.where(is_next, owner * vocab_rows + row, 0), axis=0, keepdims=True
        )
        base = batches * capacity + m * picks
        notes_ref[:, base : base + picks] = jnp.broadcast_to(ids, (devices, picks))
        chosen = stood(chosen)
        among = lax.broadcasted_iota(jnp.int32, (picks, length), 1) == chosen
        picks_ref[m, :, 0:1] = chosen
        picks_ref[m, :, 1:2] = jnp.sum(jnp.where(among, docs, 0), axis=1, keepdims=True)


def run_route(shard, row, docs, chosen, devices, vocab_rows):
    batches, length, _ = shard.shape
    picks = chosen.shape[2]
    vmem = pl.BlockSpec(memory_space=pltpu.VMEM)
    held = batches * (2 * length // devices + picks)
    return pl.pallas_call(
        functools.partial(route_kernel, vocab_rows),
        out_shape=(
            jax.ShapeDtypeStruct((devices, held), jnp.int32),
            jax.ShapeDtypeStruct((batches, length, 2), jnp.int32),
            jax.ShapeDtypeStruct((batches, picks, 2), jnp.int32),
        ),
        in_specs=[vmem] * 4,
        out_specs=(vmem,) * 3,
        compiler_params=kernel_limit(56),
        cost_estimate=kernel_cost(3),
        name="route_tokens",
    )(shard, row, docs, chosen)


def pack_kernel(
    student_ref, attn_in, attn_out, mlp_in, mlp_out, pos, vecs, t_attn_in, t_attn_out, t_mlp_in, t_mlp_out, t_pos, t_vecs, out_ref
):
    is_student = student_ref[0] == 1
    rows, width = attn_out.shape

    def write(refs):
        ins, out, up, down, spots, small = refs
        for j in range(3):
            out_ref[j * rows : (j + 1) * rows] = ins[:, j * width : (j + 1) * width].astype(low)
        out_ref[3 * rows : 4 * rows] = out[...].astype(low)
        for j in range(4):
            out_ref[(4 + j) * rows : (5 + j) * rows] = up[
                :, j * width : (j + 1) * width
            ].astype(low)
        out_ref[8 * rows : 12 * rows] = down[...].astype(low)
        end = 12 * rows + spots.shape[0]
        out_ref[12 * rows : end] = spots[...].astype(low)
        count, share = small.shape
        tall = lax.broadcasted_iota(jnp.int32, (16, count), 0)
        tall = jnp.where(tall == lax.broadcasted_iota(jnp.int32, (16, count), 1), 1.0, 0.0)
        broad = lax.broadcasted_iota(jnp.int32, (share, width), 1)
        broad = jnp.where(broad == lax.broadcasted_iota(jnp.int32, (share, width), 0), 1.0, 0.0)
        moved = dot_plain(tall.astype(low), small[...].astype(low)).astype(low)
        out_ref[end : end + 16] = dot_plain(moved, broad.astype(low)).astype(low)

    @pl.when(is_student)
    def _():
        write((attn_in, attn_out, mlp_in, mlp_out, pos, vecs))

    @pl.when(jnp.logical_not(is_student))
    def _():
        write((t_attn_in, t_attn_out, t_mlp_in, t_mlp_out, t_pos, t_vecs))


def pack_plain(attn_in, attn_out, mlp_in, mlp_out, pos, vecs):
    width = attn_out.shape[1]
    ins = [attn_in[:, j * width : (j + 1) * width] for j in range(3)]
    up = [mlp_in[:, j * width : (j + 1) * width] for j in range(4)]
    parts = [*ins, attn_out, *up, mlp_out, pos, vecs]
    return jnp.concatenate([p.astype(low) for p in parts], axis=0)


def pack(is_student, student, teacher):
    rows, width = student[1].shape

    def padded(parts):
        vecs = parts[5]
        fill = ((0, 16 - vecs.shape[0]), (0, width - vecs.shape[1]))
        return [*parts[:5], jnp.pad(vecs, fill)]

    if rows % 16 or student[4].shape[0] % 16:
        student, teacher = padded(student), padded(teacher)
        return jnp.where(is_student, pack_plain(*student), pack_plain(*teacher))
    total = 12 * rows + student[4].shape[0] + 16
    vmem = pl.BlockSpec(memory_space=pltpu.VMEM)
    return pl.pallas_call(
        pack_kernel,
        out_shape=jax.ShapeDtypeStruct((total, width), low),
        in_specs=[pl.BlockSpec(memory_space=pltpu.SMEM)] + [vmem] * 12,
        out_specs=vmem,
        compiler_params=kernel_limit(56),
        cost_estimate=kernel_cost(3),
        name="pack_weights",
    )(is_student.astype(jnp.int32).reshape(1), *student, *teacher)


def unpack(whole, pos_rows, vec_width):
    devices, _, width = whole.shape
    rows = width // devices
    base = 12 * rows
    owners = LONGEST // pos_rows
    small = whole[:, base + pos_rows : base + pos_rows + 16, :vec_width]
    vec = small.transpose(1, 0, 2).reshape(16, width).astype(wide)
    if devices != 16 or rows % 16 or pos_rows % 16:
        pos = whole[:owners, base : base + pos_rows].reshape(1, LONGEST, width)
        blocks = whole[:, : 8 * rows].reshape(devices, 8, rows, width).transpose(1, 0, 2, 3)
        tail = whole[:, 8 * rows : base].reshape(1, 4 * width, width)
        whole = jnp.concatenate([blocks.reshape(1, 8 * width, width), tail, pos], axis=1)
        owners = 1
    return whole, vec, owners


def table_part(limit, step, block, refs):
    flag_ref, own_ref, rows_ref, other_ref, rows_other_ref, asked_ref, asked_last_ref = refs[:7]
    arrived_ref, arrived_other_ref, both_ref = refs[7:]
    count = arrived_ref.shape[0]

    @pl.when((step == 0) & (flag_ref[0] == 1))
    def _():
        both_ref[:count] = arrived_other_ref[...]
        both_ref[count:] = arrived_ref[...]

    @pl.when((step == 0) & (flag_ref[0] == 0))
    def _():
        both_ref[:count] = arrived_ref[...]
        both_ref[count:] = arrived_other_ref[...]

    ids = step * block + lax.broadcasted_iota(jnp.int32, (block, 1), 0)
    wanted = jnp.where(ids == asked_ref[...], 1.0, 0.0).astype(low)
    wanted_last = jnp.where(ids == asked_last_ref[...], 1.0, 0.0).astype(low)
    is_last = flag_ref[0] == 1

    def ordered(own_ref, other_ref):
        own, other = own_ref[...], other_ref[...]
        return jnp.where(is_last, other, own), jnp.where(is_last, own, other)

    d_low_first, d_low_last = ordered(own_ref, other_ref)
    rows_first, rows_last = ordered(rows_ref, rows_other_ref)
    return ids, (
        dot_plain(d_low_first, rows_first)
        + dot_plain(d_low_last, rows_last)
        + dot_plain(wanted, both_ref[:count])
        + dot_plain(wanted_last, both_ref[count:])
    )


def table_kernel(limit, *refs):
    out_ref, square_ref, both_ref = refs[9:]
    step = pl.program_id(0)
    block = refs[1].shape[0]
    ids, gradient = table_part(limit, step, block, (*refs[:9], both_ref))
    out_ref[...] = gradient
    inside = jnp.where(ids < limit, gradient, 0.0)
    squares = jnp.sum((inside * inside).reshape(block // 8, 8, -1), axis=0)

    @pl.when(step == 0)
    def _():
        square_ref[...] = squares

    @pl.when(step > 0)
    def _():
        square_ref[...] += squares


def table_specs(parts, vocab_rows, cuts):
    block = -(-vocab_rows // (16 * cuts)) * 16
    steps = -(-vocab_rows // block)

    def fixed(dims):
        return pl.BlockSpec(dims, lambda k: (0, 0))

    tall = pl.BlockSpec((block, parts[1].shape[1]), lambda k: (k, 0))
    specs = [pl.BlockSpec(memory_space=pltpu.SMEM), tall, fixed(parts[2].shape), tall]
    specs += [fixed(part.shape) for part in parts[4:]]
    both = pltpu.VMEM((2 * parts[7].shape[0], parts[7].shape[1]), low)
    return block, steps, specs, fixed, both


def run_table(parts, vocab_rows):
    width = parts[2].shape[1]
    block, steps, specs, fixed, both = table_specs(parts, vocab_rows, 6)
    return pl.pallas_call(
        functools.partial(table_kernel, vocab_rows),
        grid=(steps,),
        out_shape=(
            jax.ShapeDtypeStruct((vocab_rows, width), wide),
            jax.ShapeDtypeStruct((8, width), wide),
        ),
        in_specs=specs,
        out_specs=(pl.BlockSpec((block, width), lambda k: (k, 0)), fixed((8, width))),
        scratch_shapes=[both],
        compiler_params=kernel_limit(58),
        cost_estimate=kernel_cost(17),
        name="table_gradient",
    )(*parts)


def norm_kernel(products_ref, squares_ref, mine_ref, theirs_ref, kl_ref, shared_ref, note_ref):
    shared = mine_ref[...].astype(wide) + theirs_ref[...].astype(wide)
    shared_ref[...] = shared
    total = jnp.sum(shared * shared) + jnp.sum(squares_ref[...]) + products_ref[0]
    lane = lax.broadcasted_iota(jnp.int32, note_ref.shape, 2)
    note_ref[...] = jnp.where(lane == 0, total, jnp.where(lane == 1, kl_ref[0], 0.0))


def run_norm(products, squares, mine, theirs, kl_local, copies):
    vmem = pl.BlockSpec(memory_space=pltpu.VMEM)
    smem = pl.BlockSpec(memory_space=pltpu.SMEM)
    return pl.pallas_call(
        norm_kernel,
        out_shape=(
            jax.ShapeDtypeStruct(mine.shape, wide),
            jax.ShapeDtypeStruct((copies, 1, LANES), wide),
        ),
        in_specs=[smem, vmem, vmem, vmem, smem],
        out_specs=(vmem, vmem),
        compiler_params=kernel_limit(16),
        cost_estimate=kernel_cost(2),
        name="norm_note",
    )(products.reshape(1), squares, mine, theirs, kl_local.reshape(1))


def adam_kernel(count, factor_ref, *refs):
    ins, outs = refs[: 4 * count], refs[4 * count :]
    for k in range(count):
        master, one, two, gradient = [ref[...] for ref in ins[4 * k : 4 * k + 4]]
        results = adam_update(master, one, two, gradient, factor_ref[0])
        for ref, value in zip(outs[3 * k : 3 * k + 3], results):
            ref[...] = value


def run_adam(factor, groups):
    flat = [value for group in groups for value in group]
    vmem = pl.BlockSpec(memory_space=pltpu.VMEM)
    outs = [jax.ShapeDtypeStruct(g[0].shape, wide) for g in groups for _ in range(3)]
    return pl.pallas_call(
        functools.partial(adam_kernel, len(groups)),
        out_shape=tuple(outs),
        in_specs=[pl.BlockSpec(memory_space=pltpu.SMEM)] + [vmem] * len(flat),
        out_specs=(vmem,) * len(outs),
        compiler_params=kernel_limit(58),
        cost_estimate=kernel_cost(6),
        name="small_updates",
    )(factor.reshape(1), *flat)


def shards(
    token_shard,
    token_row,
    doc_ids,
    loss_rows,
    teacher_table,
    teacher_pos,
    teacher_attn_in,
    teacher_attn_out,
    teacher_mlp_in,
    teacher_mlp_out,
    teacher_vecs,
    table,
    pos_table,
    attn_in,
    attn_out,
    mlp_in,
    mlp_out,
    vectors,
    table_m,
    pos_m,
    attn_in_m,
    attn_out_m,
    mlp_in_m,
    mlp_out_m,
    vectors_m,
    table_v,
    pos_v,
    attn_in_v,
    attn_out_v,
    mlp_in_v,
    mlp_out_v,
    vectors_v,
):
    part = lax.axis_index("pair")
    is_student = part == 1
    me = lax.axis_index("dp")
    devices = lax.axis_size("dp")
    vocab_rows, width = table.shape
    hidden = mlp_in.shape[1]
    rows = attn_in.shape[0]
    fold_rows = mlp_out.shape[0]
    vec_count, vec_width = vectors.shape
    pos_count = pos_table.shape[0]
    swap = [(0, 1), (1, 0)]
    to_teacher = [(1, 0)]
    to_student = [(0, 1)]

    length = token_row.shape[2]
    picks = loss_rows.shape[2]
    capacity = 2 * length // devices
    slot_count = devices * capacity
    total_rows = MB * devices * picks
    student_flag = is_student.astype(jnp.int32).reshape(1)
    docs = doc_ids
    notes, cols, picked = run_route(
        token_shard[:, 0], token_row, docs, loss_rows, devices, vocab_rows
    )
    arrived_notes = lax.all_to_all(notes, "dp", split_axis=0, concat_axis=0, tiled=True)
    arrived_notes, flag = tied(arrived_notes, is_student)
    asked = arrived_notes[:, : MB * capacity]
    targets = arrived_notes[:, MB * capacity :].reshape(devices, MB, picks).transpose(1, 0, 2)
    targets = targets.reshape(MB, devices * picks)[part]

    own_block = pack(
        flag,
        (attn_in, attn_out, mlp_in, mlp_out, pos_table, vectors),
        (
            teacher_attn_in,
            teacher_attn_out,
            teacher_mlp_in,
            teacher_mlp_out,
            teacher_pos,
            teacher_vecs,
        ),
    )
    safe = jnp.minimum(asked, vocab_rows - 1)
    found = lax.cond(
        is_student,
        lambda at: jnp.take(table, at, axis=0).astype(low),
        lambda at: jnp.take(teacher_table, at, axis=0),
        safe,
    )
    def over(value):
        return lax.ppermute(value, "pair", to_teacher)

    table_low = table.astype(low)

    def after(distance, ahead, behind):
        nonlocal table_low
        if distance == 1:
            ahead, behind, _ = tied(ahead, behind, found)
        if distance == 2:
            ahead, behind, table_low = tied(ahead, behind, table)
            table_low = table_low.astype(low)
        return ahead, behind

    if devices == 16 and rows % 16 == 0 and pos_count % 16 == 0:
        whole, early, late = ring_gather(own_block, after, over, 3 * rows)
    else:
        whole, early, late = lax.all_gather(own_block, "dp", axis=0), None, None
    back = lax.all_to_all(found, "dp", split_axis=0, concat_axis=0, tiled=True)
    whole, vec, owners_pos = unpack(whole, pos_count, vec_width)
    final, own_final, aims, x_embed, queries, mid, pre, top, lefts = run_forward(
        student_flag, cols, docs, picked, back, vec, whole, owners_pos
    )

    def on_both(value):
        return jnp.where(is_student, value, over(value))

    def across(value):
        return lax.ppermute(value, "dp", [(d, d ^ 1) for d in range(devices)])

    core = me % 2
    other_final = lax.ppermute(final, "pair", swap)
    if late is None:
        there = [over(whole[:, : 3 * width])]
    else:
        other_final, late = tied(other_final, late)
        there = [early, over(late)]
    x_over = jnp.concatenate([x_embed[0], queries[:picks].astype(wide), vec], axis=0)
    both = jnp.stack(
        [
            jnp.where(is_student, other_final, own_final),
            jnp.where(is_student, own_final, other_final),
        ]
    )
    every = lax.all_gather(both.reshape(2 * picks, width), "dp", axis=0)
    cuts = (0, 3 * length // 8, x_over.shape[0])
    x_over = [x_over[a:b] for a, b in zip(cuts, cuts[1:])]
    other_final, x_over[0] = tied(other_final, x_over[0])
    x_over[0] = over(x_over[0])
    lefts = lax.all_to_all(lefts, "dp", split_axis=0, concat_axis=0, tiled=True)
    every, lefts, x_over[0], x_over[1] = tied(every, lefts, x_over[0], x_over[1])
    lefts = lefts.reshape(-1, lefts.shape[2])
    x_over[1] = over(x_over[1])
    every = every.reshape(devices, 2, picks, width).transpose(1, 0, 2, 3)
    every = every.reshape(2, devices * picks, width)
    teacher_rows, student_rows = every[0], every[1]
    teacher_logits = dot_last(teacher_rows, teacher_table)
    logits = dot_last(student_rows, table_low)
    teacher_max = jnp.max(teacher_logits, axis=1)
    teacher_exp = jnp.exp(teacher_logits - teacher_max[:, None])
    teacher_sum = jnp.sum(teacher_exp, axis=1)
    own_max = jnp.max(logits, axis=1)
    own_exp = jnp.exp(logits - own_max[:, None])
    own_sum = jnp.sum(own_exp, axis=1)
    own_sum, *there = tied(own_sum, *there)
    near = [across(value) for value in there]
    stats = jnp.stack([teacher_max, teacher_sum, own_max, own_sum])
    high = lax.reduce_precision(stats, 8, 7)
    middle = lax.reduce_precision(stats - high, 8, 7)
    wide_rows = devices * picks * 3 == width
    pieces = jnp.stack([high, middle, stats - high - middle], axis=1).astype(low)
    pieces = pieces.reshape(-1, width)
    d_parts = jnp.concatenate(
        [
            dot_plain(teacher_exp.astype(low), table_low).astype(low).reshape(devices, picks, width),
            dot_plain(own_exp.astype(low), table_low).astype(low).reshape(devices, picks, width),
            jnp.broadcast_to(pieces[None], (devices,) + pieces.shape),
        ],
        axis=1,
    )
    d_parts = lax.all_to_all(d_parts, "dp", split_axis=0, concat_axis=0, tiled=True)
    d_parts, x_over[1] = tied(d_parts, x_over[1])
    if wide_rows:
        d_final, totals = run_combine(d_parts, picks)
        teacher_total, own_total = totals[0], totals[1]
    else:
        d_parts = d_parts.astype(wide)
        stats = jnp.sum(d_parts[:, 2 * picks :].reshape(devices, 4, 3, -1), axis=2)

        def log_total(maxima, sums):
            big = jnp.max(maxima, axis=0)
            return big + jnp.log(jnp.sum(sums * jnp.exp(maxima - big[None]), axis=0))

        teacher_total = log_total(stats[:, 0], stats[:, 1])
        own_total = log_total(stats[:, 2], stats[:, 3])

        def shares(maxima, totals):
            scale = jnp.exp(maxima - totals[None])
            return lax.dynamic_slice_in_dim(scale, me * picks, picks, 1)[..., None]

        d_final = jnp.sum(
            2.0 * shares(stats[:, 2], own_total) * d_parts[:, picks : 2 * picks]
            - shares(stats[:, 0], teacher_total) * d_parts[:, :picks],
            axis=0,
        )
    d_final_first = lax.ppermute(d_final, "pair", to_student)
    d_final = (jnp.concatenate([d_final_first, d_final], axis=0) - aims) * (1.0 / total_rows)
    teacher_total, own_total, d_final_first = tied(teacher_total, own_total, d_final_first)
    teacher_total, own_total = teacher_total[:, None], own_total[:, None]
    teacher_log = teacher_logits - teacher_total
    teacher_prob = jnp.exp(teacher_log)
    own_log = logits - own_total
    own_prob = jnp.exp(own_log)
    kl_local = jnp.sum(teacher_prob * (teacher_log - own_log))
    vocab_iota = jnp.arange(vocab_rows, dtype=jnp.int32)
    target_hit = (targets - me * vocab_rows)[:, None] == vocab_iota[None, :]
    d_logits = (2.0 * own_prob - target_hit.astype(wide) - teacher_prob) * (1.0 / total_rows)
    d_low = d_logits.astype(low)
    passed_first, passed_last, g_vecs, rights = run_upper(d_final, vec, (mid, pre, top), whole)
    passed_there, d_low = tied(over(passed_first), d_low)
    passed = jnp.where(is_student, passed_last, passed_there)
    x_last = jnp.concatenate([x_embed[1], queries[picks:].astype(wide), vec], axis=0)
    x_last = jnp.where(is_student, x_last, jnp.concatenate(x_over, axis=0))
    sent, g_attn, g_vecs, g_pos = run_lower(
        student_flag,
        (passed[:, :width], passed[:, width:].astype(low), jnp.where(is_student, g_vecs, 0.0)),
        cols[part],
        docs[part],
        picked[part],
        x_last[length + picks :],
        x_last[:length],
        x_last[length : length + picks].astype(low),
        whole,
        there,
        near,
        devices,
    )
    sent, rows_sent, d_low_sent = tied(sent, student_rows, d_low)
    rows_other = lax.ppermute(rows_sent, "pair", swap)
    arrived = lax.all_to_all(sent, "dp", split_axis=0, concat_axis=0, tiled=True)
    arrived = arrived.reshape(slot_count, width)

    pos_share = LONGEST // devices
    if pos_share % 16:
        g_vecs = jnp.pad(g_vecs.T, ((0, 0), (0, LANES - g_vecs.shape[0]))).astype(low)
        parts = g_pos.reshape(devices, pos_share, -1, LONGEST).transpose(0, 2, 1, 3)
        parts = parts.reshape(width, LONGEST).astype(low)
        shared = jnp.concatenate([g_attn, g_vecs, parts], axis=1)
    else:
        shared = g_attn
    if devices % 2:
        shared = lax.psum_scatter(shared, "dp", scatter_dimension=0, tiled=True)
    else:
        chips = shared.reshape(devices // 2, 2, rows, -1)
        near_sum = across(lax.dynamic_index_in_dim(chips, 1 - core, 1, keepdims=False))
        near_sum, rows_other = tied(near_sum, rows_other)
        mine = lax.dynamic_index_in_dim(chips, core, 1, keepdims=False)
        chips = (mine.astype(wide) + near_sum.astype(wide)).astype(low)
    d_low_other = lax.ppermute(d_low_sent, "pair", swap)

    rights = lax.all_gather(rights, "dp", axis=0, tiled=True)
    at = (0, fold_rows, fold_rows + rows, fold_rows + 2 * rows)
    ends = (0, width, width + hidden, 2 * width + hidden)
    products = [
        dot_first(lefts[:, at[k] : at[k + 1]], rights[:, ends[k] : ends[k + 1]]).astype(low)
        for k in range(3)
    ]
    squares = jnp.zeros((), wide)
    for product in products:
        squares = squares + jnp.sum(jnp.square(product.astype(wide)))
    products[1] = products[1].reshape(rows, 4, width).transpose(1, 0, 2).reshape(4 * rows, width)
    products = jnp.concatenate(products, axis=0)
    d_low_turned, d_low_other = d_low.T, d_low_other.T
    arrived, products, squares, d_low_turned, d_low_other = tied(
        arrived, products, squares, d_low_turned, d_low_other
    )
    arrived_other = lax.ppermute(arrived, "pair", swap)
    if devices % 2 == 0:
        chips, arrived = tied(chips, arrived)
        columns = [[2 * k + c for k in range(devices // 2)] for c in (0, 1)]
        chips = lax.all_to_all(
            chips, "dp", split_axis=0, concat_axis=0, axis_index_groups=columns, tiled=True
        )
    asked = asked.reshape(devices, MB, capacity).transpose(1, 0, 2).reshape(MB, 1, slot_count)
    asked_first, asked_last = asked[0], asked[1]
    own_last = is_student.astype(jnp.int32).reshape(1)
    parts = (
        own_last,
        d_low_turned,
        student_rows,
        d_low_other,
        rows_other,
        asked_first,
        asked_last,
        arrived,
        arrived_other,
    )
    if devices % 2 == 0:
        shared = jnp.sum(chips.astype(wide), axis=0).astype(low)
    pos_near = shared[:, 3 * width + LANES :]
    pos_near = pos_near.reshape(-1, pos_share, LONGEST).transpose(1, 0, 2).reshape(pos_share, width)
    pos_near = jnp.pad(pos_near, ((0, max(0, LANES // 2 - pos_share)), (0, 0)))
    pos_near = lax.all_gather(pos_near, "dp", axis=0)[:, :pos_share].reshape(LONGEST, width)
    pos_near = jnp.concatenate([pos_near, jnp.zeros((pos_count, width), low)], axis=0)
    pos_near = lax.dynamic_slice(
        pos_near, (jnp.minimum(me * pos_count, LONGEST), 0), (pos_count, width)
    )
    arrived_other, shared = tied(arrived_other, shared)
    shared_other = lax.ppermute(shared, "pair", swap)
    arrived_other, products = tied(arrived_other, products)
    products_there = over(products)
    parts = (*parts[:-1], arrived_other)
    g_table, table_squares = run_table(parts, vocab_rows)
    table_squares, products_there, shared_other = tied(
        table_squares, products_there, shared_other
    )
    shared, note = run_norm(squares, table_squares, shared, shared_other, kl_local, 2 * devices)
    totals = lax.all_to_all(note, ("pair", "dp"), split_axis=0, concat_axis=0, tiled=True)
    grad_norm = jnp.sqrt(jnp.sum(totals[devices:, 0, 0]))
    kl_mean = jnp.sum(totals[:, 0, 1]) / total_rows
    factor = jnp.minimum(1.0, clip_limit / (grad_norm + 1e-06))
    factor, pos_near = tied(factor, pos_near)
    table_out = adam_update(table, table_m, table_v, g_table, factor)
    products = jnp.where(is_student, products, products_there).astype(wide)
    g_mlp_out, g_attn_out = products[:fold_rows], products[fold_rows + 4 * rows :]
    g_mlp_in = products[fold_rows : fold_rows + 4 * rows].reshape(4, rows, width)
    g_mlp_in = g_mlp_in.transpose(1, 0, 2).reshape(rows, hidden)
    g_pos = pos_near.astype(wide) + lax.ppermute(pos_near, "pair", swap).astype(wide)
    g_attn_in = shared[:, : 3 * width]
    g_vecs = shared[:, 3 * width : 3 * width + vec_count].T
    smalls = (g_pos, g_attn_in, g_attn_out, g_mlp_in, g_mlp_out, g_vecs)
    masters = (pos_table, attn_in, attn_out, mlp_in, mlp_out, vectors)
    firsts = (pos_m, attn_in_m, attn_out_m, mlp_in_m, mlp_out_m, vectors_m)
    seconds = (pos_v, attn_in_v, attn_out_v, mlp_in_v, mlp_out_v, vectors_v)
    small_out = run_adam(factor, list(zip(masters, firsts, seconds, smalls)))
    return (*table_out, *small_out, grad_norm, kl_mean)


def solution(mesh):
    return jax.shard_map(
        shards,
        mesh=mesh,
        in_specs=(
            P(None, "dp", None, None),
            P(None, "dp", None),
            P(None, "dp", None),
            P(None, "dp", None),
            P("dp", None),
            P("dp", None),
            P("dp", None),
            P("dp", None),
            P("dp", None),
            P("dp", None),
            P(None, "dp"),
            P("dp", None),
            P("dp", None),
            P("dp", None),
            P("dp", None),
            P("dp", None),
            P("dp", None),
            P(None, "dp"),
            P("dp", None),
            P("dp", None),
            P("dp", None),
            P("dp", None),
            P("dp", None),
            P("dp", None),
            P(None, "dp"),
            P("dp", None),
            P("dp", None),
            P("dp", None),
            P("dp", None),
            P("dp", None),
            P("dp", None),
            P(None, "dp"),
        ),
        out_specs=(
            P("dp", None),
            P("dp", None),
            P("dp", None),
            P("dp", None),
            P("dp", None),
            P("dp", None),
            P("dp", None),
            P("dp", None),
            P("dp", None),
            P("dp", None),
            P("dp", None),
            P("dp", None),
            P("dp", None),
            P("dp", None),
            P("dp", None),
            P("dp", None),
            P("dp", None),
            P("dp", None),
            P(None, "dp"),
            P(None, "dp"),
            P(None, "dp"),
            P(),
            P(),
        ),
        check_vma=False,
    )
```

```python
import functools

import jax
import jax.numpy as jnp
from jax import lax
from jax.experimental import pallas as pl
from jax.experimental.pallas import tpu as pltpu
from jax.sharding import PartitionSpec as P

H = 12
MB = 2
STEP = 10
LONGEST = 256
LANES = 128
MEBI = 1024 * 1024


learn_rate = 0.25
beta_one = 0.9
beta_two = 0.999
adam_eps = 1e-08
decay_rate = 0.1
clip_limit = 0.02
norm_eps = 1e-05
neg_big = -1000000000.0
gelu_scale = 0.7978845608028654
gelu_cube = 0.044715

low = jnp.bfloat16
wide = jnp.float32


def layer_norm(values, norm_gain, norm_shift):
    center = jnp.mean(values, axis=-1, keepdims=True)
    offsets = values - center
    spread = jnp.mean(offsets * offsets, axis=-1, keepdims=True)
    return offsets * lax.rsqrt(spread + norm_eps) * norm_gain + norm_shift


def gelu_tanh(values):
    return jax.nn.gelu(values, approximate=True)


def dot_plain(left_side, right_side):
    return jnp.dot(left_side, right_side, preferred_element_type=wide)


def dot_first(left_side, right_side):
    return lax.dot_general(
        left_side, right_side, (((0,), (0,)), ((), ())), preferred_element_type=wide
    )


def dot_last(left_side, right_side):
    return lax.dot_general(
        left_side, right_side, (((1,), (1,)), ((), ())), preferred_element_type=wide
    )


def tied(*values):
    return lax.optimization_barrier(values)


def kernel_cost(micros):
    return pl.CostEstimate(
        flops=int(micros * 1e8), transcendentals=0, bytes_accessed=int(micros * 3.4e6)
    )


def kernel_limit(mebi):
    return pltpu.CompilerParams(vmem_limit_bytes=mebi * MEBI)


distances = (0, -1, 1, -2, 2, -3, 3, 4)


def ring_gather(block, after, over, share):
    devices = lax.axis_size("dp")
    chips = devices // 2
    ring = [*range(0, chips, 2), *range(chips - 1, 0, -2)]
    onward = [(2 * ring[k] + c, 2 * ring[(k + 1) % chips] + c) for k in range(chips) for c in (0, 1)]
    backward = [(there, here) for here, there in onward]
    across = [(d, d ^ 1) for d in range(devices)]
    half_rows = block.shape[0] // 32 * 16

    def keep(whole, piece, distance):
        k = 2 * distances.index(distance)
        partner = lax.ppermute(piece, "dp", across)
        whole = lax.dynamic_update_slice(whole, piece[None], (piece_slot(k, devices), 0, 0))
        return lax.dynamic_update_slice(whole, partner[None], (piece_slot(k + 1, devices), 0, 0))

    def step(ahead, behind):
        return lax.ppermute(ahead, "dp", onward), lax.ppermute(behind, "dp", backward)

    near = after(1, *step(block, block))
    far = after(2, *step(*near))
    *far, block, near_ahead, near_behind, blank = tied(
        *far, block, *near, jnp.zeros((), block.dtype)
    )
    whole = jnp.broadcast_to(blank, (devices,) + block.shape)
    sent = [over(piece[:share]) for piece in (block, near_ahead, near_behind)]
    whole = keep(whole, block, 0)
    whole = keep(whole, near_ahead, -1)
    whole = keep(whole, near_behind, 1)
    ahead, behind = after(3, *step(*far))
    ahead, behind, *sent = tied(ahead, behind, *sent)
    sent += [over(piece[:share]) for piece in far]
    whole = keep(whole, far[0], -2)
    whole = keep(whole, far[1], 2)
    first = lax.ppermute(ahead[:half_rows], "dp", onward)
    second = lax.ppermute(behind[half_rows:], "dp", backward)
    whole = keep(whole, ahead, -3)
    whole = keep(whole, behind, 3)
    last = jnp.concatenate([first, second], axis=0)
    late = jnp.stack([ahead[:share], behind[:share], last[:share]])
    return keep(whole, last, 4), jnp.stack(sent), late


def piece_slot(k, count):
    if count == 1:
        return 0
    me = lax.axis_index("dp")
    chip, core = me // 2, me % 2
    chips = count // 2
    line, side = chip // 2, chip % 2
    place = jnp.where(side == 0, line, chips - 1 - line)
    spot = lax.rem(place + distances[k // 2] + chips, chips)
    there = jnp.where(spot < chips // 2, 2 * spot, 2 * (chips - 1 - spot) + 1)
    return 2 * there + (core if k % 2 == 0 else 1 - core)


def adam_update(master, moment_one, moment_two, gradient, factor):
    clipped = gradient * factor
    new_one = beta_one * moment_one + (1.0 - beta_one) * clipped
    new_two = beta_two * moment_two + (1.0 - beta_two) * clipped * clipped
    fixed_one = new_one / (1.0 - beta_one**STEP)
    fixed_two = new_two / (1.0 - beta_two**STEP)
    updated = master - learn_rate * (
        fixed_one / (jnp.sqrt(fixed_two) + adam_eps) + decay_rate * master
    )
    return (updated, new_one, new_two)


def to_all(value, axis):
    copies = lax.axis_size(axis)
    spread = jnp.broadcast_to(value[None], (copies,) + value.shape)
    return lax.all_to_all(spread, axis, split_axis=0, concat_axis=0, tiled=True)


def norm_parts(values):
    center = jnp.mean(values, axis=-1, keepdims=True)
    offsets = values - center
    spread = jnp.mean(offsets * offsets, axis=-1, keepdims=True)
    scale = lax.rsqrt(spread + norm_eps)
    return offsets * scale, scale


def norm_back(grad, centered, scale, gain):
    inner = grad * gain
    mean_one = jnp.mean(inner, axis=-1, keepdims=True)
    mean_two = jnp.mean(inner * centered, axis=-1, keepdims=True)
    d_values = scale * (inner - mean_one - centered * mean_two)
    d_gain = jnp.sum(grad * centered, axis=0, keepdims=True)
    return d_values, d_gain, jnp.sum(grad, axis=0, keepdims=True)


def gelu_back(values):
    inner = gelu_scale * (values + gelu_cube * values * values * values)
    bend = jnp.tanh(inner)
    slope = gelu_scale * (1.0 + 3.0 * gelu_cube * values * values)
    return 0.5 * (1.0 + bend) + 0.5 * values * (1.0 - bend * bend) * slope


def spread_heads(rows, width):
    size = width // H
    head_of = lax.broadcasted_iota(jnp.int32, rows.shape, 1) // size
    nothing = jnp.zeros_like(rows)
    return jnp.concatenate([jnp.where(head_of == h, rows, nothing) for h in range(H)], axis=0)


def join_heads(spread, count, width):
    size = width // H
    head_of = lax.broadcasted_iota(jnp.int32, (count, width), 1) // size
    total = jnp.zeros((count, width), wide)
    for h in range(H):
        total = total + jnp.where(head_of == h, spread[h * count : (h + 1) * count], 0.0)
    return total


def one_hot(column, count):
    spots = lax.broadcasted_iota(jnp.int32, (column.shape[0], count), 1)
    return jnp.where(column == spots, 1.0, 0.0).astype(low)


def weight(w_ref, j):
    devices, _, width = w_ref.shape
    rows = width // devices
    return w_ref[:, j * rows : (j + 1) * rows, :].reshape(width, width)


def weight_tail(w_ref, first):
    devices, _, width = w_ref.shape
    rows = width // devices
    return w_ref[:, first * rows : (first + 4) * rows, :].reshape(4 * width, width)


def position_rows(w_ref, first, owners):
    devices, _, width = w_ref.shape
    base = first * (width // devices)
    return w_ref[:owners, base : base + LONGEST // owners, :].reshape(LONGEST, width)


def weight_copies(w_hbm, w_ref, sems):
    rows = w_ref.shape[2] // w_ref.shape[0]
    cuts = (0, 3 * rows, 4 * rows, 8 * rows, w_ref.shape[1])
    copies = []
    for k in range(4):
        span = pl.ds(cuts[k], cuts[k + 1] - cuts[k])
        copies.append(
            pltpu.make_async_copy(w_hbm.at[:, span, :], w_ref.at[:, span, :], sems.at[k])
        )
    return copies


def attention_weights(queries, keys_all, picked, docs):
    width = queries.shape[1]
    picks, length = queries.shape[0], keys_all.shape[0]
    scaling = (width // H) ** (-0.5)
    scores = dot_last(spread_heads(queries, width), keys_all) * scaling
    spots = lax.broadcasted_iota(jnp.int32, (picks, length), 1)
    allowed = (picked[:, 1:2] == docs) & (spots <= picked[:, 0:1])
    penalty = jnp.where(allowed, 0.0, 1.0)
    blocked = jnp.concatenate([penalty] * H, axis=0) > 0.5
    scores = jnp.where(blocked, neg_big, scores)
    row_max = jnp.max(scores, axis=-1, keepdims=True)
    weights_exp = jnp.exp(scores - row_max)
    return weights_exp / jnp.sum(weights_exp, axis=-1, keepdims=True)


def forward_kernel(
    owners,
    flag_ref,
    cols_ref,
    docs_ref,
    picks_ref,
    back_ref,
    vec_ref,
    w_hbm,
    send_ref,
    own_ref,
    aims_ref,
    x_ref,
    q_ref,
    mid_ref,
    pre_ref,
    top_ref,
    lefts_ref,
    w_ref,
    sems,
):
    copies = weight_copies(w_hbm, w_ref, sems)
    for k in (3, 0, 1, 2):
        copies[k].start()
    devices, held, width = back_ref.shape
    batches, length = cols_ref.shape[:2]
    picks = picks_ref.shape[1]
    capacity = held // batches
    slot_count = devices * capacity
    vec = vec_ref[...]

    def row(k):
        return vec[k : k + 1]

    mixed = []
    for m in range(batches):
        sources = back_ref[:, m * capacity : (m + 1) * capacity, :].reshape(slot_count, width)
        pick = one_hot(cols_ref[m, :, 0:1], slot_count)
        pick_pos = one_hot(cols_ref[m, :, 1:2], LONGEST)
        picked = picks_ref[m]
        select = one_hot(picked[:, 0:1], length)
        embedded = dot_plain(pick, sources)
        if m == 0:
            copies[3].wait()
        pos = position_rows(w_ref, 12, owners)
        x_embed = embedded + dot_plain(pick_pos, pos)
        x_ref[m] = x_embed
        pick_c = dot_plain(select, pick).astype(low)
        pick_pos_c = dot_plain(select, pick_pos).astype(low)
        following = one_hot(picked[:, 0:1] + 1, length)
        aims_ref[m * picks : (m + 1) * picks] = dot_plain(
            dot_plain(following, pick).astype(low), sources
        )
        x_chosen = dot_plain(pick_c, sources) + dot_plain(pick_pos_c, pos)
        normed = (norm_parts(x_embed)[0] * row(0) + row(1)).astype(low)
        normed_c = dot_plain(select, normed).astype(low)
        if m == 0:
            copies[0].wait()
        keys_all = dot_plain(normed, weight(w_ref, 1)).astype(low)
        values = (dot_plain(normed, weight(w_ref, 2)) + row(7)).astype(low)
        queries = (dot_plain(normed_c, weight(w_ref, 0)) + row(6)).astype(low)
        q_ref[m * picks : (m + 1) * picks] = queries
        probs = attention_weights(queries, keys_all, picked, docs_ref[m])
        spread = dot_plain(probs.astype(low), values)
        mixed.append(join_heads(spread, picks, width).astype(low))
        mid_ref[m * picks : (m + 1) * picks] = x_chosen
    mixed = jnp.concatenate(mixed, axis=0)
    copies[1].wait()
    x_mid = mid_ref[...] + dot_plain(mixed, weight(w_ref, 3)) + row(8)
    mid_ref[...] = x_mid
    normed_two = (norm_parts(x_mid)[0] * row(2) + row(3)).astype(low)
    copies[2].wait()
    for j in range(4):
        span = slice(j * width, (j + 1) * width)
        pre_ref[:, span] = dot_plain(normed_two, weight(w_ref, 4 + j)) + row(10 + j)
    activated = gelu_tanh(pre_ref[...]).astype(low)
    x_top = x_mid + dot_plain(activated, weight_tail(w_ref, 8)) + row(9)
    top_ref[...] = x_top
    final = (norm_parts(x_top)[0] * row(4) + row(5)).astype(low)
    is_last = flag_ref[0] == 1
    send_ref[...] = jnp.where(is_last, final[:picks], final[picks:])
    own_ref[...] = jnp.where(is_last, final[picks:], final[:picks])
    share = width // devices
    for d in range(devices):
        lefts_ref[d, :, : 4 * share] = activated[:, 4 * share * d : 4 * share * (d + 1)]
        lefts_ref[d, :, 4 * share : 5 * share] = normed_two[:, share * d : share * (d + 1)]
        lefts_ref[d, :, 5 * share :] = mixed[:, share * d : share * (d + 1)]


def run_forward(flag, cols, docs, picked, back, vec, whole, owners):
    batches, length = cols.shape[:2]
    picks = picked.shape[1]
    devices = back.shape[0]
    width = vec.shape[1]
    vmem = pl.BlockSpec(memory_space=pltpu.VMEM)
    count = batches * picks

    def shape(dims, kind):
        return jax.ShapeDtypeStruct(dims, kind)

    return pl.pallas_call(
        functools.partial(forward_kernel, owners),
        out_shape=(
            shape((picks, width), low),
            shape((picks, width), low),
            shape((count, width), wide),
            shape((batches, length, width), wide),
            shape((count, width), low),
            shape((count, width), wide),
            shape((count, 4 * width), wide),
            shape((count, width), wide),
            shape((devices, count, 6 * width // devices), low),
        ),
        in_specs=[pl.BlockSpec(memory_space=pltpu.SMEM)] + [vmem] * 5 + [pl.BlockSpec(memory_space=pl.ANY)],
        out_specs=(vmem,) * 9,
        scratch_shapes=[
            pltpu.VMEM(whole.shape, low),
            pltpu.SemaphoreType.DMA((4,)),
        ],
        compiler_params=kernel_limit(36),
        cost_estimate=kernel_cost(15),
        name="layer_forward",
    )(flag, cols, docs, picked, back, vec, whole)


def column_sum(values):
    return jnp.sum(values.astype(wide), axis=0, keepdims=True)


def upper_kernel(
    d_final_ref,
    vec_ref,
    mid_ref,
    pre_ref,
    top_ref,
    w_hbm,
    first_ref,
    last_ref,
    g_vec_ref,
    rights_ref,
    w_ref,
    sems,
):
    rows = w_ref.shape[2] // w_ref.shape[0]
    copies = []
    for k, (first, last) in enumerate(((8, 12), (4, 8), (3, 4))):
        count = (last - first) * rows
        copies.append(
            pltpu.make_async_copy(
                w_hbm.at[:, pl.ds(first * rows, count), :],
                w_ref.at[:, pl.ds((first - 3) * rows, count), :],
                sems.at[k],
            )
        )
        copies[k].start()
    width = mid_ref.shape[1]
    hidden = 4 * width
    vec = vec_ref[...]

    def row(k):
        return vec[k : k + 1]

    centered, scale = norm_parts(top_ref[...])
    d_top, d_gain, d_shift = norm_back(d_final_ref[...], centered, scale, row(4))
    g_vec_ref[0:4] = jnp.zeros((4, width), wide)
    g_vec_ref[4:5] = d_gain
    g_vec_ref[5:6] = d_shift
    g_vec_ref[6:8] = jnp.zeros((2, width), wide)
    g_vec_ref[14:16] = jnp.zeros((2, width), wide)
    d_branch = d_top.astype(low)
    rights_ref[:, :width] = d_branch
    g_vec_ref[9:10] = column_sum(d_branch)
    pre = pre_ref[...]
    bend = gelu_back(pre)
    centered, scale = norm_parts(mid_ref[...])
    copies[0].wait()
    d_pre = (dot_last(d_branch, weight_tail(w_ref, 5)) * bend).astype(low)
    rights_ref[:, width : width + hidden] = d_pre
    copies[1].wait()
    d_normed = jnp.zeros(d_top.shape, wide)
    for j in range(4):
        piece = d_pre[:, j * width : (j + 1) * width]
        g_vec_ref[10 + j : 11 + j] = column_sum(piece)
        d_normed = d_normed + dot_last(piece, weight(w_ref, 1 + j))
    d_mid, d_gain, d_shift = norm_back(d_normed, centered, scale, row(2))
    g_vec_ref[2:3] = d_gain
    g_vec_ref[3:4] = d_shift
    d_mid = d_top + d_mid
    picks = first_ref.shape[0]
    first_ref[:, :width] = d_mid[:picks]
    last_ref[:, :width] = d_mid[picks:]
    d_attn_branch = d_mid.astype(low)
    rights_ref[:, width + hidden :] = d_attn_branch
    g_vec_ref[8:9] = column_sum(d_attn_branch)
    copies[2].wait()
    d_attended = dot_last(d_attn_branch, weight(w_ref, 0)).astype(low).astype(wide)
    first_ref[:, width:] = d_attended[:picks]
    last_ref[:, width:] = d_attended[picks:]


def lower_kernel(
    count,
    flag_ref,
    d_mid_ref,
    d_attended_ref,
    g_vec_in_ref,
    cols_ref,
    docs_ref,
    picks_ref,
    vec_ref,
    x_ref,
    q_ref,
    w_hbm,
    *refs,
):
    there, near, rest = refs[:count], refs[count : 2 * count], refs[2 * count :]
    sent_ref, *outs, g_vec_ref, g_pos_ref, w_ref, sems = rest[:-1]
    g_attn_ref = outs[0] if len(outs) == 1 else rest[-1]
    length, width = x_ref.shape
    devices, capacity, _ = sent_ref.shape
    slabs, share, _ = w_ref.shape

    def slab_copy(source, slab, sem):
        return pltpu.make_async_copy(source, w_ref.at[slab], sems.at[sem])

    @pl.when(flag_ref[0] == 1)
    def _():
        for k in range(slabs):
            slab_copy(w_hbm.at[k, pl.ds(0, share)], k, k).start()

    @pl.when(flag_ref[0] == 0)
    def _():
        at = 0
        for own, other in zip(there, near):
            for k in range(own.shape[0]):
                slab_copy(own.at[k], piece_slot(at, slabs), at).start()
                if slabs > 1:
                    slab_copy(other.at[k], piece_slot(at + 1, slabs), at + 1).start()
                at = at + 2

    picks = picks_ref.shape[0]
    scaling = (width // H) ** (-0.5)
    vec = vec_ref[...]

    def row(k):
        return vec[k : k + 1]

    pick_pos = one_hot(cols_ref[:, 1:2], LONGEST)
    picked = picks_ref[...]
    select = one_hot(picked[:, 0:1], length)
    queries = q_ref[...]
    d_spread = spread_heads(d_attended_ref[...], width)
    q_spread = spread_heads(queries, width)
    g_vec_ref[...] = g_vec_in_ref[...]
    centered, scale = norm_parts(x_ref[...])
    normed = (centered * row(0) + row(1)).astype(low)
    normed_c = dot_plain(select, normed).astype(low)
    for k in range(slabs):
        slab_copy(w_hbm.at[k, pl.ds(0, share)], k, k).wait()
    keys_all = dot_plain(normed, weight(w_ref, 1)).astype(low)
    values = (dot_plain(normed, weight(w_ref, 2)) + row(7)).astype(low)
    probs = attention_weights(queries, keys_all, picked, docs_ref[...])
    d_probs = dot_last(d_spread, values)
    row_inner = jnp.sum(probs * d_probs, axis=-1, keepdims=True)
    d_scores = (probs * (d_probs - row_inner)).astype(low)
    d_query = (join_heads(dot_plain(d_scores, keys_all), picks, width) * scaling).astype(low)
    g_attn_ref[:, :width] = dot_first(normed_c, d_query).astype(low)
    g_vec_ref[6:7] += column_sum(d_query)
    d_key = (dot_first(d_scores, q_spread) * scaling).astype(low)
    d_value = dot_first(probs.astype(low), d_spread).astype(low)
    g_vec_ref[7:8] += column_sum(d_value)
    d_chosen = dot_first(select, dot_last(d_query, weight(w_ref, 0)).astype(low))
    d_normed = dot_last(d_key, weight(w_ref, 1)) + dot_last(d_value, weight(w_ref, 2))
    d_normed = d_normed + d_chosen
    d_embed, d_gain, d_shift = norm_back(d_normed, centered, scale, row(0))
    g_vec_ref[0:1] += d_gain
    g_vec_ref[1:2] += d_shift
    d_embed = d_embed + lax.dot_general(
        select.astype(wide),
        d_mid_ref[...],
        (((0,), (0,)), ((), ())),
        precision=lax.Precision.HIGHEST,
        preferred_element_type=wide,
    )
    d_embed = d_embed.astype(low)
    pick = one_hot(cols_ref[:, 0:1], devices * capacity)
    sent_ref[...] = dot_first(pick, d_embed).astype(low).reshape(devices, capacity, width)
    d_both = jnp.concatenate([d_key, d_value], axis=1)
    g_attn_ref[:, width : 3 * width] = dot_first(normed, d_both).astype(low)
    g_pos = dot_first(pick_pos, d_embed)
    pos_share = LONGEST // devices
    if pos_share % 16:
        g_pos_ref[...] = g_pos
        return
    lane = lax.broadcasted_iota(jnp.int32, (16, LANES), 1)
    unit = jnp.where(lane == lax.broadcasted_iota(jnp.int32, (16, LANES), 0), 1.0, 0.0)
    turned_vec = lax.dot_general(
        g_vec_ref[...],
        unit,
        (((0,), (0,)), ((), ())),
        precision=lax.Precision.HIGHEST,
        preferred_element_type=wide,
    )
    g_attn_ref[:, 3 * width : 3 * width + LANES] = turned_vec.astype(low)
    g_pos = g_pos.astype(low)
    folds = width // devices // pos_share
    part = width // folds
    for d in range(devices):
        for k in range(folds):
            first = (d * folds + k) * pos_share
            g_attn_ref[first : first + pos_share, 3 * width + LANES :] = g_pos[
                d * pos_share : (d + 1) * pos_share, k * part : (k + 1) * part
            ]
    g_pos_ref[...] = jnp.zeros(g_pos_ref.shape, wide)
    core = lax.rem(lax.axis_index("dp"), 2)
    held = width // devices
    for k in range(devices // 2):
        for out, side in zip(outs, (core, 1 - core)):
            first = pl.multiple_of((2 * k + side) * held, 16)
            out[k] = g_attn_ref[pl.ds(first, held), :]


def run_upper(d_final, vec, kept, whole):
    count, width = d_final.shape
    slabs = whole.shape[0]
    vmem = pl.BlockSpec(memory_space=pltpu.VMEM)
    hbm = pl.BlockSpec(memory_space=pl.ANY)
    return pl.pallas_call(
        upper_kernel,
        out_shape=(
            jax.ShapeDtypeStruct((count // MB, 2 * width), wide),
            jax.ShapeDtypeStruct((count // MB, 2 * width), wide),
            jax.ShapeDtypeStruct((16, width), wide),
            jax.ShapeDtypeStruct((count, 6 * width), low),
        ),
        in_specs=[vmem] * 5 + [hbm],
        out_specs=(vmem,) * 4,
        scratch_shapes=[
            pltpu.VMEM((slabs, 9 * width // slabs, width), low),
            pltpu.SemaphoreType.DMA((3,)),
        ],
        compiler_params=kernel_limit(44),
        cost_estimate=kernel_cost(9),
        name="upper_backward",
    )(d_final, vec, *kept, whole)


def run_lower(flag, upper, cols, docs, picked, vec, x_embed, queries, whole, there, near, devices):
    length = cols.shape[0]
    width = vec.shape[1]
    capacity = 2 * length // devices
    loose = LONGEST // devices % 16
    broad = 3 * width + (0 if loose else LANES + LONGEST)
    outs = [jax.ShapeDtypeStruct((width, broad), low)]
    if not loose:
        outs = [jax.ShapeDtypeStruct((devices // 2, width // devices, broad), low)] * 2
    vmem = pl.BlockSpec(memory_space=pltpu.VMEM)
    hbm = pl.BlockSpec(memory_space=pl.ANY)

    def shape(dims, kind):
        return jax.ShapeDtypeStruct(dims, kind)

    return pl.pallas_call(
        functools.partial(lower_kernel, len(there)),
        out_shape=(
            shape((devices, capacity, width), low),
            *outs,
            shape((16, width), wide),
            shape((LONGEST if loose else 8, width), wide),
        ),
        in_specs=[pl.BlockSpec(memory_space=pltpu.SMEM)] + [vmem] * 9 + [hbm] * (1 + 2 * len(there)),
        out_specs=(vmem,) * (3 + len(outs)),
        scratch_shapes=[
            pltpu.VMEM((whole.shape[0], 3 * width // whole.shape[0], width), low),
            pltpu.SemaphoreType.DMA((whole.shape[0],)),
            pltpu.VMEM((8, LANES) if loose else (width, broad), low),
        ],
        compiler_params=kernel_limit(44),
        cost_estimate=kernel_cost(15),
        name="lower_backward",
    )(flag, *upper, cols, docs, picked, vec, x_embed, queries, whole, *there, *near)


def combine_kernel(parts_ref, d_final_ref, totals_ref):
    devices, held, width = parts_ref.shape
    picks = d_final_ref.shape[0]
    count = width // 3
    stats = parts_ref[:, 2 * picks :, :].astype(wide)
    stats = (
        stats[:, :, :count] + stats[:, :, count : 2 * count] + stats[:, :, 2 * count :]
    )
    here = lax.axis_index("dp") * picks + lax.broadcasted_iota(jnp.int32, (picks, count), 0)
    mine = jnp.where(here == lax.broadcasted_iota(jnp.int32, (picks, count), 1), 1.0, 0.0)
    shares = []
    for k in range(2):
        maxima, sums = stats[:, 2 * k], stats[:, 2 * k + 1]
        big = jnp.max(maxima, axis=0, keepdims=True)
        total = big + jnp.log(jnp.sum(sums * jnp.exp(maxima - big), axis=0, keepdims=True))
        totals_ref[k : k + 1] = total
        shares.append(
            lax.dot_general(
                mine,
                jnp.exp(maxima - total),
                (((1,), (1,)), ((), ())),
                precision=lax.Precision.HIGHEST,
                preferred_element_type=wide,
            )
        )
    total = jnp.zeros((picks, width), wide)
    for d in range(devices):
        total = total + 2.0 * shares[1][:, d : d + 1] * parts_ref[d, picks : 2 * picks].astype(wide)
        total = total - shares[0][:, d : d + 1] * parts_ref[d, :picks].astype(wide)
    d_final_ref[...] = total


def run_combine(parts, picks):
    width = parts.shape[2]
    vmem = pl.BlockSpec(memory_space=pltpu.VMEM)
    return pl.pallas_call(
        combine_kernel,
        out_shape=(
            jax.ShapeDtypeStruct((picks, width), wide),
            jax.ShapeDtypeStruct((2, width // 3), wide),
        ),
        in_specs=[vmem],
        out_specs=(vmem, vmem),
        compiler_params=kernel_limit(16),
        cost_estimate=kernel_cost(3),
        name="combine_parts",
    )(parts)


def turned(column):
    count = column.shape[0]
    here = lax.broadcasted_iota(jnp.int32, (count, count), 0)
    there = lax.broadcasted_iota(jnp.int32, (count, count), 1)
    return jnp.sum(jnp.where(here == there, column, 0), axis=0, keepdims=True)


def stood(row):
    count = row.shape[1]
    here = lax.broadcasted_iota(jnp.int32, (count, count), 0)
    there = lax.broadcasted_iota(jnp.int32, (count, count), 1)
    return jnp.sum(jnp.where(here == there, row, 0), axis=1, keepdims=True)


def route_kernel(vocab_rows, shard_ref, row_ref, docs_ref, chosen_ref, notes_ref, cols_ref, picks_ref):
    batches, length, _ = cols_ref.shape
    picks = picks_ref.shape[1]
    devices = notes_ref.shape[0]
    capacity = 2 * length // devices
    slot_count = devices * capacity
    here = lax.broadcasted_iota(jnp.int32, (length, length), 0)
    there = lax.broadcasted_iota(jnp.int32, (length, length), 1)
    for m in range(batches):
        owner = shard_ref[m]
        row = stood(row_ref[m])
        docs = docs_ref[m]
        chosen = chosen_ref[m]
        earlier = jnp.where((owner == turned(owner)) & (there < here), 1, 0)
        slot = owner * capacity + jnp.sum(earlier, axis=1, keepdims=True)
        smaller = jnp.where(docs < stood(docs), 1, 0)
        spot = lax.broadcasted_iota(jnp.int32, (length, 1), 0)
        position = spot - jnp.sum(smaller, axis=1, keepdims=True)
        cols_ref[m, :, 0:1] = slot
        cols_ref[m, :, 1:2] = position
        slots = lax.broadcasted_iota(jnp.int32, (length, slot_count), 1)
        request = vocab_rows + jnp.sum(
            jnp.where(slots == slot, row - vocab_rows, 0), axis=0, keepdims=True
        )
        for d in range(devices):
            notes_ref[d : d + 1, m * capacity : (m + 1) * capacity] = request[
                :, d * capacity : (d + 1) * capacity
            ]
        is_next = lax.broadcasted_iota(jnp.int32, (length, picks), 0) == chosen + 1
        ids = jnp.sum(
            jnp.where(is_next, owner * vocab_rows + row, 0), axis=0, keepdims=True
        )
        base = batches * capacity + m * picks
        notes_ref[:, base : base + picks] = jnp.broadcast_to(ids, (devices, picks))
        chosen = stood(chosen)
        among = lax.broadcasted_iota(jnp.int32, (picks, length), 1) == chosen
        picks_ref[m, :, 0:1] = chosen
        picks_ref[m, :, 1:2] = jnp.sum(jnp.where(among, docs, 0), axis=1, keepdims=True)


def run_route(shard, row, docs, chosen, devices, vocab_rows):
    batches, length, _ = shard.shape
    picks = chosen.shape[2]
    vmem = pl.BlockSpec(memory_space=pltpu.VMEM)
    held = batches * (2 * length // devices + picks)
    return pl.pallas_call(
        functools.partial(route_kernel, vocab_rows),
        out_shape=(
            jax.ShapeDtypeStruct((devices, held), jnp.int32),
            jax.ShapeDtypeStruct((batches, length, 2), jnp.int32),
            jax.ShapeDtypeStruct((batches, picks, 2), jnp.int32),
        ),
        in_specs=[vmem] * 4,
        out_specs=(vmem,) * 3,
        compiler_params=kernel_limit(56),
        cost_estimate=kernel_cost(3),
        name="route_tokens",
    )(shard, row, docs, chosen)


def pack_kernel(
    student_ref, attn_in, attn_out, mlp_in, mlp_out, pos, vecs, t_attn_in, t_attn_out, t_mlp_in, t_mlp_out, t_pos, t_vecs, out_ref
):
    is_student = student_ref[0] == 1
    rows, width = attn_out.shape

    def write(refs):
        ins, out, up, down, spots, small = refs
        for j in range(3):
            out_ref[j * rows : (j + 1) * rows] = ins[:, j * width : (j + 1) * width].astype(low)
        out_ref[3 * rows : 4 * rows] = out[...].astype(low)
        for j in range(4):
            out_ref[(4 + j) * rows : (5 + j) * rows] = up[
                :, j * width : (j + 1) * width
            ].astype(low)
        out_ref[8 * rows : 12 * rows] = down[...].astype(low)
        end = 12 * rows + spots.shape[0]
        out_ref[12 * rows : end] = spots[...].astype(low)
        count, share = small.shape
        tall = lax.broadcasted_iota(jnp.int32, (16, count), 0)
        tall = jnp.where(tall == lax.broadcasted_iota(jnp.int32, (16, count), 1), 1.0, 0.0)
        broad = lax.broadcasted_iota(jnp.int32, (share, width), 1)
        broad = jnp.where(broad == lax.broadcasted_iota(jnp.int32, (share, width), 0), 1.0, 0.0)
        moved = dot_plain(tall.astype(low), small[...].astype(low)).astype(low)
        out_ref[end : end + 16] = dot_plain(moved, broad.astype(low)).astype(low)

    @pl.when(is_student)
    def _():
        write((attn_in, attn_out, mlp_in, mlp_out, pos, vecs))

    @pl.when(jnp.logical_not(is_student))
    def _():
        write((t_attn_in, t_attn_out, t_mlp_in, t_mlp_out, t_pos, t_vecs))


def pack_plain(attn_in, attn_out, mlp_in, mlp_out, pos, vecs):
    width = attn_out.shape[1]
    ins = [attn_in[:, j * width : (j + 1) * width] for j in range(3)]
    up = [mlp_in[:, j * width : (j + 1) * width] for j in range(4)]
    parts = [*ins, attn_out, *up, mlp_out, pos, vecs]
    return jnp.concatenate([p.astype(low) for p in parts], axis=0)


def pack(is_student, student, teacher):
    rows, width = student[1].shape

    def padded(parts):
        vecs = parts[5]
        fill = ((0, 16 - vecs.shape[0]), (0, width - vecs.shape[1]))
        return [*parts[:5], jnp.pad(vecs, fill)]

    if rows % 16 or student[4].shape[0] % 16:
        student, teacher = padded(student), padded(teacher)
        return jnp.where(is_student, pack_plain(*student), pack_plain(*teacher))
    total = 12 * rows + student[4].shape[0] + 16
    vmem = pl.BlockSpec(memory_space=pltpu.VMEM)
    return pl.pallas_call(
        pack_kernel,
        out_shape=jax.ShapeDtypeStruct((total, width), low),
        in_specs=[pl.BlockSpec(memory_space=pltpu.SMEM)] + [vmem] * 12,
        out_specs=vmem,
        compiler_params=kernel_limit(56),
        cost_estimate=kernel_cost(3),
        name="pack_weights",
    )(is_student.astype(jnp.int32).reshape(1), *student, *teacher)


def unpack(whole, pos_rows, vec_width):
    devices, _, width = whole.shape
    rows = width // devices
    base = 12 * rows
    owners = LONGEST // pos_rows
    small = whole[:, base + pos_rows : base + pos_rows + 16, :vec_width]
    vec = small.transpose(1, 0, 2).reshape(16, width).astype(wide)
    if devices != 16 or rows % 16 or pos_rows % 16:
        pos = whole[:owners, base : base + pos_rows].reshape(1, LONGEST, width)
        blocks = whole[:, : 8 * rows].reshape(devices, 8, rows, width).transpose(1, 0, 2, 3)
        tail = whole[:, 8 * rows : base].reshape(1, 4 * width, width)
        whole = jnp.concatenate([blocks.reshape(1, 8 * width, width), tail, pos], axis=1)
        owners = 1
    return whole, vec, owners


def table_part(limit, step, block, refs):
    flag_ref, own_ref, rows_ref, other_ref, rows_other_ref, asked_ref, asked_last_ref = refs[:7]
    arrived_ref, arrived_other_ref, both_ref = refs[7:]
    count = arrived_ref.shape[0]

    @pl.when((step == 0) & (flag_ref[0] == 1))
    def _():
        both_ref[:count] = arrived_other_ref[...]
        both_ref[count:] = arrived_ref[...]

    @pl.when((step == 0) & (flag_ref[0] == 0))
    def _():
        both_ref[:count] = arrived_ref[...]
        both_ref[count:] = arrived_other_ref[...]

    ids = step * block + lax.broadcasted_iota(jnp.int32, (block, 1), 0)
    wanted = jnp.where(ids == asked_ref[...], 1.0, 0.0).astype(low)
    wanted_last = jnp.where(ids == asked_last_ref[...], 1.0, 0.0).astype(low)
    is_last = flag_ref[0] == 1

    def ordered(own_ref, other_ref):
        own, other = own_ref[...], other_ref[...]
        return jnp.where(is_last, other, own), jnp.where(is_last, own, other)

    d_low_first, d_low_last = ordered(own_ref, other_ref)
    rows_first, rows_last = ordered(rows_ref, rows_other_ref)
    return ids, (
        dot_plain(d_low_first, rows_first)
        + dot_plain(d_low_last, rows_last)
        + dot_plain(wanted, both_ref[:count])
        + dot_plain(wanted_last, both_ref[count:])
    )


def table_kernel(limit, *refs):
    out_ref, square_ref, both_ref = refs[9:]
    step = pl.program_id(0)
    block = refs[1].shape[0]
    ids, gradient = table_part(limit, step, block, (*refs[:9], both_ref))
    out_ref[...] = gradient
    inside = jnp.where(ids < limit, gradient, 0.0)
    squares = jnp.sum((inside * inside).reshape(block // 8, 8, -1), axis=0)

    @pl.when(step == 0)
    def _():
        square_ref[...] = squares

    @pl.when(step > 0)
    def _():
        square_ref[...] += squares


def table_specs(parts, vocab_rows, cuts):
    block = -(-vocab_rows // (16 * cuts)) * 16
    steps = -(-vocab_rows // block)

    def fixed(dims):
        return pl.BlockSpec(dims, lambda k: (0, 0))

    tall = pl.BlockSpec((block, parts[1].shape[1]), lambda k: (k, 0))
    specs = [pl.BlockSpec(memory_space=pltpu.SMEM), tall, fixed(parts[2].shape), tall]
    specs += [fixed(part.shape) for part in parts[4:]]
    both = pltpu.VMEM((2 * parts[7].shape[0], parts[7].shape[1]), low)
    return block, steps, specs, fixed, both


def run_table(parts, vocab_rows):
    width = parts[2].shape[1]
    block, steps, specs, fixed, both = table_specs(parts, vocab_rows, 6)
    return pl.pallas_call(
        functools.partial(table_kernel, vocab_rows),
        grid=(steps,),
        out_shape=(
            jax.ShapeDtypeStruct((vocab_rows, width), wide),
            jax.ShapeDtypeStruct((8, width), wide),
        ),
        in_specs=specs,
        out_specs=(pl.BlockSpec((block, width), lambda k: (k, 0)), fixed((8, width))),
        scratch_shapes=[both],
        compiler_params=kernel_limit(58),
        cost_estimate=kernel_cost(17),
        name="table_gradient",
    )(*parts)


def norm_kernel(products_ref, squares_ref, mine_ref, theirs_ref, kl_ref, shared_ref, note_ref):
    shared = mine_ref[...].astype(wide) + theirs_ref[...].astype(wide)
    shared_ref[...] = shared
    total = jnp.sum(shared * shared) + jnp.sum(squares_ref[...]) + products_ref[0]
    lane = lax.broadcasted_iota(jnp.int32, note_ref.shape, 2)
    note_ref[...] = jnp.where(lane == 0, total, jnp.where(lane == 1, kl_ref[0], 0.0))


def run_norm(products, squares, mine, theirs, kl_local, copies):
    vmem = pl.BlockSpec(memory_space=pltpu.VMEM)
    smem = pl.BlockSpec(memory_space=pltpu.SMEM)
    return pl.pallas_call(
        norm_kernel,
        out_shape=(
            jax.ShapeDtypeStruct(mine.shape, wide),
            jax.ShapeDtypeStruct((copies, 1, LANES), wide),
        ),
        in_specs=[smem, vmem, vmem, vmem, smem],
        out_specs=(vmem, vmem),
        compiler_params=kernel_limit(16),
        cost_estimate=kernel_cost(2),
        name="norm_note",
    )(products.reshape(1), squares, mine, theirs, kl_local.reshape(1))


def adam_kernel(count, factor_ref, *refs):
    ins, outs = refs[: 4 * count], refs[4 * count :]
    for k in range(count):
        master, one, two, gradient = [ref[...] for ref in ins[4 * k : 4 * k + 4]]
        results = adam_update(master, one, two, gradient, factor_ref[0])
        for ref, value in zip(outs[3 * k : 3 * k + 3], results):
            ref[...] = value


def run_adam(factor, groups):
    flat = [value for group in groups for value in group]
    vmem = pl.BlockSpec(memory_space=pltpu.VMEM)
    outs = [jax.ShapeDtypeStruct(g[0].shape, wide) for g in groups for _ in range(3)]
    return pl.pallas_call(
        functools.partial(adam_kernel, len(groups)),
        out_shape=tuple(outs),
        in_specs=[pl.BlockSpec(memory_space=pltpu.SMEM)] + [vmem] * len(flat),
        out_specs=(vmem,) * len(outs),
        compiler_params=kernel_limit(58),
        cost_estimate=kernel_cost(6),
        name="small_updates",
    )(factor.reshape(1), *flat)


def shards(
    token_shard,
    token_row,
    doc_ids,
    loss_rows,
    teacher_table,
    teacher_pos,
    teacher_attn_in,
    teacher_attn_out,
    teacher_mlp_in,
    teacher_mlp_out,
    teacher_vecs,
    table,
    pos_table,
    attn_in,
    attn_out,
    mlp_in,
    mlp_out,
    vectors,
    table_m,
    pos_m,
    attn_in_m,
    attn_out_m,
    mlp_in_m,
    mlp_out_m,
    vectors_m,
    table_v,
    pos_v,
    attn_in_v,
    attn_out_v,
    mlp_in_v,
    mlp_out_v,
    vectors_v,
):
    part = lax.axis_index("pair")
    is_student = part == 1
    me = lax.axis_index("dp")
    devices = lax.axis_size("dp")
    vocab_rows, width = table.shape
    hidden = mlp_in.shape[1]
    rows = attn_in.shape[0]
    fold_rows = mlp_out.shape[0]
    vec_count, vec_width = vectors.shape
    pos_count = pos_table.shape[0]
    swap = [(0, 1), (1, 0)]
    to_teacher = [(1, 0)]
    to_student = [(0, 1)]

    length = token_row.shape[2]
    picks = loss_rows.shape[2]
    capacity = 2 * length // devices
    slot_count = devices * capacity
    total_rows = MB * devices * picks
    student_flag = is_student.astype(jnp.int32).reshape(1)
    docs = doc_ids
    notes, cols, picked = run_route(
        token_shard[:, 0], token_row, docs, loss_rows, devices, vocab_rows
    )
    arrived_notes = lax.all_to_all(notes, "dp", split_axis=0, concat_axis=0, tiled=True)
    arrived_notes, flag = tied(arrived_notes, is_student)
    asked = arrived_notes[:, : MB * capacity]
    targets = arrived_notes[:, MB * capacity :].reshape(devices, MB, picks).transpose(1, 0, 2)
    targets = targets.reshape(MB, devices * picks)[part]

    own_block = pack(
        flag,
        (attn_in, attn_out, mlp_in, mlp_out, pos_table, vectors),
        (
            teacher_attn_in,
            teacher_attn_out,
            teacher_mlp_in,
            teacher_mlp_out,
            teacher_pos,
            teacher_vecs,
        ),
    )
    safe = jnp.minimum(asked, vocab_rows - 1)
    found = lax.cond(
        is_student,
        lambda at: jnp.take(table, at, axis=0).astype(low),
        lambda at: jnp.take(teacher_table, at, axis=0),
        safe,
    )
    def over(value):
        return lax.ppermute(value, "pair", to_teacher)

    table_low = table.astype(low)

    def after(distance, ahead, behind):
        nonlocal table_low
        if distance == 1:
            ahead, behind, _ = tied(ahead, behind, found)
        if distance == 2:
            ahead, behind, table_low = tied(ahead, behind, table)
            table_low = table_low.astype(low)
        return ahead, behind

    if devices == 16 and rows % 16 == 0 and pos_count % 16 == 0:
        whole, early, late = ring_gather(own_block, after, over, 3 * rows)
    else:
        whole, early, late = lax.all_gather(own_block, "dp", axis=0), None, None
    back = lax.all_to_all(found, "dp", split_axis=0, concat_axis=0, tiled=True)
    whole, vec, owners_pos = unpack(whole, pos_count, vec_width)
    final, own_final, aims, x_embed, queries, mid, pre, top, lefts = run_forward(
        student_flag, cols, docs, picked, back, vec, whole, owners_pos
    )

    def on_both(value):
        return jnp.where(is_student, value, over(value))

    def across(value):
        return lax.ppermute(value, "dp", [(d, d ^ 1) for d in range(devices)])

    core = me % 2
    other_final = lax.ppermute(final, "pair", swap)
    if late is None:
        there = [over(whole[:, : 3 * width])]
    else:
        other_final, late = tied(other_final, late)
        there = [early, over(late)]
    x_over = jnp.concatenate([x_embed[0], queries[:picks].astype(wide), vec], axis=0)
    both = jnp.stack(
        [
            jnp.where(is_student, other_final, own_final),
            jnp.where(is_student, own_final, other_final),
        ]
    )
    every = lax.all_gather(both.reshape(2 * picks, width), "dp", axis=0)
    cuts = (0, 13 * length // 32, x_over.shape[0])
    x_over = [x_over[a:b] for a, b in zip(cuts, cuts[1:])]
    other_final, x_over[0] = tied(other_final, x_over[0])
    x_over[0] = over(x_over[0])
    lefts = lax.all_to_all(lefts, "dp", split_axis=0, concat_axis=0, tiled=True)
    every, lefts, x_over[0], x_over[1] = tied(every, lefts, x_over[0], x_over[1])
    lefts = lefts.reshape(-1, lefts.shape[2])
    x_over[1] = over(x_over[1])
    every = every.reshape(devices, 2, picks, width).transpose(1, 0, 2, 3)
    every = every.reshape(2, devices * picks, width)
    teacher_rows, student_rows = every[0], every[1]
    teacher_logits = dot_last(teacher_rows, teacher_table)
    logits = dot_last(student_rows, table_low)
    teacher_max = jnp.max(teacher_logits, axis=1)
    teacher_exp = jnp.exp(teacher_logits - teacher_max[:, None])
    teacher_sum = jnp.sum(teacher_exp, axis=1)
    own_max = jnp.max(logits, axis=1)
    own_exp = jnp.exp(logits - own_max[:, None])
    own_sum = jnp.sum(own_exp, axis=1)
    own_sum, *there = tied(own_sum, *there)
    near = [across(value) for value in there]
    stats = jnp.stack([teacher_max, teacher_sum, own_max, own_sum])
    high = lax.reduce_precision(stats, 8, 7)
    middle = lax.reduce_precision(stats - high, 8, 7)
    wide_rows = devices * picks * 3 == width
    pieces = jnp.stack([high, middle, stats - high - middle], axis=1).astype(low)
    pieces = pieces.reshape(-1, width)
    d_parts = jnp.concatenate(
        [
            dot_plain(teacher_exp.astype(low), table_low).astype(low).reshape(devices, picks, width),
            dot_plain(own_exp.astype(low), table_low).astype(low).reshape(devices, picks, width),
            jnp.broadcast_to(pieces[None], (devices,) + pieces.shape),
        ],
        axis=1,
    )
    d_parts = lax.all_to_all(d_parts, "dp", split_axis=0, concat_axis=0, tiled=True)
    d_parts, x_over[1] = tied(d_parts, x_over[1])
    if wide_rows:
        d_final, totals = run_combine(d_parts, picks)
        teacher_total, own_total = totals[0], totals[1]
    else:
        d_parts = d_parts.astype(wide)
        stats = jnp.sum(d_parts[:, 2 * picks :].reshape(devices, 4, 3, -1), axis=2)

        def log_total(maxima, sums):
            big = jnp.max(maxima, axis=0)
            return big + jnp.log(jnp.sum(sums * jnp.exp(maxima - big[None]), axis=0))

        teacher_total = log_total(stats[:, 0], stats[:, 1])
        own_total = log_total(stats[:, 2], stats[:, 3])

        def shares(maxima, totals):
            scale = jnp.exp(maxima - totals[None])
            return lax.dynamic_slice_in_dim(scale, me * picks, picks, 1)[..., None]

        d_final = jnp.sum(
            2.0 * shares(stats[:, 2], own_total) * d_parts[:, picks : 2 * picks]
            - shares(stats[:, 0], teacher_total) * d_parts[:, :picks],
            axis=0,
        )
    d_final_first = lax.ppermute(d_final, "pair", to_student)
    d_final = (jnp.concatenate([d_final_first, d_final], axis=0) - aims) * (1.0 / total_rows)
    teacher_total, own_total, d_final_first = tied(teacher_total, own_total, d_final_first)
    teacher_total, own_total = teacher_total[:, None], own_total[:, None]
    teacher_log = teacher_logits - teacher_total
    teacher_prob = jnp.exp(teacher_log)
    own_log = logits - own_total
    own_prob = jnp.exp(own_log)
    kl_local = jnp.sum(teacher_prob * (teacher_log - own_log))
    vocab_iota = jnp.arange(vocab_rows, dtype=jnp.int32)
    target_hit = (targets - me * vocab_rows)[:, None] == vocab_iota[None, :]
    d_logits = (2.0 * own_prob - target_hit.astype(wide) - teacher_prob) * (1.0 / total_rows)
    d_low = d_logits.astype(low)
    passed_first, passed_last, g_vecs, rights = run_upper(d_final, vec, (mid, pre, top), whole)
    passed_there, d_low = tied(over(passed_first), d_low)
    passed = jnp.where(is_student, passed_last, passed_there)
    x_last = jnp.concatenate([x_embed[1], queries[picks:].astype(wide), vec], axis=0)
    x_last = jnp.where(is_student, x_last, jnp.concatenate(x_over, axis=0))
    sent, *halves, g_vecs, g_pos = run_lower(
        student_flag,
        (passed[:, :width], passed[:, width:].astype(low), jnp.where(is_student, g_vecs, 0.0)),
        cols[part],
        docs[part],
        picked[part],
        x_last[length + picks :],
        x_last[:length],
        x_last[length : length + picks].astype(low),
        whole,
        there,
        near,
        devices,
    )
    sent, rows_sent, d_low_sent = tied(sent, student_rows, d_low)
    rows_other = lax.ppermute(rows_sent, "pair", swap)
    arrived = lax.all_to_all(sent, "dp", split_axis=0, concat_axis=0, tiled=True)
    arrived = arrived.reshape(slot_count, width)

    pos_share = LONGEST // devices
    if pos_share % 16:
        g_vecs = jnp.pad(g_vecs.T, ((0, 0), (0, LANES - g_vecs.shape[0]))).astype(low)
        parts = g_pos.reshape(devices, pos_share, -1, LONGEST).transpose(0, 2, 1, 3)
        parts = parts.reshape(width, LONGEST).astype(low)
        shared = jnp.concatenate([halves[0], g_vecs, parts], axis=1)
        chips = shared.reshape(devices // 2, 2, rows, -1)
        halves = [lax.dynamic_index_in_dim(chips, c, 1, keepdims=False) for c in (core, 1 - core)]
    near_sum, rows_other = tied(across(halves[1]), rows_other)
    chips = (halves[0].astype(wide) + near_sum.astype(wide)).astype(low)
    d_low_other = lax.ppermute(d_low_sent, "pair", swap)

    rights = lax.all_gather(rights, "dp", axis=0, tiled=True)
    at = (0, fold_rows, fold_rows + rows, fold_rows + 2 * rows)
    ends = (0, width, width + hidden, 2 * width + hidden)
    products = [
        dot_first(lefts[:, at[k] : at[k + 1]], rights[:, ends[k] : ends[k + 1]]).astype(low)
        for k in range(3)
    ]
    squares = jnp.zeros((), wide)
    for product in products:
        squares = squares + jnp.sum(jnp.square(product.astype(wide)))
    products[1] = products[1].reshape(rows, 4, width).transpose(1, 0, 2).reshape(4 * rows, width)
    products = jnp.concatenate(products, axis=0)
    d_low_turned, d_low_other = d_low.T, d_low_other.T
    arrived, products, squares, d_low_turned, d_low_other = tied(
        arrived, products, squares, d_low_turned, d_low_other
    )
    arrived_other = lax.ppermute(arrived, "pair", swap)
    if devices % 2 == 0:
        chips, arrived = tied(chips, arrived)
        columns = [[2 * k + c for k in range(devices // 2)] for c in (0, 1)]
        chips = lax.all_to_all(
            chips, "dp", split_axis=0, concat_axis=0, axis_index_groups=columns, tiled=True
        )
    asked = asked.reshape(devices, MB, capacity).transpose(1, 0, 2).reshape(MB, 1, slot_count)
    asked_first, asked_last = asked[0], asked[1]
    own_last = is_student.astype(jnp.int32).reshape(1)
    parts = (
        own_last,
        d_low_turned,
        student_rows,
        d_low_other,
        rows_other,
        asked_first,
        asked_last,
        arrived,
        arrived_other,
    )
    if devices % 2 == 0:
        shared = jnp.sum(chips.astype(wide), axis=0).astype(low)
    pos_near = shared[:, 3 * width + LANES :]
    pos_near = pos_near.reshape(-1, pos_share, LONGEST).transpose(1, 0, 2).reshape(pos_share, width)
    pos_near = jnp.pad(pos_near, ((0, max(0, LANES // 2 - pos_share)), (0, 0)))
    pos_near = lax.all_gather(pos_near, "dp", axis=0)[:, :pos_share].reshape(LONGEST, width)
    pos_near = jnp.concatenate([pos_near, jnp.zeros((pos_count, width), low)], axis=0)
    pos_near = lax.dynamic_slice(
        pos_near, (jnp.minimum(me * pos_count, LONGEST), 0), (pos_count, width)
    )
    arrived_other, shared = tied(arrived_other, shared)
    shared_other = lax.ppermute(shared, "pair", swap)
    arrived_other, products = tied(arrived_other, products)
    products_there = over(products)
    parts = (*parts[:-1], arrived_other)
    g_table, table_squares = run_table(parts, vocab_rows)
    table_squares, products_there, shared_other = tied(
        table_squares, products_there, shared_other
    )
    shared, note = run_norm(squares, table_squares, shared, shared_other, kl_local, 2 * devices)
    totals = lax.all_to_all(note, ("pair", "dp"), split_axis=0, concat_axis=0, tiled=True)
    grad_norm = jnp.sqrt(jnp.sum(totals[devices:, 0, 0]))
    kl_mean = jnp.sum(totals[:, 0, 1]) / total_rows
    factor = jnp.minimum(1.0, clip_limit / (grad_norm + 1e-06))
    table_out = adam_update(table, table_m, table_v, g_table, factor)
    products = jnp.where(is_student, products, products_there).astype(wide)
    g_mlp_out, g_attn_out = products[:fold_rows], products[fold_rows + 4 * rows :]
    g_mlp_in = products[fold_rows : fold_rows + 4 * rows].reshape(4, rows, width)
    g_mlp_in = g_mlp_in.transpose(1, 0, 2).reshape(rows, hidden)
    g_pos = pos_near.astype(wide) + lax.ppermute(pos_near, "pair", swap).astype(wide)
    g_attn_in = shared[:, : 3 * width]
    g_vecs = shared[:, 3 * width : 3 * width + vec_count].T
    smalls = (g_attn_in, g_attn_out, g_mlp_in, g_mlp_out, g_vecs)
    masters = (attn_in, attn_out, mlp_in, mlp_out, vectors)
    firsts = (attn_in_m, attn_out_m, mlp_in_m, mlp_out_m, vectors_m)
    seconds = (attn_in_v, attn_out_v, mlp_in_v, mlp_out_v, vectors_v)
    small_out = run_adam(factor, list(zip(masters, firsts, seconds, smalls)))
    pos_out = adam_update(pos_table, pos_m, pos_v, g_pos, factor)
    return (*table_out, *pos_out, *small_out, grad_norm, kl_mean)


def solution(mesh):
    return jax.shard_map(
        shards,
        mesh=mesh,
        in_specs=(
            P(None, "dp", None, None),
            P(None, "dp", None),
            P(None, "dp", None),
            P(None, "dp", None),
            P("dp", None),
            P("dp", None),
            P("dp", None),
            P("dp", None),
            P("dp", None),
            P("dp", None),
            P(None, "dp"),
            P("dp", None),
            P("dp", None),
            P("dp", None),
            P("dp", None),
            P("dp", None),
            P("dp", None),
            P(None, "dp"),
            P("dp", None),
            P("dp", None),
            P("dp", None),
            P("dp", None),
            P("dp", None),
            P("dp", None),
            P(None, "dp"),
            P("dp", None),
            P("dp", None),
            P("dp", None),
            P("dp", None),
            P("dp", None),
            P("dp", None),
            P(None, "dp"),
        ),
        out_specs=(
            P("dp", None),
            P("dp", None),
            P("dp", None),
            P("dp", None),
            P("dp", None),
            P("dp", None),
            P("dp", None),
            P("dp", None),
            P("dp", None),
            P("dp", None),
            P("dp", None),
            P("dp", None),
            P("dp", None),
            P("dp", None),
            P("dp", None),
            P("dp", None),
            P("dp", None),
            P("dp", None),
            P(None, "dp"),
            P(None, "dp"),
            P(None, "dp"),
            P(),
            P(),
        ),
        check_vma=False,
    )
```
